256 devices in a mesh: region: 4 (over x), member: 64 (over z, y, core).
Axes of the slice: x: 4, y: 4, z: 8, core: 2. Of those that a mesh axis runs over, the one named last changes fastest.
Arguments:
- right_side: float32 [3, 262144], P(None, ('region', 'member')), may hold values from -6 to 6
- fine_blocks: float32 [27, 3, 3, 262144], P(None, None, None, ('region', 'member')), as said below
- fine_links: int32 [26, 262144], P(None, ('region', 'member')), may hold values from 0 to 1279, as said below
- coarse_blocks: float32 [27, 3, 3, 32768], P(None, None, None, ('region', 'member')), as said below
- coarse_links: int32 [26, 32768], P(None, ('region', 'member')), may hold values from 0 to 255, as said below
Outputs:
- correction: float32 [3, 262144], P(None, ('region', 'member'))
- final_residual: float32 [3, 262144], P(None, ('region', 'member'))
The draws below stay inside these ranges and needn't reach their ends.
Inputs may be any that keep to these rules, and one draw needn't show every extreme that they name: `fine_links`: A code of 1024 or more occurs only for one of the first 64 blocks of a device, and only toward a device that exists: the device before or after it in the same region, or the device with the same member index in the region before or after. `coarse_links`: as for fine_links, with 128 coarse nodes a device and 32 in place of 64. `fine_blocks`: each node's diagonal block is strictly dominant: in each row the diagonal entry exceeds 1.1 times the sum of magnitudes of that row's other entries over all 27 blocks. `coarse_blocks`: diagonally dominant as fine_blocks.
All inputs are finite; a program needn't handle non-finite values.
Results may differ from the reference program's by a relative error of at most 0.0003.
Values sent between devices are 32-bit elements; how exact they have to be, the bound alone decides.
A program may use at most 128 MiB of HBM per device.

```python
import math
import jax
import jax.numpy as jnp

COMPS = 3
STEPS = 3
NODE_DEV = 1024
COARSE_DEV = 128
FACE = 64
COARSE_FACE = 32
NODES = 262144
COARSE_NODES = 32768
N_REGION = 4
N_MEMBER = 64


def neighbour_codes(key, per_dev, face):
    nodes = per_dev * N_REGION * N_MEMBER
    node = jnp.arange(nodes, dtype=jnp.int32)
    device = node // per_dev
    local = node % per_dev
    region = device // N_MEMBER
    member = device % N_MEMBER
    inside = jax.random.randint(jax.random.fold_in(key, 1), (26, nodes), 0, per_dev)
    pick = jax.random.randint(jax.random.fold_in(key, 2), (26, nodes), 0, face)
    slot = jnp.arange(26, dtype=jnp.int32)[:, None] % 13
    edge = (local < face)[None]
    result = inside
    result = jnp.where((slot == 0) & edge & (member > 0)[None], per_dev + pick, result)
    result = jnp.where((slot == 1) & edge & (member < N_MEMBER - 1)[None], per_dev + face + pick, result)
    result = jnp.where((slot == 2) & edge & (region > 0)[None], per_dev + 2 * face + pick, result)
    result = jnp.where((slot == 3) & edge & (region < N_REGION - 1)[None], per_dev + 3 * face + pick, result)
    return result.astype(jnp.int32)


def build_blocks(key, nodes, leading):
    spread = jax.random.uniform(jax.random.fold_in(key, 5), (27, 3, 3, nodes), jnp.float32, -1.0, 1.0) / 80.0
    slot = jnp.arange(27)[:, None, None, None]
    row = jnp.arange(3)[None, :, None, None]
    col = jnp.arange(3)[None, None, :, None]
    main = (slot == 26) & (row == col)
    blocks = jnp.where(main, leading[None, None, None, :], spread)
    return blocks


def draw_fine_links(key, part):
    key = jax.random.fold_in(key, 11)
    return neighbour_codes(key, NODE_DEV, FACE)


def draw_coarse_links(key, part):
    key = jax.random.fold_in(key, 12)
    return neighbour_codes(key, COARSE_DEV, COARSE_FACE)


def draw_fine_blocks(key, part):
    key = jax.random.fold_in(key, 13)
    leading = jnp.exp(jax.random.uniform(jax.random.fold_in(key, 7), (NODES,), jnp.float32, math.log(1.1), math.log(4.0)))
    return build_blocks(key, NODES, leading)


def draw_coarse_blocks(key, part):
    key = jax.random.fold_in(key, 14)
    leading = jnp.exp(jax.random.uniform(jax.random.fold_in(key, 7), (COARSE_NODES,), jnp.float32, math.log(1.1), math.log(4.0)))
    return build_blocks(key, COARSE_NODES, leading)


def block_levels(own_key, shape, shards, low, largest):
    def one(dim, shards_of):
        draws = jax.random.uniform(jax.random.fold_in(jax.random.fold_in(own_key, 6), dim), (shards_of,), jnp.float32, low / len(shards), largest / len(shards))
        return jnp.repeat(jnp.exp(draws), shape[dim] // shards_of).reshape((-1,) + (1,) * (len(shape) - dim - 1))

    factor_of = one(*shards[0])
    for cut in shards[1:]:
        factor_of = factor_of * one(*cut)
    return factor_of


def noise(rng, dims, scale, limit, pieces=(), held_as=jnp.bfloat16):
    entries = scale * jax.random.normal(rng, dims, jnp.float32)
    if pieces:
        entries = entries * block_levels(rng, dims, pieces, -0.22, 0.18)
    return jnp.clip(entries, -limit, limit).astype(held_as)


def setup_inputs(seed: int = 0) -> dict:
    seeds = jax.random.split(jax.random.key(seed), 6)
    return {
        "right_side": noise(seeds[0], (COMPS, NODES), 1.0, 6.0, ((1, 256),), jnp.float32),
        "fine_blocks": draw_fine_blocks(jax.random.fold_in(seeds[5], 71), 0),
        "fine_links": draw_fine_links(jax.random.fold_in(seeds[5], 71), 0),
        "coarse_blocks": draw_coarse_blocks(jax.random.fold_in(seeds[5], 71), 0),
        "coarse_links": draw_coarse_links(jax.random.fold_in(seeds[5], 71), 0),
    }


relax = 0.6


def invert(block):
    a, b, c = block[0, 0], block[0, 1], block[0, 2]
    d, e, f = block[1, 0], block[1, 1], block[1, 2]
    g, h, i = block[2, 0], block[2, 1], block[2, 2]
    co_a = e * i - f * h
    co_b = f * g - d * i
    co_c = d * h - e * g
    det = a * co_a + b * co_b + c * co_c
    rows = [[co_a, c * h - b * i, b * f - c * e],
            [co_b, a * i - c * g, c * d - a * f],
            [co_c, b * g - a * h, a * e - b * d]]
    return jnp.stack([jnp.stack(row) for row in rows]) / det


def blockmul(matrix, vector):
    return jnp.sum(matrix * vector[None], axis=1)


def decode(codes, per_dev, face):
    count = codes.shape[1]
    device = (jnp.arange(count, dtype=jnp.int32) // per_dev)[None, :]
    base = device * per_dev
    result = jnp.where(codes < per_dev, base + codes,
             jnp.where(codes < per_dev + face, base - face + (codes - per_dev),
             jnp.where(codes < per_dev + 2 * face, base + per_dev + (codes - per_dev - face),
             jnp.where(codes < per_dev + 3 * face, base - N_MEMBER * per_dev + (codes - per_dev - 2 * face),
                       base + N_MEMBER * per_dev + (codes - per_dev - 3 * face)))))
    return result.astype(jnp.int32)


def operate(blocks, links, field):
    result = blockmul(blocks[26], field)
    for slot in range(26):
        result = result + blockmul(blocks[slot], field[:, links[slot]])
    return result


def reference(right_side, fine_blocks, fine_links, coarse_blocks, coarse_links):
    fine_ids = decode(fine_links, NODE_DEV, FACE)
    coarse_ids = decode(coarse_links, COARSE_DEV, COARSE_FACE)
    inverse_fine = invert(fine_blocks[26])
    first = relax * blockmul(inverse_fine, right_side)
    first_res = right_side - operate(fine_blocks, fine_ids, first)
    smoothed = first + relax * blockmul(inverse_fine, first_res)
    smooth_res = right_side - operate(fine_blocks, fine_ids, smoothed)
    coarse_rhs = jnp.sum(smooth_res.reshape(3, -1, 8), axis=2)
    shadow = coarse_rhs
    resid = coarse_rhs
    direction = coarse_rhs
    error = jnp.zeros_like(coarse_rhs)
    rho = jnp.sum(resid * resid)
    for step in range(STEPS):
        image = operate(coarse_blocks, coarse_ids, direction)
        alpha = rho / jnp.sum(shadow * image)
        middle = resid - alpha * image
        second = operate(coarse_blocks, coarse_ids, middle)
        omega = jnp.sum(second * middle) / jnp.sum(second * second)
        error = error + alpha * direction + omega * middle
        resid = middle - omega * second
        if step + 1 < STEPS:
            rho_new = jnp.sum(shadow * resid)
            beta = (rho_new / rho) * (alpha / omega)
            direction = resid + beta * (direction - omega * image)
            rho = rho_new
    lifted = smoothed + jnp.repeat(error, 8, axis=1)
    lifted_res = right_side - operate(fine_blocks, fine_ids, lifted)
    correction = lifted + relax * blockmul(inverse_fine, lifted_res)
    final_residual = right_side - operate(fine_blocks, fine_ids, correction)
    return correction, final_residual
```

```python
import functools

import jax
import jax.numpy as jnp
from jax import lax
from jax.experimental import pallas as pl
from jax.experimental.pallas import tpu as pltpu
from jax.sharding import PartitionSpec as P

STEPS = 3
BASIS = 2 * STEPS + 1
RELAX = 0.6
SLOTS = 27
PAD = 32
UNROLL = 2
MESH = pl.DeviceIdType.MESH
OFFSETS = ((-1, -1), (-1, 1), (1, -1), (1, 1), (0, 2), (2, 0), (0, -1), (0, 1), (-1, 0), (1, 0))
F32 = jnp.float32


def lanes_of(shape):
    return lax.broadcasted_iota(jnp.int32, shape, len(shape) - 1)


def rows_of(shape):
    return lax.broadcasted_iota(jnp.int32, shape, len(shape) - 2)


def take(table, index):
    return jnp.take_along_axis(table, index, axis=1, mode="promise_in_bounds")


def spread(row):
    return jnp.broadcast_to(row, (8, 128))


def combine(accs):
    rows = rows_of((8, 128))
    sums = [jnp.sum(acc, axis=0, keepdims=True) for acc in accs]
    tile = jnp.where(rows & 3 == 2, sums[2], 0.0)
    tile = jnp.where(rows & 3 == 1, sums[1], tile)
    return jnp.where(rows & 3 == 0, sums[0], tile)


def combine_pair(accs):
    return jnp.where(rows_of((8, 128)) < 4, combine(accs[:3]), combine(accs[3:]))


def coefficients(gram, shift):
    def image(x):
        y = [None] * (len(x) + 1)
        for i, value in enumerate(x):
            y[i] = value * shift if y[i] is None else y[i] + value * shift
            y[i + 1] = value
        return y

    def dot(x, y):
        terms = []
        for i, left in enumerate(x):
            inner = None
            for j, right in enumerate(y):
                term = gram[min(i, j), max(i, j)] * right
                inner = term if inner is None else inner + term
            terms.append(left * inner)
        return functools.reduce(lambda a, b: a + b, terms)

    def axpy(x, a, y):
        out = []
        for i in range(max(len(x), len(y))):
            if i >= len(y):
                out.append(x[i])
            elif i >= len(x):
                out.append(a * y[i])
            else:
                out.append(x[i] + a * y[i])
        return out

    def shadow(x):
        total = gram[0, 0] * x[0]
        for j in range(1, len(x)):
            total = total + gram[0, j] * x[j]
        return total

    one = jnp.ones_like(shift)
    resid, direction = [one], [one]
    error = []
    rho = gram[0, 0]
    for step in range(STEPS):
        move = image(direction)
        alpha = rho / shadow(move)
        middle = axpy(resid, -alpha, move)
        second = image(middle)
        omega = dot(second, middle) / dot(second, second)
        error = axpy(axpy(error, alpha, direction), omega, middle)
        if step + 1 < STEPS:
            resid = axpy(middle, -omega, second)
            rho_new = shadow(resid)
            beta = rho_new / rho * (alpha / omega)
            direction = axpy(resid, beta, axpy(direction, -omega, move))
            rho = rho_new
    return error


def kernel(
    regions, depth_y, depth_z, fine_dev, coarse_dev,
    rhs_hbm, fb_hbm, fl_hbm, cb_hbm, cl_hbm,
    both_out,
    rhs_raw, fb, fb_tail, fbh, fl, fl_tail, cb_raw, cb, cl, cidx, inv, rhs, fa, fc, fd, fa_image, steps, step_images, fl_halo, lift, pairs, images, tab, kv,
    hsend, hrecv, ksend, krecv, bsend, brecv, isend, irecv, fcb, e1, e2, g1, g2, row_send,
    load_sem, halo_send_sem, halo_recv_sem, k_send_sem, k_recv_sem, b_send_sem, b_recv_sem,
    red_send_sem, red_recv_sem,
):
    members = depth_y * depth_z * 2
    tiles = fine_dev // 128
    region = lax.axis_index("region")
    member = lax.axis_index("member")
    z, y, core = lax.div(member, 2 * depth_y), lax.rem(lax.div(member, 2), depth_y), lax.rem(member, 2)
    n1, n2 = regions * depth_y, depth_z * 2
    me1, me2 = region * depth_y + y, z * 2 + core
    region_at = [region] + [lax.rem(region + s, regions) for s in range(1, regions)]
    y_at = [member] + [member + 2 * (lax.rem(y + s, depth_y) - y) for s in range(1, depth_y)]
    z_at = [member] + [member + 2 * depth_y * (lax.rem(z + s, depth_z) - z) for s in range(1, depth_z)]
    peers1 = [(r, m) for r in region_at for m in y_at][1:]
    peers2 = [(region, m + flip) for m in z_at for flip in (0, 1 - 2 * core)][1:]

    def at(dr, dm):
        r = region if dr == 0 else lax.rem(region + (regions + dr), regions)
        m = member if dm == 0 else lax.rem(member + (members + dm), members)
        return r, m

    after, before, above, below = at(0, 1), at(0, -1), at(1, 0), at(-1, 0)

    loads = [
        pltpu.make_async_copy(rhs_hbm, rhs_raw, load_sem.at[4]),
        pltpu.make_async_copy(fb_hbm, fb, load_sem.at[0]),
        pltpu.make_async_copy(cb_hbm, cb_raw, load_sem.at[1]),
        pltpu.make_async_copy(cl_hbm, cl, load_sem.at[2]),
        pltpu.make_async_copy(fl_hbm, fl, load_sem.at[3]),
    ]
    loads[0].start()
    for i in range(3):
        for j in range(3):
            pltpu.make_async_copy(fb_hbm.at[i, j], fb.at[i, j], load_sem.at[0]).start()
    for load in loads[2:]:
        load.start()

    barrier = pltpu.get_barrier_semaphore()
    for dr, dm in OFFSETS:
        device = at(-dr, -dm)
        pl.semaphore_signal(barrier, inc=1, device_id=device, device_id_type=MESH)

    for device in peers1 + peers2:
        pl.semaphore_signal(barrier, inc=1, device_id=device, device_id_type=MESH)

    lane = lanes_of((8, 128))
    rows = rows_of((8, 128))

    def halo_copies(ex, which):
        pairs = (
            (1, 0, after),
            (0, 1, before),
            (0, 2, above),
            (0, 3, below),
        )
        return [
            pltpu.make_async_remote_copy(
                src_ref=hsend.at[2 * ex + src],
                dst_ref=hrecv.at[4 * ex + dst],
                send_sem=halo_send_sem,
                recv_sem=halo_recv_sem.at[ex],
                device_id=device,
                device_id_type=MESH,
            )
            for src, dst, device in pairs
            if src in which
        ]

    def halo_send(ex, first, last):
        hsend[2 * ex] = first
        hsend[2 * ex + 1] = last
        for copy in halo_copies(ex, (0, 1)):
            copy.start()

    def halo_wait(ex):
        block = hrecv.at[pl.ds(4 * ex, 4)]
        pltpu.make_async_copy(block, block, halo_recv_sem.at[ex]).wait()
        return [hrecv[4 * ex + k] for k in range(4)]

    def reduce_start(which, buffer, peers, me, value):
        row_send[which] = value
        buffer[me] = value
        for device in peers:
            pltpu.make_async_remote_copy(
                src_ref=row_send.at[which],
                dst_ref=buffer.at[me],
                send_sem=red_send_sem,
                recv_sem=red_recv_sem.at[which],
                device_id=device,
                device_id_type=MESH,
            ).start()

    def reduce_wait(which, buffer, count, op):
        block = buffer.at[pl.ds(0, count - 1)]
        pltpu.make_async_copy(block, block, red_recv_sem.at[which]).wait()
        return functools.reduce(op, [buffer[k] for k in range(count)])

    def smooth(value, columns=slice(None)):
        total = inv[0, :, columns] * value[0:1, :]
        for j in range(1, 3):
            total = total + inv[j, :, columns] * value[j : j + 1, :]
        return total

    def links(g, columns):
        return fl[8 * g : 8 * g + 8, columns] if g < 3 else fl_tail[:, columns]

    def blocks_at(i, j, g, columns):
        return fb[i, j, 8 * g : 8 * g + 8, columns] if g < 3 else fb_tail[i, j, :, columns]

    def fine_local(source, target, count=1):
        for n in range(count):
            for j in range(3):
                for r in range(tiles):
                    row = 4 * n + j
                    tab[3 * n + j, r] = spread(source[row : row + 1, 128 * r : 128 * r + 128])

        def tile(t, carry):
            columns = pl.ds(pl.multiple_of(t * 128, 128), 128)
            accs = [None] * (3 * count)
            for g in range(4):
                index = links(g, columns)
                where = index & 127
                bits = [(index & (128 << k)) != 0 for k in range(3)]
                for j in range(3):
                    values = []
                    for n in range(count):
                        found = [take(tab[3 * n + j, r], where) for r in range(tiles)]
                        for bit in bits:
                            found = [
                                jnp.where(bit, found[2 * q + 1], found[2 * q])
                                for q in range(len(found) // 2)
                            ]
                        values.append(found[0])
                    for i in range(3):
                        block = blocks_at(i, j, g, columns)
                        for n in range(count):
                            term = block * values[n]
                            k = 3 * n + i
                            accs[k] = term if accs[k] is None else accs[k] + term
            for k in range(3 * count):
                pairs[k, t] = accs[k]
            return carry

        lax.fori_loop(0, tiles, tile, 0, unroll=UNROLL if count == 1 else 1)
        for t in range(tiles):
            sums = [pairs[k, t] for k in range(3 * count)]
            target[:, 128 * t : 128 * t + 128] = combine(sums) if count == 1 else combine_pair(sums)

    def fine_remote(halves):
        accs = [None] * 3
        for g in range(4):
            part = slice(8 * g, 8 * g + 8)
            index = links(g, slice(0, 128))
            where = index & 127
            bit = (index & 128) != 0
            for j in range(3):
                low, high = (take(spread(half[j : j + 1, :]), where) for half in halves)
                value = jnp.where(bit, high, low)
                for i in range(3):
                    term = fbh[i, j, part, :] * value
                    accs[i] = term if accs[i] is None else accs[i] + term
        return combine(accs)

    def fine_send(ex, field):
        within = lane & 63
        halo_send(
            ex,
            take(field[:, 0:128], within),
            take(field[:, fine_dev - 128 : fine_dev], within + 64),
        )

    def fine_wait(ex):
        left, right, lower, upper = halo_wait(ex)
        return jnp.where(lane < 64, left, right), jnp.where(lane < 64, lower, upper)

    rhs[...] = jnp.zeros((8, fine_dev), F32)
    loads[0].wait()
    rhs[0:3, :] = rhs_raw[...]
    rhs[4:7, :] = rhs_raw[...]
    loads[1].wait()

    def start_tile(t, carry):
        columns = pl.ds(pl.multiple_of(t * 128, 128), 128)
        (a, b, c), (d, e, f), (g_, h_, i_) = [
            [spread(fb[i, j, 26:27, columns]) for j in range(3)] for i in range(3)
        ]
        co_a = e * i_ - f * h_
        co_b = f * g_ - d * i_
        co_c = d * h_ - e * g_
        scale = RELAX / (a * co_a + b * co_b + c * co_c)
        adjugate = [
            [co_a, c * h_ - b * i_, b * f - c * e],
            [co_b, a * i_ - c * g_, c * d - a * f],
            [co_c, b * g_ - a * h_, a * e - b * d],
        ]
        total = None
        for j in range(3):
            column = jnp.where(rows & 3 == 2, adjugate[2][j], 0.0)
            column = jnp.where(rows & 3 == 1, adjugate[1][j], column)
            column = jnp.where(rows & 3 == 0, adjugate[0][j], column) * scale
            inv[j, :, columns] = column
            term = column * spread(rhs[j : j + 1, columns])
            total = term if total is None else total + term
        fa[:, columns] = total
        return carry

    lax.fori_loop(0, tiles, start_tile, 0, unroll=UNROLL)
    pl.semaphore_wait(barrier, len(OFFSETS) + (n1 - 1) + (n2 - 1))
    fine_send(0, fa)

    fl_tail[...] = jnp.where(rows_of((8, fine_dev)) == 2, lanes_of((8, fine_dev)), 0)
    fb_tail[...] = jnp.zeros((3, 3, 8, fine_dev), F32)
    fb_tail[:, :, 0:3, :] = fb[:, :, 24:27, :]
    loads[4].wait()
    fl_tail[0:2, :] = fl[24:26, :]
    for g in range(4):
        part = slice(8 * g, 8 * g + 8)
        outside = links(g, slice(0, 128)) >= fine_dev
        for i in range(3):
            for j in range(3):
                block = blocks_at(i, j, g, slice(0, 128))
                fbh[i, j, part, :] = jnp.where(outside, block, 0.0)
                inside = jnp.where(outside, 0.0, block)
                if g < 3:
                    fb[i, j, part, 0:128] = inside
                else:
                    fb_tail[i, j, :, 0:128] = inside

    kv[...] = jnp.zeros((3, 8, 128), F32)
    cidx[24:32, :] = jnp.where(rows == 2, lane, 0)
    cb[:, :, 24:32, :] = jnp.zeros((3, 3, 8, 128), F32)
    loads[2].wait()
    loads[3].wait()
    cb[:, :, 0:27, :] = cb_raw[...]
    cidx[0:26, :] = cl[...]
    diagonal = [cb[i, i, 26:27, :] for i in range(3)]
    largest = functools.reduce(jnp.maximum, diagonal)
    smallest = -functools.reduce(jnp.minimum, diagonal)
    largest, smallest = spread(largest), spread(smallest)
    swap = lane ^ 64
    largest = jnp.maximum(largest, take(largest, swap))
    smallest = jnp.maximum(smallest, take(smallest, swap))
    extremes = jnp.where(lane < 64, largest, smallest)[0:1]

    reduce_start(0, e1, peers1, me1, extremes)
    fine_local(fa, fc)

    quarter = lane >> 5

    def packed(pieces, start):
        rolled = [pltpu.roll(piece, (128 + 32 * g - start) % 128, 1) for g, piece in enumerate(pieces)]
        low = jnp.where(quarter == 0, rolled[0], rolled[1])
        return jnp.where(quarter < 2, low, jnp.where(quarter == 2, rolled[2], rolled[3]))

    parts = [slice(8 * g, 8 * g + 8) for g in range(4)]
    codes = [cidx[part, :] for part in parts]
    for end, start in ((0, 0), (1, coarse_dev - 32)):
        isend[end] = packed(codes, start)
        for i in range(3):
            for j in range(3):
                bsend[end, 3 * i + j] = packed([cb[i, j, part, :] for part in parts], start)
    face_code = isend[0]
    for i in range(3):
        for j in range(3):
            fcb[i, j] = jnp.where(face_code >= coarse_dev, bsend[0, 3 * i + j], 0.0)
            for g in range(4):
                cb[i, j, parts[g], :] = jnp.where(codes[g] >= coarse_dev, 0.0, cb[i, j, parts[g], :])
    for g in range(4):
        cidx[parts[g], :] = codes[g] & 127
    side_copies = []
    for src, dst, device in ((1, 0, after), (0, 1, before), (0, 2, above), (0, 3, below)):
        for kind, (source, sink) in enumerate(((bsend, brecv), (isend, irecv))):
            side_copies.append(
                pltpu.make_async_remote_copy(
                    src_ref=source.at[src],
                    dst_ref=sink.at[dst],
                    send_sem=b_send_sem.at[kind],
                    recv_sem=b_recv_sem.at[kind],
                    device_id=device,
                    device_id_type=MESH,
                )
            )
    for copy in side_copies:
        copy.start()
    head, rest = slice(0, 128), slice(128, fine_dev)
    fa[:, rest] += smooth(rhs[:, rest] - fc[:, rest], rest)
    halves = fine_wait(0)
    fa[:, head] += smooth(rhs[:, head] - fc[:, head] - fine_remote(halves), head)
    fine_send(1, fa)
    extremes = reduce_wait(0, e1, n1, jnp.maximum)
    reduce_start(1, e2, peers2, me2, extremes)
    fine_local(fa, fc)

    def eighths(part):
        for k in (1, 2, 4):
            part = part + pltpu.roll(part, 128 - k, 1)
        return take(part, (lane & 15) * 8)

    def restrict(ref):
        out = eighths(ref[:, 0:128])
        for t in range(1, tiles):
            picked = eighths(ref[:, 128 * t : 128 * t + 128])
            out = jnp.where(lane >> 4 == t, picked, out)
        return out

    fc[...] = rhs[...] - fc[...]
    coarse = restrict(fc)
    remote = fine_remote(fine_wait(1))
    fc[:, head] -= remote
    coarse = coarse - jnp.where(lane < 16, eighths(remote), 0.0)

    def coarse_send(ex, field):
        edge = take(field, jnp.where(lane < 32, lane + (coarse_dev - 32), lane & 31))
        tile = jnp.where(rows < 4, field, edge)
        ksend[ex] = tile
        for k, (dr, dm) in enumerate(OFFSETS):
            pltpu.make_async_remote_copy(
                src_ref=ksend.at[ex],
                dst_ref=krecv.at[ex, k],
                send_sem=k_send_sem,
                recv_sem=k_recv_sem.at[ex],
                device_id=at(-dr, -dm),
                device_id_type=MESH,
            ).start()
        return tile

    def coarse_wait(ex):
        block = krecv.at[ex]
        pltpu.make_async_copy(block, block, k_recv_sem.at[ex]).wait()
        return {offset: krecv[ex, k] for k, offset in enumerate(OFFSETS)}

    def beside(left, right, lower, upper):
        low = jnp.where(quarter == 0, left, right)
        return jnp.where(quarter < 2, low, jnp.where(quarter == 2, lower, upper))

    def folded(accs):
        tile = combine(accs)
        tile = tile + pltpu.roll(tile, 64, 1)
        return tile + pltpu.roll(tile, 32, 1)

    def coarse_local(field):
        accs = [None] * 3
        tables = [spread(field[j : j + 1, :]) for j in range(3)]
        for g in range(4):
            index = cidx[parts[g], :]
            for j in range(3):
                value = take(tables[j], index)
                for i in range(3):
                    term = cb[i, j, parts[g], :] * value
                    accs[i] = term if accs[i] is None else accs[i] + term
        return combine(accs)

    def coarse_remote(halo):
        accs = [None] * 3
        index = isend[0] & 127
        for j in range(3):
            value = take(spread(halo[4 + j : 5 + j, :]), index)
            for i in range(3):
                term = fcb[i, j] * value
                accs[i] = term if accs[i] is None else accs[i] + term
        return jnp.where(lane < 32, folded(accs), 0.0)

    def coarse_ghost(tiles_of, mine):
        around = (
            ((0, -1), None),
            ((0, 1), (mine, tiles_of[0, 2], tiles_of[-1, 1], tiles_of[1, 1])),
            ((-1, 0), (tiles_of[-1, -1], tiles_of[-1, 1], tiles_of[2, 0], mine)),
            ((1, 0), (tiles_of[1, -1], tiles_of[1, 1], mine, tiles_of[2, 0])),
        )
        out = None
        for q, (offset, edges) in enumerate(around):
            code = irecv[q]
            index = code & 127
            full = tiles_of[offset]
            outer = None if edges is None else beside(*edges)
            accs = [None] * 3
            for j in range(3):
                value = take(spread(full[j : j + 1, :]), index)
                if outer is not None:
                    far = take(spread(outer[4 + j : 5 + j, :]), index)
                    value = jnp.where(code >= coarse_dev, far, value)
                for i in range(3):
                    term = brecv[q, 3 * i + j] * value
                    accs[i] = term if accs[i] is None else accs[i] + term
            tile = folded(accs)
            out = tile if out is None else jnp.where(quarter == q, tile, out)
        return out

    def lift_pair(ex, fields, halos):
        for n in range(2):
            for j in range(3):
                lift[n, j] = spread(fields[n][j : j + 1, :])

        def tile(t, carry):
            columns = pl.ds(pl.multiple_of(t * 128, 128), 128)
            accs = [None] * 6
            for g in range(4):
                where = (links(g, columns) >> 3) & 127
                for j in range(3):
                    values = [take(lift[n, j], where) for n in range(2)]
                    for i in range(3):
                        block = blocks_at(i, j, g, columns)
                        for n in range(2):
                            term = block * values[n]
                            k = 3 * n + i
                            accs[k] = term if accs[k] is None else accs[k] + term
            for k in range(6):
                pairs[k, t] = accs[k]
            return carry

        lax.fori_loop(0, tiles, tile, 0, unroll=UNROLL)
        accs = [pairs[k, 0] for k in range(6)]
        for g in range(4):
            where = fl_halo[parts[g], :]
            for j in range(3):
                values = [take(spread(halos[n][4 + j : 5 + j, :]), where) for n in range(2)]
                for i in range(3):
                    block = fbh[i, j, parts[g], :]
                    for n in range(2):
                        accs[3 * n + i] = accs[3 * n + i] + block * values[n]
        images[ex, :, 0:128] = combine_pair(accs)
        for t in range(1, tiles):
            images[ex, :, 128 * t : 128 * t + 128] = combine_pair([pairs[k, t] for k in range(6)])

        def faces(columns):
            total = None
            for j in range(3):
                value = jnp.where(
                    rows < 4, spread(images[ex, j : j + 1, columns]), spread(images[ex, j + 4 : j + 5, columns])
                )
                term = inv[j, :, columns] * value
                total = term if total is None else total + term
            return total

        for t in range(tiles):
            columns = slice(128 * t, 128 * t + 128)
            steps[:, columns] = faces(columns)
        fine_send(3 + ex, steps)

    mine = coarse_send(0, coarse)
    for g in range(4):
        node = links(g, slice(0, 128)) & 255
        fl_halo[parts[g], :] = ((node >> 6) << 5) + ((node & 63) >> 3) + jnp.where(node < 64, 24, 0)
    update = smooth(fc[...])
    fd[...] = update
    fine_send(2, fd)
    fine_local(fd, fa_image)
    extremes = spread(reduce_wait(1, e2, n2, jnp.maximum))
    lowest = jnp.min(extremes)
    largest = jnp.max(jnp.where(lane < 64, extremes, lowest), axis=1, keepdims=True)
    smallest = -jnp.max(jnp.where(lane < 64, lowest, extremes), axis=1, keepdims=True)
    largest, smallest = jnp.broadcast_to(largest, (8, 128)), jnp.broadcast_to(smallest, (8, 128))
    centre = 0.5 * largest + 0.5 * smallest
    width = 0.5 * largest - 0.5 * smallest + 0.125 * largest
    shrink = 1.0 / width
    for kind, sink in enumerate((brecv, irecv)):
        pltpu.make_async_copy(sink, sink, b_recv_sem.at[kind]).wait()

    def keep(ref, k, field):
        for j in range(3):
            ref[j, k : k + 1, :] = field[j : j + 1, :]

    for ex in range(STEPS):
        local = coarse_local(coarse) - centre * coarse
        keep(kv, 2 * ex, coarse)
        base = coarse
        tiles_of = coarse_wait(ex)
        halo = beside(tiles_of[0, -1], tiles_of[0, 1], tiles_of[-1, 0], tiles_of[1, 0])
        coarse = (local + coarse_remote(halo)) * shrink
        ghost = (coarse_ghost(tiles_of, mine) - centre * halo) * shrink
        keep(kv, 2 * ex + 1, coarse)
        pair = (base, coarse), (halo, ghost)
        coarse = (coarse_local(coarse) - centre * coarse + coarse_remote(ghost)) * shrink
        if ex + 1 < STEPS:
            mine = coarse_send(ex + 1, coarse)
            lift_pair(ex, *pair)
            fine_local(steps, step_images.at[ex], 2)
    for j in range(3):
        kv[j, BASIS - 1 : BASIS, :] = coarse[j : j + 1, :]

    basis = jnp.concatenate([kv[0], kv[1], kv[2]], axis=1)
    gram = lax.dot_general(
        basis, basis, (((1,), (1,)), ((), ())),
        precision=lax.Precision.HIGHEST, preferred_element_type=F32,
    )
    gram = jnp.concatenate([gram, jnp.zeros((8, 120), F32)], axis=1)
    gram = jnp.where(rows == lane >> 3, take(gram, lane & 7), 0.0)
    gram = jnp.sum(gram, axis=0, keepdims=True)
    reduce_start(2, g1, peers1, me1, gram)
    lift_pair(STEPS - 1, *pair)
    gram = reduce_wait(2, g1, n1, jnp.add)
    reduce_start(3, g2, peers2, me2, gram)
    fine_local(steps, step_images.at[STEPS - 1], 2)
    gram = spread(reduce_wait(3, g2, n2, jnp.add))
    entries = {
        (i, j): take(gram, jnp.full((8, 128), 8 * i + j, jnp.int32))
        for i in range(BASIS)
        for j in range(i, BASIS)
    }
    weights = [weight * shrink for weight in coefficients(entries, centre * shrink)]

    def mix(ref):
        out = []
        for j in range(3):
            total = None
            for k, weight in enumerate(weights):
                term = weight[0:1] * ref[j, k : k + 1, :]
                total = term if total is None else total + term
            out.append(total)
        tile = jnp.where(rows == 1, out[1], jnp.where(rows == 2, out[2], 0.0))
        return jnp.where(rows == 0, out[0], tile)

    doubled = [jnp.where(rows < 4, weights[2 * ex], weights[2 * ex + 1]) for ex in range(STEPS)]

    def mix_pairs(tiles_of):
        total = functools.reduce(jnp.add, [w * tile for w, tile in zip(doubled, tiles_of)])
        return total + pltpu.roll(total, 4, 0)

    for t in range(tiles):
        columns = slice(128 * t, 128 * t + 128)
        fc[:, columns] = fc[:, columns] - mix_pairs([images[ex, :, columns] for ex in range(STEPS)])
    error = mix(kv)
    update = smooth(fc[...])
    low, high = fine_wait(2)
    others = [fine_wait(3 + ex) for ex in range(STEPS)]
    halves = [
        low - mix_pairs([other[0] for other in others]),
        high - mix_pairs([other[1] for other in others]),
    ]
    remote = fine_remote(halves)
    for t in range(tiles):
        columns = slice(128 * t, 128 * t + 128)
        both_out[0, :, columns] = (fa[:, columns] + update[:, columns] + take(error, 16 * t + (lane >> 3)))[0:3]
        final = fc[:, columns] - fa_image[:, columns]
        final = final + mix_pairs([step_images[ex, :, columns] for ex in range(STEPS)])
        both_out[1, :, columns] = (final - remote if t == 0 else final)[0:3]

    pltpu.make_async_copy(hrecv, hrecv, halo_send_sem).wait()
    pltpu.make_async_copy(krecv, krecv, k_send_sem).wait()
    for kind, sink in enumerate((brecv, irecv)):
        pltpu.make_async_copy(sink, sink, b_send_sem.at[kind]).wait()
    for buffer, count in ((e1, n1), (e2, n2), (g1, n1), (g2, n2)):
        block = buffer.at[pl.ds(0, count - 1)]
        pltpu.make_async_copy(block, block, red_send_sem).wait()


def body(regions, depth_y, depth_z, right_side, fine_blocks, fine_links, coarse_blocks, coarse_links):
    fine_dev, coarse_dev = right_side.shape[1], coarse_blocks.shape[3]
    n1, n2 = regions * depth_y, depth_z * 2
    exchanges = 3 + STEPS
    reach = len(OFFSETS)
    vmem = pl.BlockSpec(memory_space=pltpu.VMEM)
    hbm = pl.BlockSpec(memory_space=pltpu.HBM)
    out = pltpu.VMEM((2, 3, fine_dev), F32)
    both = pl.pallas_call(
        functools.partial(kernel, regions, depth_y, depth_z, fine_dev, coarse_dev),
        out_shape=out,
        in_specs=[hbm] * 5,
        out_specs=vmem,
        scratch_shapes=[
            pltpu.VMEM((3, fine_dev), F32),
            pltpu.VMEM((3, 3, SLOTS, fine_dev), F32),
            pltpu.VMEM((3, 3, 8, fine_dev), F32),
            pltpu.VMEM((3, 3, PAD, 128), F32),
            pltpu.VMEM((SLOTS - 1, fine_dev), jnp.int32),
            pltpu.VMEM((8, fine_dev), jnp.int32),
            pltpu.VMEM((3, 3, SLOTS, 128), F32),
            pltpu.VMEM((3, 3, PAD, 128), F32),
            pltpu.VMEM((SLOTS - 1, 128), jnp.int32),
            pltpu.VMEM((PAD, 128), jnp.int32),
            pltpu.VMEM((3, 8, fine_dev), F32),
            pltpu.VMEM((8, fine_dev), F32),
            pltpu.VMEM((8, fine_dev), F32),
            pltpu.VMEM((8, fine_dev), F32),
            pltpu.VMEM((8, fine_dev), F32),
            pltpu.VMEM((8, fine_dev), F32),
            pltpu.VMEM((8, fine_dev), F32),
            pltpu.VMEM((STEPS, 8, fine_dev), F32),
            pltpu.VMEM((PAD, 128), jnp.int32),
            pltpu.VMEM((2, 3, 8, 128), F32),
            pltpu.VMEM((6, fine_dev // 128, 8, 128), F32),
            pltpu.VMEM((STEPS, 8, fine_dev), F32),
            pltpu.VMEM((6, fine_dev // 128, 8, 128), F32),
            pltpu.VMEM((3, 8, 128), F32),
            pltpu.VMEM((2 * exchanges, 8, 128), F32),
            pltpu.VMEM((4 * exchanges, 8, 128), F32),
            pltpu.VMEM((STEPS, 8, 128), F32),
            pltpu.VMEM((STEPS, reach, 8, 128), F32),
            pltpu.VMEM((2, 9, 8, 128), F32),
            pltpu.VMEM((4, 9, 8, 128), F32),
            pltpu.VMEM((2, 8, 128), jnp.int32),
            pltpu.VMEM((4, 8, 128), jnp.int32),
            pltpu.VMEM((3, 3, 8, 128), F32),
            pltpu.VMEM((n1, 1, 128), F32),
            pltpu.VMEM((n2, 1, 128), F32),
            pltpu.VMEM((n1, 1, 128), F32),
            pltpu.VMEM((n2, 1, 128), F32),
            pltpu.VMEM((4, 1, 128), F32),
            pltpu.SemaphoreType.DMA((5,)),
            pltpu.SemaphoreType.DMA,
            pltpu.SemaphoreType.DMA((exchanges,)),
            pltpu.SemaphoreType.DMA,
            pltpu.SemaphoreType.DMA((STEPS,)),
            pltpu.SemaphoreType.DMA((2,)),
            pltpu.SemaphoreType.DMA((2,)),
            pltpu.SemaphoreType.DMA,
            pltpu.SemaphoreType.DMA((4,)),
        ],
        compiler_params=pltpu.CompilerParams(
            collective_id=0, has_side_effects=True, vmem_limit_bytes=60 * 1024 * 1024
        ),
    )(
        right_side,
        jnp.transpose(fine_blocks, (1, 2, 0, 3)),
        fine_links,
        jnp.transpose(coarse_blocks, (1, 2, 0, 3)),
        coarse_links,
    )
    return both[0], both[1]


def solution(mesh):
    regions, members = mesh.shape["region"], mesh.shape["member"]
    depth_y = 4 if members % 8 == 0 else 2
    depth_z = members // (2 * depth_y)
    flat = ("region", "member")
    return jax.shard_map(
        functools.partial(body, regions, depth_y, depth_z),
        mesh=mesh,
        in_specs=(
            P(None, flat),
            P(None, None, None, flat),
            P(None, flat),
            P(None, None, None, flat),
            P(None, flat),
        ),
        out_specs=(P(None, flat), P(None, flat)),
        check_vma=False,
    )
```

```python
import functools

import jax
import jax.numpy as jnp
from jax import lax
from jax.experimental import pallas as pl
from jax.experimental.pallas import tpu as pltpu
from jax.sharding import PartitionSpec as P

STEPS = 3
BASIS = 2 * STEPS + 1
RELAX = 0.6
SLOTS = 27
PAD = 32
UNROLL = 2
MESH = pl.DeviceIdType.MESH
OFFSETS = ((-1, -1), (-1, 1), (1, -1), (1, 1), (0, 2), (2, 0), (0, -1), (0, 1), (-1, 0), (1, 0))
F32 = jnp.float32


def lanes_of(shape):
    return lax.broadcasted_iota(jnp.int32, shape, len(shape) - 1)


def rows_of(shape):
    return lax.broadcasted_iota(jnp.int32, shape, len(shape) - 2)


def take(table, index):
    return jnp.take_along_axis(table, index, axis=1, mode="promise_in_bounds")


def spread(row):
    return jnp.broadcast_to(row, (8, 128))


def combine(accs):
    rows = rows_of((8, 128))
    sums = [jnp.sum(acc, axis=0, keepdims=True) for acc in accs]
    tile = jnp.where(rows & 3 == 2, sums[2], 0.0)
    tile = jnp.where(rows & 3 == 1, sums[1], tile)
    return jnp.where(rows & 3 == 0, sums[0], tile)


def combine_pair(accs):
    return jnp.where(rows_of((8, 128)) < 4, combine(accs[:3]), combine(accs[3:]))


def coefficients(gram, shift):
    def image(x):
        y = [None] * (len(x) + 1)
        for i, value in enumerate(x):
            y[i] = value * shift if y[i] is None else y[i] + value * shift
            y[i + 1] = value
        return y

    def total(terms):
        while len(terms) > 1:
            terms = [terms[k] + terms[k + 1] if k + 1 < len(terms) else terms[k] for k in range(0, len(terms), 2)]
        return terms[0]

    def products(x, count):
        return [
            total([gram[min(i, j), max(i, j)] * value for j, value in enumerate(x)]) for i in range(count)
        ]

    def dot(x, y):
        return total([left * right for left, right in zip(x, y)])

    def axpy(x, a, y):
        out = []
        for i in range(max(len(x), len(y))):
            if i >= len(y):
                out.append(x[i])
            elif i >= len(x):
                out.append(a * y[i])
            else:
                out.append(x[i] + a * y[i])
        return out

    def shadow(x):
        return total([gram[0, j] * value for j, value in enumerate(x)])

    one = jnp.ones_like(shift)
    resid, direction = [one], [one]
    error = []
    rho = gram[0, 0]
    for step in range(STEPS):
        move = image(direction)
        alpha = rho / shadow(move)
        middle = axpy(resid, -alpha, move)
        second = image(middle)
        against = products(second, len(second))
        omega = dot(middle, against) / dot(second, against)
        error = axpy(axpy(error, alpha, direction), omega, middle)
        if step + 1 < STEPS:
            resid = axpy(middle, -omega, second)
            rho_new = shadow(resid)
            beta = rho_new / rho * (alpha / omega)
            direction = axpy(resid, beta, axpy(direction, -omega, move))
            rho = rho_new
    return error


def kernel(
    regions, depth_y, depth_z, fine_dev, coarse_dev,
    rhs_hbm, fb_hbm, fl_hbm, cb_hbm, cl_hbm,
    both_out,
    rhs_raw, fb, fb_tail, fbh, fl, fl_tail, cb_raw, cb, cl, cidx, inv, rhs, fa, fc, fd, fa_image, steps, step_images, fl_halo, lift, pairs, images, tab, kv,
    hsend, hrecv, ksend, krecv, bsend, brecv, isend, irecv, fcb, e1, e2, g1, g2, row_send,
    load_sem, halo_send_sem, halo_recv_sem, k_send_sem, k_recv_sem, b_send_sem, b_recv_sem,
    red_send_sem, red_recv_sem,
):
    members = depth_y * depth_z * 2
    tiles = fine_dev // 128
    region = lax.axis_index("region")
    member = lax.axis_index("member")
    z, y, core = lax.div(member, 2 * depth_y), lax.rem(lax.div(member, 2), depth_y), lax.rem(member, 2)
    n1, n2 = regions * depth_y, depth_z * 2
    me1, me2 = region * depth_y + y, z * 2 + core
    region_at = [region] + [lax.rem(region + s, regions) for s in range(1, regions)]
    y_at = [member] + [member + 2 * (lax.rem(y + s, depth_y) - y) for s in range(1, depth_y)]
    z_at = [member] + [member + 2 * depth_y * (lax.rem(z + s, depth_z) - z) for s in range(1, depth_z)]
    def far_first(outer, inner, pair):
        around = lambda s, count: min(s, count - s)
        steps = [(s, t) for s in range(len(outer)) for t in range(len(inner))][1:]
        steps.sort(key=lambda st: -around(st[0], len(outer)) - around(st[1], len(inner)))
        return [pair(outer[s], inner[t]) for s, t in steps]

    peers1 = far_first(region_at, y_at, lambda r, m: (r, m))
    peers2 = far_first(z_at, [0, 1 - 2 * core], lambda m, flip: (region, m + flip))

    def at(dr, dm):
        r = region if dr == 0 else lax.rem(region + (regions + dr), regions)
        m = member if dm == 0 else lax.rem(member + (members + dm), members)
        return r, m

    after, before, above, below = at(0, 1), at(0, -1), at(1, 0), at(-1, 0)

    loads = [
        pltpu.make_async_copy(rhs_hbm, rhs_raw, load_sem.at[4]),
        pltpu.make_async_copy(fb_hbm, fb, load_sem.at[0]),
        pltpu.make_async_copy(cb_hbm, cb_raw, load_sem.at[1]),
        pltpu.make_async_copy(cl_hbm, cl, load_sem.at[2]),
        pltpu.make_async_copy(fl_hbm, fl, load_sem.at[3]),
    ]
    loads[0].start()
    for i in range(3):
        for j in range(3):
            pltpu.make_async_copy(fb_hbm.at[i, j], fb.at[i, j], load_sem.at[0]).start()
    for load in loads[2:]:
        load.start()

    barrier = pltpu.get_barrier_semaphore()
    for dr, dm in OFFSETS:
        device = at(-dr, -dm)
        pl.semaphore_signal(barrier, inc=1, device_id=device, device_id_type=MESH)

    for device in peers1 + peers2:
        pl.semaphore_signal(barrier, inc=1, device_id=device, device_id_type=MESH)

    lane = lanes_of((8, 128))
    rows = rows_of((8, 128))

    def halo_copies(ex, which):
        pairs = (
            (1, 0, after),
            (0, 1, before),
            (0, 2, above),
            (0, 3, below),
        )
        return [
            pltpu.make_async_remote_copy(
                src_ref=hsend.at[2 * ex + src],
                dst_ref=hrecv.at[4 * ex + dst],
                send_sem=halo_send_sem,
                recv_sem=halo_recv_sem.at[ex],
                device_id=device,
                device_id_type=MESH,
            )
            for src, dst, device in pairs
            if src in which
        ]

    def halo_send(ex, first, last):
        hsend[2 * ex] = first
        hsend[2 * ex + 1] = last
        for copy in halo_copies(ex, (0, 1)):
            copy.start()

    def halo_wait(ex):
        block = hrecv.at[pl.ds(4 * ex, 4)]
        pltpu.make_async_copy(block, block, halo_recv_sem.at[ex]).wait()
        return [hrecv[4 * ex + k] for k in range(4)]

    def reduce_start(which, buffer, peers, me, value):
        row_send[which] = value
        buffer[me] = value
        for device in peers:
            pltpu.make_async_remote_copy(
                src_ref=row_send.at[which],
                dst_ref=buffer.at[me],
                send_sem=red_send_sem,
                recv_sem=red_recv_sem.at[which],
                device_id=device,
                device_id_type=MESH,
            ).start()

    def reduce_wait(which, buffer, count, op):
        block = buffer.at[pl.ds(0, count - 1)]
        pltpu.make_async_copy(block, block, red_recv_sem.at[which]).wait()
        return functools.reduce(op, [buffer[k] for k in range(count)])

    def smooth(value, columns=slice(None)):
        total = inv[0, :, columns] * value[0:1, :]
        for j in range(1, 3):
            total = total + inv[j, :, columns] * value[j : j + 1, :]
        return total

    def links(g, columns):
        return fl[8 * g : 8 * g + 8, columns] if g < 3 else fl_tail[:, columns]

    def blocks_at(i, j, g, columns):
        return fb[i, j, 8 * g : 8 * g + 8, columns] if g < 3 else fb_tail[i, j, :, columns]

    def fine_local(source, target, count=1):
        for n in range(count):
            for j in range(3):
                for r in range(tiles):
                    row = 4 * n + j
                    tab[3 * n + j, r] = spread(source[row : row + 1, 128 * r : 128 * r + 128])

        def tile(t, carry):
            columns = pl.ds(pl.multiple_of(t * 128, 128), 128)
            accs = [None] * (3 * count)
            for g in range(4):
                index = links(g, columns)
                where = index & 127
                bits = [(index & (128 << k)) != 0 for k in range(3)]
                for j in range(3):
                    values = []
                    for n in range(count):
                        found = [take(tab[3 * n + j, r], where) for r in range(tiles)]
                        for bit in bits:
                            found = [
                                jnp.where(bit, found[2 * q + 1], found[2 * q])
                                for q in range(len(found) // 2)
                            ]
                        values.append(found[0])
                    for i in range(3):
                        block = blocks_at(i, j, g, columns)
                        for n in range(count):
                            term = block * values[n]
                            k = 3 * n + i
                            accs[k] = term if accs[k] is None else accs[k] + term
            for k in range(3 * count):
                pairs[k, t] = accs[k]
            return carry

        lax.fori_loop(0, tiles, tile, 0, unroll=UNROLL if count == 1 else 1)
        for t in range(tiles):
            sums = [pairs[k, t] for k in range(3 * count)]
            target[:, 128 * t : 128 * t + 128] = combine(sums) if count == 1 else combine_pair(sums)

    def fine_remote(halves, count=1):
        accs = [None] * (3 * count)
        for g in range(4):
            part = slice(8 * g, 8 * g + 8)
            index = links(g, slice(0, 128))
            where = index & 127
            bit = (index & 128) != 0
            for j in range(3):
                values = []
                for n in range(count):
                    row = 4 * n + j
                    low, high = (take(spread(half[row : row + 1, :]), where) for half in halves)
                    values.append(jnp.where(bit, high, low))
                for i in range(3):
                    block = fbh[i, j, part, :]
                    for n in range(count):
                        term = block * values[n]
                        k = 3 * n + i
                        accs[k] = term if accs[k] is None else accs[k] + term
        return combine(accs) if count == 1 else combine_pair(accs)

    def fine_send(ex, field):
        within = lane & 63
        halo_send(
            ex,
            take(field[:, 0:128], within),
            take(field[:, fine_dev - 128 : fine_dev], within + 64),
        )

    def fine_wait(ex):
        left, right, lower, upper = halo_wait(ex)
        return jnp.where(lane < 64, left, right), jnp.where(lane < 64, lower, upper)

    rhs[...] = jnp.zeros((8, fine_dev), F32)
    loads[0].wait()
    rhs[0:3, :] = rhs_raw[...]
    rhs[4:7, :] = rhs_raw[...]
    loads[1].wait()

    def start_tile(t, carry):
        columns = pl.ds(pl.multiple_of(t * 128, 128), 128)
        (a, b, c), (d, e, f), (g_, h_, i_) = [
            [spread(fb[i, j, 26:27, columns]) for j in range(3)] for i in range(3)
        ]
        co_a = e * i_ - f * h_
        co_b = f * g_ - d * i_
        co_c = d * h_ - e * g_
        scale = RELAX / (a * co_a + b * co_b + c * co_c)
        adjugate = [
            [co_a, c * h_ - b * i_, b * f - c * e],
            [co_b, a * i_ - c * g_, c * d - a * f],
            [co_c, b * g_ - a * h_, a * e - b * d],
        ]
        total = None
        for j in range(3):
            column = jnp.where(rows & 3 == 2, adjugate[2][j], 0.0)
            column = jnp.where(rows & 3 == 1, adjugate[1][j], column)
            column = jnp.where(rows & 3 == 0, adjugate[0][j], column) * scale
            inv[j, :, columns] = column
            term = column * spread(rhs[j : j + 1, columns])
            total = term if total is None else total + term
        fa[:, columns] = total
        return carry

    start_tile(0, 0)
    start_tile(tiles - 1, 0)
    pl.semaphore_wait(barrier, len(OFFSETS) + (n1 - 1) + (n2 - 1))
    fine_send(0, fa)
    lax.fori_loop(1, tiles - 1, start_tile, 0, unroll=UNROLL)

    fl_tail[...] = jnp.where(rows_of((8, fine_dev)) == 2, lanes_of((8, fine_dev)), 0)
    fb_tail[...] = jnp.zeros((3, 3, 8, fine_dev), F32)
    fb_tail[:, :, 0:3, :] = fb[:, :, 24:27, :]
    loads[4].wait()
    fl_tail[0:2, :] = fl[24:26, :]
    for g in range(4):
        part = slice(8 * g, 8 * g + 8)
        outside = links(g, slice(0, 128)) >= fine_dev
        for i in range(3):
            for j in range(3):
                block = blocks_at(i, j, g, slice(0, 128))
                fbh[i, j, part, :] = jnp.where(outside, block, 0.0)
                inside = jnp.where(outside, 0.0, block)
                if g < 3:
                    fb[i, j, part, 0:128] = inside
                else:
                    fb_tail[i, j, :, 0:128] = inside

    kv[...] = jnp.zeros((3, 8, 128), F32)
    cidx[24:32, :] = jnp.where(rows == 2, lane, 0)
    cb[:, :, 24:32, :] = jnp.zeros((3, 3, 8, 128), F32)
    loads[2].wait()
    loads[3].wait()
    cb[:, :, 0:27, :] = cb_raw[...]
    cidx[0:26, :] = cl[...]
    diagonal = [cb[i, i, 26:27, :] for i in range(3)]
    largest = functools.reduce(jnp.maximum, diagonal)
    smallest = -functools.reduce(jnp.minimum, diagonal)
    largest, smallest = spread(largest), spread(smallest)
    swap = lane ^ 64
    largest = jnp.maximum(largest, take(largest, swap))
    smallest = jnp.maximum(smallest, take(smallest, swap))
    extremes = jnp.where(lane < 64, largest, smallest)[0:1]

    reduce_start(0, e1, peers1, me1, extremes)
    fine_local(fa, fc)

    quarter = lane >> 5

    def packed(pieces, start):
        rolled = [pltpu.roll(piece, (128 + 32 * g - start) % 128, 1) for g, piece in enumerate(pieces)]
        low = jnp.where(quarter == 0, rolled[0], rolled[1])
        return jnp.where(quarter < 2, low, jnp.where(quarter == 2, rolled[2], rolled[3]))

    parts = [slice(8 * g, 8 * g + 8) for g in range(4)]
    codes = [cidx[part, :] for part in parts]
    for end, start in ((0, 0), (1, coarse_dev - 32)):
        isend[end] = packed(codes, start)
        for i in range(3):
            for j in range(3):
                bsend[end, 3 * i + j] = packed([cb[i, j, part, :] for part in parts], start)
    face_code = isend[0]
    for i in range(3):
        for j in range(3):
            fcb[i, j] = jnp.where(face_code >= coarse_dev, bsend[0, 3 * i + j], 0.0)
            for g in range(4):
                cb[i, j, parts[g], :] = jnp.where(codes[g] >= coarse_dev, 0.0, cb[i, j, parts[g], :])
    for g in range(4):
        cidx[parts[g], :] = codes[g] & 127
    side_copies = []
    for src, dst, device in ((1, 0, after), (0, 1, before), (0, 2, above), (0, 3, below)):
        for kind, (source, sink) in enumerate(((bsend, brecv), (isend, irecv))):
            side_copies.append(
                pltpu.make_async_remote_copy(
                    src_ref=source.at[src],
                    dst_ref=sink.at[dst],
                    send_sem=b_send_sem.at[kind],
                    recv_sem=b_recv_sem.at[kind],
                    device_id=device,
                    device_id_type=MESH,
                )
            )
    for copy in side_copies:
        copy.start()
    head, rest = slice(0, 128), slice(128, fine_dev)
    fa[:, rest] += smooth(rhs[:, rest] - fc[:, rest], rest)
    halves = fine_wait(0)
    fa[:, head] += smooth(rhs[:, head] - fc[:, head] - fine_remote(halves), head)
    fine_send(1, fa)
    extremes = reduce_wait(0, e1, n1, jnp.maximum)
    reduce_start(1, e2, peers2, me2, extremes)
    fine_local(fa, fc)

    def eighths(part):
        for k in (1, 2, 4):
            part = part + pltpu.roll(part, 128 - k, 1)
        return take(part, (lane & 15) * 8)

    def restrict(ref):
        out = eighths(ref[:, 0:128])
        for t in range(1, tiles):
            picked = eighths(ref[:, 128 * t : 128 * t + 128])
            out = jnp.where(lane >> 4 == t, picked, out)
        return out

    fc[...] = rhs[...] - fc[...]
    coarse = restrict(fc)
    remote = fine_remote(fine_wait(1))
    fc[:, head] -= remote
    coarse = coarse - jnp.where(lane < 16, eighths(remote), 0.0)

    def coarse_send(ex, field):
        edge = take(field, jnp.where(lane < 32, lane + (coarse_dev - 32), lane & 31))
        tile = jnp.where(rows < 4, field, edge)
        ksend[ex] = tile
        for k, (dr, dm) in enumerate(OFFSETS):
            pltpu.make_async_remote_copy(
                src_ref=ksend.at[ex],
                dst_ref=krecv.at[ex, k],
                send_sem=k_send_sem,
                recv_sem=k_recv_sem.at[ex],
                device_id=at(-dr, -dm),
                device_id_type=MESH,
            ).start()
        return tile

    def coarse_wait(ex):
        block = krecv.at[ex]
        pltpu.make_async_copy(block, block, k_recv_sem.at[ex]).wait()
        return {offset: krecv[ex, k] for k, offset in enumerate(OFFSETS)}

    def beside(left, right, lower, upper):
        low = jnp.where(quarter == 0, left, right)
        return jnp.where(quarter < 2, low, jnp.where(quarter == 2, lower, upper))

    def folded(accs):
        tile = combine(accs)
        tile = tile + pltpu.roll(tile, 64, 1)
        return tile + pltpu.roll(tile, 32, 1)

    def coarse_local(field):
        accs = [None] * 3
        tables = [spread(field[j : j + 1, :]) for j in range(3)]
        for g in range(4):
            index = cidx[parts[g], :]
            for j in range(3):
                value = take(tables[j], index)
                for i in range(3):
                    term = cb[i, j, parts[g], :] * value
                    accs[i] = term if accs[i] is None else accs[i] + term
        return combine(accs)

    def coarse_remote(halo):
        accs = [None] * 3
        index = isend[0] & 127
        for j in range(3):
            value = take(spread(halo[4 + j : 5 + j, :]), index)
            for i in range(3):
                term = fcb[i, j] * value
                accs[i] = term if accs[i] is None else accs[i] + term
        return jnp.where(lane < 32, folded(accs), 0.0)

    def coarse_ghost(tiles_of, mine):
        around = (
            ((0, -1), None),
            ((0, 1), (mine, tiles_of[0, 2], tiles_of[-1, 1], tiles_of[1, 1])),
            ((-1, 0), (tiles_of[-1, -1], tiles_of[-1, 1], tiles_of[2, 0], mine)),
            ((1, 0), (tiles_of[1, -1], tiles_of[1, 1], mine, tiles_of[2, 0])),
        )
        out = None
        for q, (offset, edges) in enumerate(around):
            code = irecv[q]
            index = code & 127
            full = tiles_of[offset]
            outer = None if edges is None else beside(*edges)
            accs = [None] * 3
            for j in range(3):
                value = take(spread(full[j : j + 1, :]), index)
                if outer is not None:
                    far = take(spread(outer[4 + j : 5 + j, :]), index)
                    value = jnp.where(code >= coarse_dev, far, value)
                for i in range(3):
                    term = brecv[q, 3 * i + j] * value
                    accs[i] = term if accs[i] is None else accs[i] + term
            tile = folded(accs)
            out = tile if out is None else jnp.where(quarter == q, tile, out)
        return out

    def lift_pair(ex, fields, halos):
        for n in range(2):
            for j in range(3):
                lift[n, j] = spread(fields[n][j : j + 1, :])

        def tile(t, carry):
            columns = pl.ds(pl.multiple_of(t * 128, 128), 128)
            accs = [None] * 6
            for g in range(4):
                where = (links(g, columns) >> 3) & 127
                for j in range(3):
                    values = [take(lift[n, j], where) for n in range(2)]
                    for i in range(3):
                        block = blocks_at(i, j, g, columns)
                        for n in range(2):
                            term = block * values[n]
                            k = 3 * n + i
                            accs[k] = term if accs[k] is None else accs[k] + term
            for k in range(6):
                pairs[k, t] = accs[k]
            return carry

        lax.fori_loop(0, tiles, tile, 0, unroll=UNROLL)
        accs = [pairs[k, 0] for k in range(6)]
        for g in range(4):
            where = fl_halo[parts[g], :]
            for j in range(3):
                values = [take(spread(halos[n][4 + j : 5 + j, :]), where) for n in range(2)]
                for i in range(3):
                    block = fbh[i, j, parts[g], :]
                    for n in range(2):
                        accs[3 * n + i] = accs[3 * n + i] + block * values[n]
        images[ex, :, 0:128] = combine_pair(accs)
        for t in range(1, tiles):
            images[ex, :, 128 * t : 128 * t + 128] = combine_pair([pairs[k, t] for k in range(6)])

        def faces(columns):
            total = None
            for j in range(3):
                value = jnp.where(
                    rows < 4, spread(images[ex, j : j + 1, columns]), spread(images[ex, j + 4 : j + 5, columns])
                )
                term = inv[j, :, columns] * value
                total = term if total is None else total + term
            return total

        for t in range(tiles):
            columns = slice(128 * t, 128 * t + 128)
            steps[:, columns] = faces(columns)
        fine_send(3 + ex, steps)

    mine = coarse_send(0, coarse)
    for g in range(4):
        node = links(g, slice(0, 128)) & 255
        fl_halo[parts[g], :] = ((node >> 6) << 5) + ((node & 63) >> 3) + jnp.where(node < 64, 24, 0)
    update = smooth(fc[...])
    fd[...] = update
    fine_send(2, fd)
    fine_local(fd, fa_image)
    extremes = spread(reduce_wait(1, e2, n2, jnp.maximum))
    lowest = jnp.min(extremes)
    largest = jnp.max(jnp.where(lane < 64, extremes, lowest), axis=1, keepdims=True)
    smallest = -jnp.max(jnp.where(lane < 64, lowest, extremes), axis=1, keepdims=True)
    largest, smallest = jnp.broadcast_to(largest, (8, 128)), jnp.broadcast_to(smallest, (8, 128))
    centre = 0.5 * largest + 0.5 * smallest
    width = 0.5 * largest - 0.5 * smallest + 0.125 * largest
    shrink = 1.0 / width
    for kind, sink in enumerate((brecv, irecv)):
        pltpu.make_async_copy(sink, sink, b_recv_sem.at[kind]).wait()

    def keep(ref, k, field):
        for j in range(3):
            ref[j, k : k + 1, :] = field[j : j + 1, :]

    for ex in range(STEPS):
        local = coarse_local(coarse) - centre * coarse
        keep(kv, 2 * ex, coarse)
        base = coarse
        tiles_of = coarse_wait(ex)
        halo = beside(tiles_of[0, -1], tiles_of[0, 1], tiles_of[-1, 0], tiles_of[1, 0])
        coarse = (local + coarse_remote(halo)) * shrink
        ghost = (coarse_ghost(tiles_of, mine) - centre * halo) * shrink
        keep(kv, 2 * ex + 1, coarse)
        pair = (base, coarse), (halo, ghost)
        coarse = (coarse_local(coarse) - centre * coarse + coarse_remote(ghost)) * shrink
        if ex + 1 < STEPS:
            mine = coarse_send(ex + 1, coarse)
            lift_pair(ex, *pair)
            fine_local(steps, step_images.at[ex], 2)
            if ex == 1:
                fa_image[:, head] += fine_remote(fine_wait(2))
                step_images[0, :, head] += fine_remote(fine_wait(3), 2)
    for j in range(3):
        kv[j, BASIS - 1 : BASIS, :] = coarse[j : j + 1, :]

    gram = jnp.zeros((8, 128), F32)
    for k in range(BASIS):
        column = None
        for j in range(3):
            term = kv[j] * spread(kv[j, k : k + 1, :])
            column = term if column is None else column + term
        gram = jnp.where(lane & 7 == k, jnp.sum(column, axis=1, keepdims=True), gram)
    gram = jnp.where(rows == lane >> 3, gram, 0.0)
    gram = jnp.sum(gram, axis=0, keepdims=True)
    reduce_start(2, g1, peers1, me1, gram)
    lift_pair(STEPS - 1, *pair)
    gram = reduce_wait(2, g1, n1, jnp.add)
    reduce_start(3, g2, peers2, me2, gram)
    fine_local(steps, step_images.at[STEPS - 1], 2)
    for ex in range(1, STEPS):
        step_images[ex, :, head] += fine_remote(fine_wait(3 + ex), 2)
    gram = spread(reduce_wait(3, g2, n2, jnp.add))
    entries = {
        (i, j): take(gram, jnp.full((8, 128), 8 * i + j, jnp.int32))
        for i in range(BASIS)
        for j in range(i, BASIS)
    }
    weights = [weight * shrink for weight in coefficients(entries, centre * shrink)]

    def mix(ref):
        out = []
        for j in range(3):
            total = None
            for k, weight in enumerate(weights):
                term = weight[0:1] * ref[j, k : k + 1, :]
                total = term if total is None else total + term
            out.append(total)
        tile = jnp.where(rows == 1, out[1], jnp.where(rows == 2, out[2], 0.0))
        return jnp.where(rows == 0, out[0], tile)

    doubled = [jnp.where(rows < 4, weights[2 * ex], weights[2 * ex + 1]) for ex in range(STEPS)]

    def mix_pairs(tiles_of):
        total = functools.reduce(jnp.add, [w * tile for w, tile in zip(doubled, tiles_of)])
        return total + pltpu.roll(total, 4, 0)

    for t in range(tiles):
        columns = slice(128 * t, 128 * t + 128)
        fc[:, columns] = fc[:, columns] - mix_pairs([images[ex, :, columns] for ex in range(STEPS)])
    error = mix(kv)
    update = smooth(fc[...])
    for t in range(tiles):
        columns = slice(128 * t, 128 * t + 128)
        both_out[0, :, columns] = (fa[:, columns] + update[:, columns] + take(error, 16 * t + (lane >> 3)))[0:3]
        final = fc[:, columns] - fa_image[:, columns]
        final = final + mix_pairs([step_images[ex, :, columns] for ex in range(STEPS)])
        both_out[1, :, columns] = final[0:3]

    pltpu.make_async_copy(hrecv, hrecv, halo_send_sem).wait()
    pltpu.make_async_copy(krecv, krecv, k_send_sem).wait()
    for kind, sink in enumerate((brecv, irecv)):
        pltpu.make_async_copy(sink, sink, b_send_sem.at[kind]).wait()
    for buffer, count in ((e1, n1), (e2, n2), (g1, n1), (g2, n2)):
        block = buffer.at[pl.ds(0, count - 1)]
        pltpu.make_async_copy(block, block, red_send_sem).wait()


def body(regions, depth_y, depth_z, right_side, fine_blocks, fine_links, coarse_blocks, coarse_links):
    fine_dev, coarse_dev = right_side.shape[1], coarse_blocks.shape[3]
    n1, n2 = regions * depth_y, depth_z * 2
    exchanges = 3 + STEPS
    reach = len(OFFSETS)
    vmem = pl.BlockSpec(memory_space=pltpu.VMEM)
    hbm = pl.BlockSpec(memory_space=pltpu.HBM)
    out = pltpu.VMEM((2, 3, fine_dev), F32)
    both = pl.pallas_call(
        functools.partial(kernel, regions, depth_y, depth_z, fine_dev, coarse_dev),
        out_shape=out,
        in_specs=[hbm] * 5,
        out_specs=vmem,
        scratch_shapes=[
            pltpu.VMEM((3, fine_dev), F32),
            pltpu.VMEM((3, 3, SLOTS, fine_dev), F32),
            pltpu.VMEM((3, 3, 8, fine_dev), F32),
            pltpu.VMEM((3, 3, PAD, 128), F32),
            pltpu.VMEM((SLOTS - 1, fine_dev), jnp.int32),
            pltpu.VMEM((8, fine_dev), jnp.int32),
            pltpu.VMEM((3, 3, SLOTS, 128), F32),
            pltpu.VMEM((3, 3, PAD, 128), F32),
            pltpu.VMEM((SLOTS - 1, 128), jnp.int32),
            pltpu.VMEM((PAD, 128), jnp.int32),
            pltpu.VMEM((3, 8, fine_dev), F32),
            pltpu.VMEM((8, fine_dev), F32),
            pltpu.VMEM((8, fine_dev), F32),
            pltpu.VMEM((8, fine_dev), F32),
            pltpu.VMEM((8, fine_dev), F32),
            pltpu.VMEM((8, fine_dev), F32),
            pltpu.VMEM((8, fine_dev), F32),
            pltpu.VMEM((STEPS, 8, fine_dev), F32),
            pltpu.VMEM((PAD, 128), jnp.int32),
            pltpu.VMEM((2, 3, 8, 128), F32),
            pltpu.VMEM((6, fine_dev // 128, 8, 128), F32),
            pltpu.VMEM((STEPS, 8, fine_dev), F32),
            pltpu.VMEM((6, fine_dev // 128, 8, 128), F32),
            pltpu.VMEM((3, 8, 128), F32),
            pltpu.VMEM((2 * exchanges, 8, 128), F32),
            pltpu.VMEM((4 * exchanges, 8, 128), F32),
            pltpu.VMEM((STEPS, 8, 128), F32),
            pltpu.VMEM((STEPS, reach, 8, 128), F32),
            pltpu.VMEM((2, 9, 8, 128), F32),
            pltpu.VMEM((4, 9, 8, 128), F32),
            pltpu.VMEM((2, 8, 128), jnp.int32),
            pltpu.VMEM((4, 8, 128), jnp.int32),
            pltpu.VMEM((3, 3, 8, 128), F32),
            pltpu.VMEM((n1, 1, 128), F32),
            pltpu.VMEM((n2, 1, 128), F32),
            pltpu.VMEM((n1, 1, 128), F32),
            pltpu.VMEM((n2, 1, 128), F32),
            pltpu.VMEM((4, 1, 128), F32),
            pltpu.SemaphoreType.DMA((5,)),
            pltpu.SemaphoreType.DMA,
            pltpu.SemaphoreType.DMA((exchanges,)),
            pltpu.SemaphoreType.DMA,
            pltpu.SemaphoreType.DMA((STEPS,)),
            pltpu.SemaphoreType.DMA((2,)),
            pltpu.SemaphoreType.DMA((2,)),
            pltpu.SemaphoreType.DMA,
            pltpu.SemaphoreType.DMA((4,)),
        ],
        compiler_params=pltpu.CompilerParams(
            collective_id=0, has_side_effects=True, vmem_limit_bytes=60 * 1024 * 1024
        ),
    )(
        right_side,
        jnp.transpose(fine_blocks, (1, 2, 0, 3)),
        fine_links,
        jnp.transpose(coarse_blocks, (1, 2, 0, 3)),
        coarse_links,
    )
    return both[0], both[1]


def solution(mesh):
    regions, members = mesh.shape["region"], mesh.shape["member"]
    depth_y = 4 if members % 8 == 0 else 2
    depth_z = members // (2 * depth_y)
    flat = ("region", "member")
    return jax.shard_map(
        functools.partial(body, regions, depth_y, depth_z),
        mesh=mesh,
        in_specs=(
            P(None, flat),
            P(None, None, None, flat),
            P(None, flat),
            P(None, None, None, flat),
            P(None, flat),
        ),
        out_specs=(P(None, flat), P(None, flat)),
        check_vma=False,
    )
```

```python
import functools

import jax
import jax.numpy as jnp
from jax import lax
from jax.experimental import pallas as pl
from jax.experimental.pallas import tpu as pltpu
from jax.sharding import PartitionSpec as P

STEPS = 3
BASIS = 2 * STEPS + 1
RELAX = 0.6
SLOTS = 27
PAD = 32
UNROLL = 2
MESH = pl.DeviceIdType.MESH
OFFSETS = ((-1, -1), (-1, 1), (1, -1), (1, 1), (0, 2), (2, 0), (0, -1), (0, 1), (-1, 0), (1, 0))
F32 = jnp.float32


def lanes_of(shape):
    return lax.broadcasted_iota(jnp.int32, shape, len(shape) - 1)


def rows_of(shape):
    return lax.broadcasted_iota(jnp.int32, shape, len(shape) - 2)


def take(table, index):
    return jnp.take_along_axis(table, index, axis=1, mode="promise_in_bounds")


def spread(row):
    return jnp.broadcast_to(row, (8, 128))


def combine(accs):
    rows = rows_of((8, 128))
    sums = [jnp.sum(acc, axis=0, keepdims=True) for acc in accs]
    tile = jnp.where(rows & 3 == 2, sums[2], 0.0)
    tile = jnp.where(rows & 3 == 1, sums[1], tile)
    return jnp.where(rows & 3 == 0, sums[0], tile)


def combine_pair(accs):
    return jnp.where(rows_of((8, 128)) < 4, combine(accs[:3]), combine(accs[3:]))


def coefficients(gram, shifts):
    def image(x):
        y = [None] * (len(x) + 1)
        for i, value in enumerate(x):
            y[i] = value * shifts[i] if y[i] is None else y[i] + value * shifts[i]
            y[i + 1] = value
        return y

    def total(terms):
        while len(terms) > 1:
            terms = [terms[k] + terms[k + 1] if k + 1 < len(terms) else terms[k] for k in range(0, len(terms), 2)]
        return terms[0]

    def products(x, count):
        return [
            total([gram[min(i, j), max(i, j)] * value for j, value in enumerate(x)]) for i in range(count)
        ]

    def dot(x, y):
        return total([left * right for left, right in zip(x, y)])

    def axpy(x, a, y):
        out = []
        for i in range(max(len(x), len(y))):
            if i >= len(y):
                out.append(x[i])
            elif i >= len(x):
                out.append(a * y[i])
            else:
                out.append(x[i] + a * y[i])
        return out

    def shadow(x):
        return total([gram[0, j] * value for j, value in enumerate(x)])

    one = jnp.ones_like(shifts[0])
    resid, direction = [one], [one]
    error = []
    rho = gram[0, 0]
    for step in range(STEPS):
        move = image(direction)
        alpha = rho / shadow(move)
        middle = axpy(resid, -alpha, move)
        second = image(middle)
        against = products(second, len(second))
        omega = dot(middle, against) / dot(second, against)
        error = axpy(axpy(error, alpha, direction), omega, middle)
        if step + 1 < STEPS:
            resid = axpy(middle, -omega, second)
            rho_new = shadow(resid)
            beta = rho_new / rho * (alpha / omega)
            direction = axpy(resid, beta, axpy(direction, -omega, move))
            rho = rho_new
    return error


def kernel(
    regions, depth_y, depth_z, fine_dev, coarse_dev,
    rhs_hbm, fb_hbm, fl_hbm, cb_hbm, cl_hbm,
    both_out,
    rhs_raw, fb, fb_tail, fbh, fl, fl_tail, cb_raw, cb, cl, cidx, inv, rhs, fa, fc, fd, fa_image, steps, step_images, fl_halo, lift, pairs, images, tab, kv,
    hsend, hrecv, ksend, krecv, bsend, brecv, isend, irecv, fcb, e1, e2, g1, g2, row_send,
    load_sem, halo_send_sem, halo_recv_sem, k_send_sem, k_recv_sem, b_send_sem, b_recv_sem,
    red_send_sem, red_recv_sem,
):
    members = depth_y * depth_z * 2
    tiles = fine_dev // 128
    region = lax.axis_index("region")
    member = lax.axis_index("member")
    z, y, core = lax.div(member, 2 * depth_y), lax.rem(lax.div(member, 2), depth_y), lax.rem(member, 2)
    n1, n2 = regions * depth_y, depth_z * 2
    me1, me2 = region * depth_y + y, z * 2 + core
    region_at = [region] + [lax.rem(region + s, regions) for s in range(1, regions)]
    y_at = [member] + [member + 2 * (lax.rem(y + s, depth_y) - y) for s in range(1, depth_y)]
    z_at = [member] + [member + 2 * depth_y * (lax.rem(z + s, depth_z) - z) for s in range(1, depth_z)]
    def far_first(outer, inner, pair):
        around = lambda s, count: min(s, count - s)
        steps = [(s, t) for s in range(len(outer)) for t in range(len(inner))][1:]
        steps.sort(key=lambda st: -around(st[0], len(outer)) - around(st[1], len(inner)))
        return [pair(outer[s], inner[t]) for s, t in steps]

    peers1 = far_first(region_at, y_at, lambda r, m: (r, m))
    peers2 = far_first(z_at, [0, 1 - 2 * core], lambda m, flip: (region, m + flip))

    def at(dr, dm):
        r = region if dr == 0 else lax.rem(region + (regions + dr), regions)
        m = member if dm == 0 else lax.rem(member + (members + dm), members)
        return r, m

    after, before, above, below = at(0, 1), at(0, -1), at(1, 0), at(-1, 0)

    loads = [
        pltpu.make_async_copy(rhs_hbm, rhs_raw, load_sem.at[4]),
        pltpu.make_async_copy(fb_hbm, fb, load_sem.at[0]),
        pltpu.make_async_copy(cb_hbm, cb_raw, load_sem.at[1]),
        pltpu.make_async_copy(cl_hbm, cl, load_sem.at[2]),
        pltpu.make_async_copy(fl_hbm, fl, load_sem.at[3]),
    ]
    loads[0].start()
    for i in range(3):
        for j in range(3):
            pltpu.make_async_copy(fb_hbm.at[i, j], fb.at[i, j], load_sem.at[0]).start()
    for load in loads[2:]:
        load.start()

    barrier = pltpu.get_barrier_semaphore()
    for dr, dm in OFFSETS:
        device = at(-dr, -dm)
        pl.semaphore_signal(barrier, inc=1, device_id=device, device_id_type=MESH)

    for device in peers1 + peers2:
        pl.semaphore_signal(barrier, inc=1, device_id=device, device_id_type=MESH)

    lane = lanes_of((8, 128))
    rows = rows_of((8, 128))

    def halo_copies(ex, which):
        pairs = (
            (1, 0, after),
            (0, 1, before),
            (0, 2, above),
            (0, 3, below),
        )
        return [
            pltpu.make_async_remote_copy(
                src_ref=hsend.at[2 * ex + src],
                dst_ref=hrecv.at[4 * ex + dst],
                send_sem=halo_send_sem,
                recv_sem=halo_recv_sem.at[ex],
                device_id=device,
                device_id_type=MESH,
            )
            for src, dst, device in pairs
            if src in which
        ]

    def halo_send(ex, first, last):
        hsend[2 * ex] = first
        hsend[2 * ex + 1] = last
        for copy in halo_copies(ex, (0, 1)):
            copy.start()

    def halo_wait(ex):
        block = hrecv.at[pl.ds(4 * ex, 4)]
        pltpu.make_async_copy(block, block, halo_recv_sem.at[ex]).wait()
        return [hrecv[4 * ex + k] for k in range(4)]

    def reduce_start(which, buffer, peers, me, value):
        row_send[which] = value
        buffer[me] = value
        for device in peers:
            pltpu.make_async_remote_copy(
                src_ref=row_send.at[which],
                dst_ref=buffer.at[me],
                send_sem=red_send_sem,
                recv_sem=red_recv_sem.at[which],
                device_id=device,
                device_id_type=MESH,
            ).start()

    def reduce_wait(which, buffer, count, op):
        block = buffer.at[pl.ds(0, count - 1)]
        pltpu.make_async_copy(block, block, red_recv_sem.at[which]).wait()
        return functools.reduce(op, [buffer[k] for k in range(count)])

    def smooth(value, columns=slice(None)):
        total = inv[0, :, columns] * value[0:1, :]
        for j in range(1, 3):
            total = total + inv[j, :, columns] * value[j : j + 1, :]
        return total

    def links(g, columns):
        return fl[8 * g : 8 * g + 8, columns] if g < 3 else fl_tail[:, columns]

    def blocks_at(i, j, g, columns):
        return fb[i, j, 8 * g : 8 * g + 8, columns] if g < 3 else fb_tail[i, j, :, columns]

    def fine_local(source, target, count=1):
        for n in range(count):
            for j in range(3):
                for r in range(tiles):
                    row = 4 * n + j
                    tab[3 * n + j, r] = spread(source[row : row + 1, 128 * r : 128 * r + 128])

        def tile(t, carry):
            columns = pl.ds(pl.multiple_of(t * 128, 128), 128)
            accs = [None] * (3 * count)
            for g in range(4):
                index = links(g, columns)
                where = index & 127
                bits = [(index & (128 << k)) != 0 for k in range(3)]
                for j in range(3):
                    values = []
                    for n in range(count):
                        found = [take(tab[3 * n + j, r], where) for r in range(tiles)]
                        for bit in bits:
                            found = [
                                jnp.where(bit, found[2 * q + 1], found[2 * q])
                                for q in range(len(found) // 2)
                            ]
                        values.append(found[0])
                    for i in range(3):
                        block = blocks_at(i, j, g, columns)
                        for n in range(count):
                            term = block * values[n]
                            k = 3 * n + i
                            accs[k] = term if accs[k] is None else accs[k] + term
            for k in range(3 * count):
                pairs[k, t] = accs[k]
            return carry

        lax.fori_loop(0, tiles, tile, 0, unroll=UNROLL if count == 1 else 1)
        for t in range(tiles):
            sums = [pairs[k, t] for k in range(3 * count)]
            target[:, 128 * t : 128 * t + 128] = combine(sums) if count == 1 else combine_pair(sums)

    def fine_remote(halves, count=1):
        accs = [None] * (3 * count)
        for g in range(4):
            part = slice(8 * g, 8 * g + 8)
            index = links(g, slice(0, 128))
            where = index & 127
            bit = (index & 128) != 0
            for j in range(3):
                values = []
                for n in range(count):
                    row = 4 * n + j
                    low, high = (take(spread(half[row : row + 1, :]), where) for half in halves)
                    values.append(jnp.where(bit, high, low))
                for i in range(3):
                    block = fbh[i, j, part, :]
                    for n in range(count):
                        term = block * values[n]
                        k = 3 * n + i
                        accs[k] = term if accs[k] is None else accs[k] + term
        return combine(accs) if count == 1 else combine_pair(accs)

    def fine_send(ex, field):
        within = lane & 63
        halo_send(
            ex,
            take(field[:, 0:128], within),
            take(field[:, fine_dev - 128 : fine_dev], within + 64),
        )

    def fine_wait(ex):
        left, right, lower, upper = halo_wait(ex)
        return jnp.where(lane < 64, left, right), jnp.where(lane < 64, lower, upper)

    rhs[...] = jnp.zeros((8, fine_dev), F32)
    loads[0].wait()
    rhs[0:3, :] = rhs_raw[...]
    rhs[4:7, :] = rhs_raw[...]
    loads[1].wait()

    def start_tile(t, carry):
        columns = pl.ds(pl.multiple_of(t * 128, 128), 128)
        (a, b, c), (d, e, f), (g_, h_, i_) = [
            [spread(fb[i, j, 26:27, columns]) for j in range(3)] for i in range(3)
        ]
        co_a = e * i_ - f * h_
        co_b = f * g_ - d * i_
        co_c = d * h_ - e * g_
        scale = RELAX / (a * co_a + b * co_b + c * co_c)
        adjugate = [
            [co_a, c * h_ - b * i_, b * f - c * e],
            [co_b, a * i_ - c * g_, c * d - a * f],
            [co_c, b * g_ - a * h_, a * e - b * d],
        ]
        total = None
        for j in range(3):
            column = jnp.where(rows & 3 == 2, adjugate[2][j], 0.0)
            column = jnp.where(rows & 3 == 1, adjugate[1][j], column)
            column = jnp.where(rows & 3 == 0, adjugate[0][j], column) * scale
            inv[j, :, columns] = column
            term = column * spread(rhs[j : j + 1, columns])
            total = term if total is None else total + term
        fa[:, columns] = total
        return carry

    start_tile(0, 0)
    start_tile(tiles - 1, 0)
    pl.semaphore_wait(barrier, len(OFFSETS) + (n1 - 1) + (n2 - 1))
    fine_send(0, fa)
    lax.fori_loop(1, tiles - 1, start_tile, 0, unroll=UNROLL)

    fl_tail[...] = jnp.where(rows_of((8, fine_dev)) == 2, lanes_of((8, fine_dev)), 0)
    fb_tail[...] = jnp.zeros((3, 3, 8, fine_dev), F32)
    fb_tail[:, :, 0:3, :] = fb[:, :, 24:27, :]
    loads[4].wait()
    fl_tail[0:2, :] = fl[24:26, :]
    for g in range(4):
        part = slice(8 * g, 8 * g + 8)
        outside = links(g, slice(0, 128)) >= fine_dev
        for i in range(3):
            for j in range(3):
                block = blocks_at(i, j, g, slice(0, 128))
                fbh[i, j, part, :] = jnp.where(outside, block, 0.0)
                inside = jnp.where(outside, 0.0, block)
                if g < 3:
                    fb[i, j, part, 0:128] = inside
                else:
                    fb_tail[i, j, :, 0:128] = inside

    kv[...] = jnp.zeros((3, 8, 128), F32)
    cidx[24:32, :] = jnp.where(rows == 2, lane, 0)
    cb[:, :, 24:32, :] = jnp.zeros((3, 3, 8, 128), F32)
    loads[2].wait()
    loads[3].wait()
    cb[:, :, 0:27, :] = cb_raw[...]
    cidx[0:26, :] = cl[...]
    diagonal = [cb[i, i, 26:27, :] for i in range(3)]
    largest = functools.reduce(jnp.maximum, diagonal)
    smallest = -functools.reduce(jnp.minimum, diagonal)
    largest, smallest = spread(largest), spread(smallest)
    swap = lane ^ 64
    largest = jnp.maximum(largest, take(largest, swap))
    smallest = jnp.maximum(smallest, take(smallest, swap))
    extremes = jnp.where(lane < 64, largest, smallest)[0:1]

    reduce_start(0, e1, peers1, me1, extremes)
    fine_local(fa, fc)

    quarter = lane >> 5

    def packed(pieces, start):
        rolled = [pltpu.roll(piece, (128 + 32 * g - start) % 128, 1) for g, piece in enumerate(pieces)]
        low = jnp.where(quarter == 0, rolled[0], rolled[1])
        return jnp.where(quarter < 2, low, jnp.where(quarter == 2, rolled[2], rolled[3]))

    parts = [slice(8 * g, 8 * g + 8) for g in range(4)]
    codes = [cidx[part, :] for part in parts]
    for end, start in ((0, 0), (1, coarse_dev - 32)):
        isend[end] = packed(codes, start)
        for i in range(3):
            for j in range(3):
                bsend[end, 3 * i + j] = packed([cb[i, j, part, :] for part in parts], start)
    face_code = isend[0]
    for i in range(3):
        for j in range(3):
            fcb[i, j] = jnp.where(face_code >= coarse_dev, bsend[0, 3 * i + j], 0.0)
            for g in range(4):
                cb[i, j, parts[g], :] = jnp.where(codes[g] >= coarse_dev, 0.0, cb[i, j, parts[g], :])
    for g in range(4):
        cidx[parts[g], :] = codes[g] & 127
    side_copies = []
    for src, dst, device in ((1, 0, after), (0, 1, before), (0, 2, above), (0, 3, below)):
        for kind, (source, sink) in enumerate(((bsend, brecv), (isend, irecv))):
            side_copies.append(
                pltpu.make_async_remote_copy(
                    src_ref=source.at[src],
                    dst_ref=sink.at[dst],
                    send_sem=b_send_sem.at[kind],
                    recv_sem=b_recv_sem.at[kind],
                    device_id=device,
                    device_id_type=MESH,
                )
            )
    for copy in side_copies:
        copy.start()
    head, rest = slice(0, 128), slice(128, fine_dev)
    fa[:, rest] += smooth(rhs[:, rest] - fc[:, rest], rest)
    halves = fine_wait(0)
    fa[:, head] += smooth(rhs[:, head] - fc[:, head] - fine_remote(halves), head)
    fine_send(1, fa)
    extremes = reduce_wait(0, e1, n1, jnp.maximum)
    reduce_start(1, e2, peers2, me2, extremes)
    fine_local(fa, fc)

    def eighths(part):
        for k in (1, 2, 4):
            part = part + pltpu.roll(part, 128 - k, 1)
        return take(part, (lane & 15) * 8)

    def restrict(ref):
        out = eighths(ref[:, 0:128])
        for t in range(1, tiles):
            picked = eighths(ref[:, 128 * t : 128 * t + 128])
            out = jnp.where(lane >> 4 == t, picked, out)
        return out

    fc[...] = rhs[...] - fc[...]
    coarse = restrict(fc)
    remote = fine_remote(fine_wait(1))
    fc[:, head] -= remote
    coarse = coarse - jnp.where(lane < 16, eighths(remote), 0.0)

    def coarse_send(ex, field):
        edge = take(field, jnp.where(lane < 32, lane + (coarse_dev - 32), lane & 31))
        tile = jnp.where(rows < 4, field, edge)
        ksend[ex] = tile
        for k, (dr, dm) in enumerate(OFFSETS):
            pltpu.make_async_remote_copy(
                src_ref=ksend.at[ex],
                dst_ref=krecv.at[ex, k],
                send_sem=k_send_sem,
                recv_sem=k_recv_sem.at[ex],
                device_id=at(-dr, -dm),
                device_id_type=MESH,
            ).start()
        return tile

    def coarse_wait(ex):
        block = krecv.at[ex]
        pltpu.make_async_copy(block, block, k_recv_sem.at[ex]).wait()
        return {offset: krecv[ex, k] for k, offset in enumerate(OFFSETS)}

    def beside(left, right, lower, upper):
        low = jnp.where(quarter == 0, left, right)
        return jnp.where(quarter < 2, low, jnp.where(quarter == 2, lower, upper))

    def folded(accs):
        tile = combine(accs)
        tile = tile + pltpu.roll(tile, 64, 1)
        return tile + pltpu.roll(tile, 32, 1)

    def coarse_local(field):
        accs = [None] * 3
        tables = [spread(field[j : j + 1, :]) for j in range(3)]
        for g in range(4):
            index = cidx[parts[g], :]
            for j in range(3):
                value = take(tables[j], index)
                for i in range(3):
                    term = cb[i, j, parts[g], :] * value
                    accs[i] = term if accs[i] is None else accs[i] + term
        return combine(accs)

    def coarse_remote(halo):
        accs = [None] * 3
        index = isend[0] & 127
        for j in range(3):
            value = take(spread(halo[4 + j : 5 + j, :]), index)
            for i in range(3):
                term = fcb[i, j] * value
                accs[i] = term if accs[i] is None else accs[i] + term
        return jnp.where(lane < 32, folded(accs), 0.0)

    def coarse_ghost(tiles_of, mine):
        around = (
            ((0, -1), None),
            ((0, 1), (mine, tiles_of[0, 2], tiles_of[-1, 1], tiles_of[1, 1])),
            ((-1, 0), (tiles_of[-1, -1], tiles_of[-1, 1], tiles_of[2, 0], mine)),
            ((1, 0), (tiles_of[1, -1], tiles_of[1, 1], mine, tiles_of[2, 0])),
        )
        out = None
        for q, (offset, edges) in enumerate(around):
            code = irecv[q]
            index = code & 127
            full = tiles_of[offset]
            outer = None if edges is None else beside(*edges)
            accs = [None] * 3
            for j in range(3):
                value = take(spread(full[j : j + 1, :]), index)
                if outer is not None:
                    far = take(spread(outer[4 + j : 5 + j, :]), index)
                    value = jnp.where(code >= coarse_dev, far, value)
                for i in range(3):
                    term = brecv[q, 3 * i + j] * value
                    accs[i] = term if accs[i] is None else accs[i] + term
            tile = folded(accs)
            out = tile if out is None else jnp.where(quarter == q, tile, out)
        return out

    def lift_pair(ex, fields, halos):
        for n in range(2):
            for j in range(3):
                lift[n, j] = spread(fields[n][j : j + 1, :])

        def tile(t, carry):
            columns = pl.ds(pl.multiple_of(t * 128, 128), 128)
            accs = [None] * 6
            for g in range(4):
                where = (links(g, columns) >> 3) & 127
                for j in range(3):
                    values = [take(lift[n, j], where) for n in range(2)]
                    for i in range(3):
                        block = blocks_at(i, j, g, columns)
                        for n in range(2):
                            term = block * values[n]
                            k = 3 * n + i
                            accs[k] = term if accs[k] is None else accs[k] + term
            for k in range(6):
                pairs[k, t] = accs[k]
            return carry

        lax.fori_loop(0, tiles, tile, 0, unroll=UNROLL)
        accs = [pairs[k, 0] for k in range(6)]
        for g in range(4):
            where = fl_halo[parts[g], :]
            for j in range(3):
                values = [take(spread(halos[n][4 + j : 5 + j, :]), where) for n in range(2)]
                for i in range(3):
                    block = fbh[i, j, parts[g], :]
                    for n in range(2):
                        accs[3 * n + i] = accs[3 * n + i] + block * values[n]
        images[ex, :, 0:128] = combine_pair(accs)
        for t in range(1, tiles):
            images[ex, :, 128 * t : 128 * t + 128] = combine_pair([pairs[k, t] for k in range(6)])

        def faces(columns):
            total = None
            for j in range(3):
                value = jnp.where(
                    rows < 4, spread(images[ex, j : j + 1, columns]), spread(images[ex, j + 4 : j + 5, columns])
                )
                term = inv[j, :, columns] * value
                total = term if total is None else total + term
            return total

        for t in range(tiles):
            columns = slice(128 * t, 128 * t + 128)
            steps[:, columns] = faces(columns)
        fine_send(3 + ex, steps)

    mine = coarse_send(0, coarse)
    for g in range(4):
        node = links(g, slice(0, 128)) & 255
        fl_halo[parts[g], :] = ((node >> 6) << 5) + ((node & 63) >> 3) + jnp.where(node < 64, 24, 0)
    update = smooth(fc[...])
    fd[...] = update
    fine_send(2, fd)
    fine_local(fd, fa_image)
    extremes = spread(reduce_wait(1, e2, n2, jnp.maximum))
    lowest = jnp.min(extremes)
    largest = jnp.max(jnp.where(lane < 64, extremes, lowest), axis=1, keepdims=True)
    smallest = -jnp.max(jnp.where(lane < 64, lowest, extremes), axis=1, keepdims=True)
    largest, smallest = jnp.broadcast_to(largest, (8, 128)), jnp.broadcast_to(smallest, (8, 128))
    middle = 0.5 * largest + 0.5 * smallest
    centres = [middle, 0.1 * smallest, 1.3 * largest, smallest, largest, middle]
    width = 0.5 * largest - 0.5 * smallest + 0.125 * largest
    shrink = 1.0 / width
    for kind, sink in enumerate((brecv, irecv)):
        pltpu.make_async_copy(sink, sink, b_recv_sem.at[kind]).wait()

    def keep(ref, k, field):
        for j in range(3):
            ref[j, k : k + 1, :] = field[j : j + 1, :]

    for ex in range(STEPS):
        local = coarse_local(coarse) - centres[2 * ex] * coarse
        keep(kv, 2 * ex, coarse)
        base = coarse
        tiles_of = coarse_wait(ex)
        halo = beside(tiles_of[0, -1], tiles_of[0, 1], tiles_of[-1, 0], tiles_of[1, 0])
        coarse = (local + coarse_remote(halo)) * shrink
        ghost = (coarse_ghost(tiles_of, mine) - centres[2 * ex] * halo) * shrink
        keep(kv, 2 * ex + 1, coarse)
        pair = (base, coarse), (halo, ghost)
        coarse = (coarse_local(coarse) - centres[2 * ex + 1] * coarse + coarse_remote(ghost)) * shrink
        if ex + 1 < STEPS:
            mine = coarse_send(ex + 1, coarse)
            lift_pair(ex, *pair)
            fine_local(steps, step_images.at[ex], 2)
            if ex == 1:
                fa_image[:, head] += fine_remote(fine_wait(2))
                step_images[0, :, head] += fine_remote(fine_wait(3), 2)
    for j in range(3):
        kv[j, BASIS - 1 : BASIS, :] = coarse[j : j + 1, :]

    gram = jnp.zeros((8, 128), F32)
    for k in range(BASIS):
        column = None
        for j in range(3):
            term = kv[j] * spread(kv[j, k : k + 1, :])
            column = term if column is None else column + term
        gram = jnp.where(lane & 7 == k, jnp.sum(column, axis=1, keepdims=True), gram)
    gram = jnp.where(rows == lane >> 3, gram, 0.0)
    gram = jnp.sum(gram, axis=0, keepdims=True)
    reduce_start(2, g1, peers1, me1, gram)
    lift_pair(STEPS - 1, *pair)
    gram = reduce_wait(2, g1, n1, jnp.add)
    reduce_start(3, g2, peers2, me2, gram)
    fine_local(steps, step_images.at[STEPS - 1], 2)
    for ex in range(1, STEPS):
        step_images[ex, :, head] += fine_remote(fine_wait(3 + ex), 2)
    gram = spread(reduce_wait(3, g2, n2, jnp.add))
    entries = {
        (i, j): take(gram, jnp.full((8, 128), 8 * i + j, jnp.int32))
        for i in range(BASIS)
        for j in range(i, BASIS)
    }
    weights = [weight * shrink for weight in coefficients(entries, [centre * shrink for centre in centres])]

    def mix(ref):
        out = []
        for j in range(3):
            total = None
            for k, weight in enumerate(weights):
                term = weight[0:1] * ref[j, k : k + 1, :]
                total = term if total is None else total + term
            out.append(total)
        tile = jnp.where(rows == 1, out[1], jnp.where(rows == 2, out[2], 0.0))
        return jnp.where(rows == 0, out[0], tile)

    doubled = [jnp.where(rows < 4, weights[2 * ex], weights[2 * ex + 1]) for ex in range(STEPS)]

    def mix_pairs(tiles_of):
        total = functools.reduce(jnp.add, [w * tile for w, tile in zip(doubled, tiles_of)])
        return total + pltpu.roll(total, 4, 0)

    for t in range(tiles):
        columns = slice(128 * t, 128 * t + 128)
        fc[:, columns] = fc[:, columns] - mix_pairs([images[ex, :, columns] for ex in range(STEPS)])
    error = mix(kv)
    update = smooth(fc[...])
    for t in range(tiles):
        columns = slice(128 * t, 128 * t + 128)
        both_out[0, :, columns] = (fa[:, columns] + update[:, columns] + take(error, 16 * t + (lane >> 3)))[0:3]
        final = fc[:, columns] - fa_image[:, columns]
        final = final + mix_pairs([step_images[ex, :, columns] for ex in range(STEPS)])
        both_out[1, :, columns] = final[0:3]

    pltpu.make_async_copy(hrecv, hrecv, halo_send_sem).wait()
    pltpu.make_async_copy(krecv, krecv, k_send_sem).wait()
    for kind, sink in enumerate((brecv, irecv)):
        pltpu.make_async_copy(sink, sink, b_send_sem.at[kind]).wait()
    for buffer, count in ((e1, n1), (e2, n2), (g1, n1), (g2, n2)):
        block = buffer.at[pl.ds(0, count - 1)]
        pltpu.make_async_copy(block, block, red_send_sem).wait()


def body(regions, depth_y, depth_z, right_side, fine_blocks, fine_links, coarse_blocks, coarse_links):
    fine_dev, coarse_dev = right_side.shape[1], coarse_blocks.shape[3]
    n1, n2 = regions * depth_y, depth_z * 2
    exchanges = 3 + STEPS
    reach = len(OFFSETS)
    vmem = pl.BlockSpec(memory_space=pltpu.VMEM)
    hbm = pl.BlockSpec(memory_space=pltpu.HBM)
    out = pltpu.VMEM((2, 3, fine_dev), F32)
    both = pl.pallas_call(
        functools.partial(kernel, regions, depth_y, depth_z, fine_dev, coarse_dev),
        out_shape=out,
        in_specs=[hbm] * 5,
        out_specs=vmem,
        scratch_shapes=[
            pltpu.VMEM((3, fine_dev), F32),
            pltpu.VMEM((3, 3, SLOTS, fine_dev), F32),
            pltpu.VMEM((3, 3, 8, fine_dev), F32),
            pltpu.VMEM((3, 3, PAD, 128), F32),
            pltpu.VMEM((SLOTS - 1, fine_dev), jnp.int32),
            pltpu.VMEM((8, fine_dev), jnp.int32),
            pltpu.VMEM((3, 3, SLOTS, 128), F32),
            pltpu.VMEM((3, 3, PAD, 128), F32),
            pltpu.VMEM((SLOTS - 1, 128), jnp.int32),
            pltpu.VMEM((PAD, 128), jnp.int32),
            pltpu.VMEM((3, 8, fine_dev), F32),
            pltpu.VMEM((8, fine_dev), F32),
            pltpu.VMEM((8, fine_dev), F32),
            pltpu.VMEM((8, fine_dev), F32),
            pltpu.VMEM((8, fine_dev), F32),
            pltpu.VMEM((8, fine_dev), F32),
            pltpu.VMEM((8, fine_dev), F32),
            pltpu.VMEM((STEPS, 8, fine_dev), F32),
            pltpu.VMEM((PAD, 128), jnp.int32),
            pltpu.VMEM((2, 3, 8, 128), F32),
            pltpu.VMEM((6, fine_dev // 128, 8, 128), F32),
            pltpu.VMEM((STEPS, 8, fine_dev), F32),
            pltpu.VMEM((6, fine_dev // 128, 8, 128), F32),
            pltpu.VMEM((3, 8, 128), F32),
            pltpu.VMEM((2 * exchanges, 8, 128), F32),
            pltpu.VMEM((4 * exchanges, 8, 128), F32),
            pltpu.VMEM((STEPS, 8, 128), F32),
            pltpu.VMEM((STEPS, reach, 8, 128), F32),
            pltpu.VMEM((2, 9, 8, 128), F32),
            pltpu.VMEM((4, 9, 8, 128), F32),
            pltpu.VMEM((2, 8, 128), jnp.int32),
            pltpu.VMEM((4, 8, 128), jnp.int32),
            pltpu.VMEM((3, 3, 8, 128), F32),
            pltpu.VMEM((n1, 1, 128), F32),
            pltpu.VMEM((n2, 1, 128), F32),
            pltpu.VMEM((n1, 1, 128), F32),
            pltpu.VMEM((n2, 1, 128), F32),
            pltpu.VMEM((4, 1, 128), F32),
            pltpu.SemaphoreType.DMA((5,)),
            pltpu.SemaphoreType.DMA,
            pltpu.SemaphoreType.DMA((exchanges,)),
            pltpu.SemaphoreType.DMA,
            pltpu.SemaphoreType.DMA((STEPS,)),
            pltpu.SemaphoreType.DMA((2,)),
            pltpu.SemaphoreType.DMA((2,)),
            pltpu.SemaphoreType.DMA,
            pltpu.SemaphoreType.DMA((4,)),
        ],
        compiler_params=pltpu.CompilerParams(
            collective_id=0, has_side_effects=True, vmem_limit_bytes=60 * 1024 * 1024
        ),
    )(
        right_side,
        jnp.transpose(fine_blocks, (1, 2, 0, 3)),
        fine_links,
        jnp.transpose(coarse_blocks, (1, 2, 0, 3)),
        coarse_links,
    )
    return both[0], both[1]


def solution(mesh):
    regions, members = mesh.shape["region"], mesh.shape["member"]
    depth_y = 4 if members % 8 == 0 else 2
    depth_z = members // (2 * depth_y)
    flat = ("region", "member")
    return jax.shard_map(
        functools.partial(body, regions, depth_y, depth_z),
        mesh=mesh,
        in_specs=(
            P(None, flat),
            P(None, None, None, flat),
            P(None, flat),
            P(None, None, None, flat),
            P(None, flat),
        ),
        out_specs=(P(None, flat), P(None, flat)),
        check_vma=False,
    )
```

```python
import functools

import jax
import jax.numpy as jnp
from jax import lax
from jax.experimental import pallas as pl
from jax.experimental.pallas import tpu as pltpu
from jax.sharding import PartitionSpec as P

STEPS = 3
BASIS = 2 * STEPS + 1
RELAX = 0.6
SLOTS = 27
PAD = 32
UNROLL = 2
MESH = pl.DeviceIdType.MESH
OFFSETS = ((-1, -1), (-1, 1), (1, -1), (1, 1), (0, 2), (2, 0), (0, -1), (0, 1), (-1, 0), (1, 0))
F32 = jnp.float32


def lanes_of(shape):
    return lax.broadcasted_iota(jnp.int32, shape, len(shape) - 1)


def rows_of(shape):
    return lax.broadcasted_iota(jnp.int32, shape, len(shape) - 2)


def take(table, index):
    return jnp.take_along_axis(table, index, axis=1, mode="promise_in_bounds")


def spread(row):
    return jnp.broadcast_to(row, (8, 128))


def combine(accs):
    rows = rows_of((8, 128))
    sums = [jnp.sum(acc, axis=0, keepdims=True) for acc in accs]
    tile = jnp.where(rows & 3 == 2, sums[2], 0.0)
    tile = jnp.where(rows & 3 == 1, sums[1], tile)
    return jnp.where(rows & 3 == 0, sums[0], tile)


def combine_pair(accs):
    return jnp.where(rows_of((8, 128)) < 4, combine(accs[:3]), combine(accs[3:]))


def coefficients(gram, shifts):
    def image(x):
        y = [None] * (len(x) + 1)
        for i, value in enumerate(x):
            y[i] = value * shifts[i] if y[i] is None else y[i] + value * shifts[i]
            y[i + 1] = value
        return y

    def total(terms):
        while len(terms) > 1:
            terms = [terms[k] + terms[k + 1] if k + 1 < len(terms) else terms[k] for k in range(0, len(terms), 2)]
        return terms[0]

    def products(x, count):
        return [
            total([gram[min(i, j), max(i, j)] * value for j, value in enumerate(x)]) for i in range(count)
        ]

    def dot(x, y):
        return total([left * right for left, right in zip(x, y)])

    def axpy(x, a, y):
        out = []
        for i in range(max(len(x), len(y))):
            if i >= len(y):
                out.append(x[i])
            elif i >= len(x):
                out.append(a * y[i])
            else:
                out.append(x[i] + a * y[i])
        return out

    def shadow(x):
        return total([gram[0, j] * value for j, value in enumerate(x)])

    one = jnp.ones_like(shifts[0])
    resid, direction = [one], [one]
    error = []
    rho = gram[0, 0]
    for step in range(STEPS):
        move = image(direction)
        alpha = rho / shadow(move)
        middle = axpy(resid, -alpha, move)
        second = image(middle)
        against = products(second, len(second))
        omega = dot(middle, against) / dot(second, against)
        error = axpy(axpy(error, alpha, direction), omega, middle)
        if step + 1 < STEPS:
            resid = axpy(middle, -omega, second)
            rho_new = shadow(resid)
            beta = rho_new / rho * (alpha / omega)
            direction = axpy(resid, beta, axpy(direction, -omega, move))
            rho = rho_new
    return error


def kernel(
    regions, depth_y, depth_z, fine_dev, coarse_dev,
    rhs_hbm, fb_hbm, fl_hbm, cb_hbm, cl_hbm,
    both_out,
    rhs_raw, fb, fb_tail, fbh, fl, fl_tail, cb_raw, cb, cl, cidx, inv, rhs, fa, fc, fd, fa_image, steps, step_images, fl_halo, lift, pairs, images, tab, kv,
    hsend, hrecv, ksend, krecv, bsend, brecv, isend, irecv, fcb, e1, e2, g1, g2, row_send,
    load_sem, halo_send_sem, halo_recv_sem, k_send_sem, k_recv_sem, b_send_sem, b_recv_sem,
    red_send_sem, red_recv_sem,
):
    members = depth_y * depth_z * 2
    tiles = fine_dev // 128
    region = lax.axis_index("region")
    member = lax.axis_index("member")
    z, y, core = lax.div(member, 2 * depth_y), lax.rem(lax.div(member, 2), depth_y), lax.rem(member, 2)
    n1, n2 = regions * depth_y, depth_z * 2
    me1, me2 = region * depth_y + y, z * 2 + core
    region_at = [region] + [lax.rem(region + s, regions) for s in range(1, regions)]
    y_at = [member] + [member + 2 * (lax.rem(y + s, depth_y) - y) for s in range(1, depth_y)]
    z_at = [member] + [member + 2 * depth_y * (lax.rem(z + s, depth_z) - z) for s in range(1, depth_z)]
    def far_first(outer, inner, pair):
        around = lambda s, count: min(s, count - s)
        steps = [(s, t) for s in range(len(outer)) for t in range(len(inner))][1:]
        steps.sort(key=lambda st: -around(st[0], len(outer)) - around(st[1], len(inner)))
        return [pair(outer[s], inner[t]) for s, t in steps]

    peers1 = far_first(region_at, y_at, lambda r, m: (r, m))
    peers2 = far_first(z_at, [0, 1 - 2 * core], lambda m, flip: (region, m + flip))

    def at(dr, dm):
        r = region if dr == 0 else lax.rem(region + (regions + dr), regions)
        m = member if dm == 0 else lax.rem(member + (members + dm), members)
        return r, m

    after, before, above, below = at(0, 1), at(0, -1), at(1, 0), at(-1, 0)

    def block_tile(t, which):
        columns = pl.ds(128 * t, 128)
        return pltpu.make_async_copy(
            fb_hbm.at[:, :, :, columns], fb.at[:, :, :, columns], load_sem.at[which]
        )

    middle_tiles = fb.at[:, :, :, pl.ds(128, fine_dev - 256)]
    loads = [
        pltpu.make_async_copy(rhs_hbm, rhs_raw, load_sem.at[4]),
        pltpu.make_async_copy(middle_tiles, middle_tiles, load_sem.at[0]),
        pltpu.make_async_copy(cb_hbm, cb_raw, load_sem.at[1]),
        pltpu.make_async_copy(cl_hbm, cl, load_sem.at[2]),
        pltpu.make_async_copy(fl_hbm, fl, load_sem.at[3]),
    ]
    loads[0].start()
    face_loads = [block_tile(0, 5), block_tile(tiles - 1, 6)]
    for load in face_loads:
        load.start()
    for t in range(1, tiles - 1):
        block_tile(t, 0).start()
    for load in loads[2:]:
        load.start()

    barrier = pltpu.get_barrier_semaphore()
    for dr, dm in OFFSETS:
        device = at(-dr, -dm)
        pl.semaphore_signal(barrier, inc=1, device_id=device, device_id_type=MESH)

    for device in peers1 + peers2:
        pl.semaphore_signal(barrier, inc=1, device_id=device, device_id_type=MESH)

    lane = lanes_of((8, 128))
    rows = rows_of((8, 128))

    def halo_copies(ex, which):
        pairs = (
            (1, 0, after),
            (0, 1, before),
            (0, 2, above),
            (0, 3, below),
        )
        return [
            pltpu.make_async_remote_copy(
                src_ref=hsend.at[2 * ex + src],
                dst_ref=hrecv.at[4 * ex + dst],
                send_sem=halo_send_sem,
                recv_sem=halo_recv_sem.at[ex],
                device_id=device,
                device_id_type=MESH,
            )
            for src, dst, device in pairs
            if src in which
        ]

    def halo_send(ex, first, last):
        hsend[2 * ex] = first
        hsend[2 * ex + 1] = last
        for copy in halo_copies(ex, (0, 1)):
            copy.start()

    def halo_wait(ex):
        block = hrecv.at[pl.ds(4 * ex, 4)]
        pltpu.make_async_copy(block, block, halo_recv_sem.at[ex]).wait()
        return [hrecv[4 * ex + k] for k in range(4)]

    def reduce_start(which, buffer, peers, me, value):
        row_send[which] = value
        buffer[me] = value
        for device in peers:
            pltpu.make_async_remote_copy(
                src_ref=row_send.at[which],
                dst_ref=buffer.at[me],
                send_sem=red_send_sem,
                recv_sem=red_recv_sem.at[which],
                device_id=device,
                device_id_type=MESH,
            ).start()

    def reduce_wait(which, buffer, count, op):
        block = buffer.at[pl.ds(0, count - 1)]
        pltpu.make_async_copy(block, block, red_recv_sem.at[which]).wait()
        return functools.reduce(op, [buffer[k] for k in range(count)])

    def smooth(value, columns=slice(None)):
        total = inv[0, :, columns] * value[0:1, :]
        for j in range(1, 3):
            total = total + inv[j, :, columns] * value[j : j + 1, :]
        return total

    def links(g, columns):
        return fl[8 * g : 8 * g + 8, columns] if g < 3 else fl_tail[:, columns]

    def blocks_at(i, j, g, columns):
        return fb[i, j, 8 * g : 8 * g + 8, columns] if g < 3 else fb_tail[i, j, :, columns]

    def fine_local(source, target, count=1):
        for n in range(count):
            for j in range(3):
                for r in range(tiles):
                    row = 4 * n + j
                    tab[3 * n + j, r] = spread(source[row : row + 1, 128 * r : 128 * r + 128])

        def tile(t, carry):
            columns = pl.ds(pl.multiple_of(t * 128, 128), 128)
            accs = [None] * (3 * count)
            for g in range(4):
                index = links(g, columns)
                where = index & 127
                bits = [(index & (128 << k)) != 0 for k in range(3)]
                for j in range(3):
                    values = []
                    for n in range(count):
                        found = [take(tab[3 * n + j, r], where) for r in range(tiles)]
                        for bit in bits:
                            found = [
                                jnp.where(bit, found[2 * q + 1], found[2 * q])
                                for q in range(len(found) // 2)
                            ]
                        values.append(found[0])
                    for i in range(3):
                        block = blocks_at(i, j, g, columns)
                        for n in range(count):
                            term = block * values[n]
                            k = 3 * n + i
                            accs[k] = term if accs[k] is None else accs[k] + term
            for k in range(3 * count):
                pairs[k, t] = accs[k]
            return carry

        lax.fori_loop(0, tiles, tile, 0, unroll=UNROLL if count == 1 else 1)
        for t in range(tiles):
            sums = [pairs[k, t] for k in range(3 * count)]
            target[:, 128 * t : 128 * t + 128] = combine(sums) if count == 1 else combine_pair(sums)

    def fine_remote(halves, count=1):
        accs = [None] * (3 * count)
        for g in range(4):
            part = slice(8 * g, 8 * g + 8)
            index = links(g, slice(0, 128))
            where = index & 127
            bit = (index & 128) != 0
            for j in range(3):
                values = []
                for n in range(count):
                    row = 4 * n + j
                    low, high = (take(spread(half[row : row + 1, :]), where) for half in halves)
                    values.append(jnp.where(bit, high, low))
                for i in range(3):
                    block = fbh[i, j, part, :]
                    for n in range(count):
                        term = block * values[n]
                        k = 3 * n + i
                        accs[k] = term if accs[k] is None else accs[k] + term
        return combine(accs) if count == 1 else combine_pair(accs)

    def fine_send(ex, field):
        within = lane & 63
        halo_send(
            ex,
            take(field[:, 0:128], within),
            take(field[:, fine_dev - 128 : fine_dev], within + 64),
        )

    def fine_wait(ex):
        left, right, lower, upper = halo_wait(ex)
        return jnp.where(lane < 64, left, right), jnp.where(lane < 64, lower, upper)

    rhs[...] = jnp.zeros((8, fine_dev), F32)
    loads[0].wait()
    rhs[0:3, :] = rhs_raw[...]
    rhs[4:7, :] = rhs_raw[...]
    for load in face_loads:
        load.wait()

    def start_tile(t, carry):
        columns = pl.ds(pl.multiple_of(t * 128, 128), 128)
        (a, b, c), (d, e, f), (g_, h_, i_) = [
            [spread(fb[i, j, 26:27, columns]) for j in range(3)] for i in range(3)
        ]
        co_a = e * i_ - f * h_
        co_b = f * g_ - d * i_
        co_c = d * h_ - e * g_
        scale = RELAX / (a * co_a + b * co_b + c * co_c)
        adjugate = [
            [co_a, c * h_ - b * i_, b * f - c * e],
            [co_b, a * i_ - c * g_, c * d - a * f],
            [co_c, b * g_ - a * h_, a * e - b * d],
        ]
        total = None
        for j in range(3):
            column = jnp.where(rows & 3 == 2, adjugate[2][j], 0.0)
            column = jnp.where(rows & 3 == 1, adjugate[1][j], column)
            column = jnp.where(rows & 3 == 0, adjugate[0][j], column) * scale
            inv[j, :, columns] = column
            term = column * spread(rhs[j : j + 1, columns])
            total = term if total is None else total + term
        fa[:, columns] = total
        return carry

    start_tile(0, 0)
    start_tile(tiles - 1, 0)
    pl.semaphore_wait(barrier, len(OFFSETS) + (n1 - 1) + (n2 - 1))
    fine_send(0, fa)
    loads[1].wait()
    lax.fori_loop(1, tiles - 1, start_tile, 0, unroll=UNROLL)

    fl_tail[...] = jnp.where(rows_of((8, fine_dev)) == 2, lanes_of((8, fine_dev)), 0)
    fb_tail[...] = jnp.zeros((3, 3, 8, fine_dev), F32)
    fb_tail[:, :, 0:3, :] = fb[:, :, 24:27, :]
    loads[4].wait()
    fl_tail[0:2, :] = fl[24:26, :]
    for g in range(4):
        part = slice(8 * g, 8 * g + 8)
        outside = links(g, slice(0, 128)) >= fine_dev
        for i in range(3):
            for j in range(3):
                block = blocks_at(i, j, g, slice(0, 128))
                fbh[i, j, part, :] = jnp.where(outside, block, 0.0)
                inside = jnp.where(outside, 0.0, block)
                if g < 3:
                    fb[i, j, part, 0:128] = inside
                else:
                    fb_tail[i, j, :, 0:128] = inside

    kv[...] = jnp.zeros((3, 8, 128), F32)
    cidx[24:32, :] = jnp.where(rows == 2, lane, 0)
    cb[:, :, 24:32, :] = jnp.zeros((3, 3, 8, 128), F32)
    loads[2].wait()
    loads[3].wait()
    cb[:, :, 0:27, :] = cb_raw[...]
    cidx[0:26, :] = cl[...]
    diagonal = [cb[i, i, 26:27, :] for i in range(3)]
    largest = functools.reduce(jnp.maximum, diagonal)
    smallest = -functools.reduce(jnp.minimum, diagonal)
    largest, smallest = spread(largest), spread(smallest)
    swap = lane ^ 64
    largest = jnp.maximum(largest, take(largest, swap))
    smallest = jnp.maximum(smallest, take(smallest, swap))
    extremes = jnp.where(lane < 64, largest, smallest)[0:1]

    reduce_start(0, e1, peers1, me1, extremes)
    fine_local(fa, fc)

    head, rest = slice(0, 128), slice(128, fine_dev)
    fa[:, rest] += smooth(rhs[:, rest] - fc[:, rest], rest)
    halves = fine_wait(0)
    fa[:, head] += smooth(rhs[:, head] - fc[:, head] - fine_remote(halves), head)
    fine_send(1, fa)
    extremes = reduce_wait(0, e1, n1, jnp.maximum)
    reduce_start(1, e2, peers2, me2, extremes)
    fine_local(fa, fc)

    quarter = lane >> 5

    def packed(pieces, start):
        rolled = [pltpu.roll(piece, (128 + 32 * g - start) % 128, 1) for g, piece in enumerate(pieces)]
        low = jnp.where(quarter == 0, rolled[0], rolled[1])
        return jnp.where(quarter < 2, low, jnp.where(quarter == 2, rolled[2], rolled[3]))

    parts = [slice(8 * g, 8 * g + 8) for g in range(4)]
    codes = [cidx[part, :] for part in parts]
    for end, start in ((0, 0), (1, coarse_dev - 32)):
        isend[end] = packed(codes, start)
        for i in range(3):
            for j in range(3):
                bsend[end, 3 * i + j] = packed([cb[i, j, part, :] for part in parts], start)
    face_code = isend[0]
    for i in range(3):
        for j in range(3):
            fcb[i, j] = jnp.where(face_code >= coarse_dev, bsend[0, 3 * i + j], 0.0)
            for g in range(4):
                cb[i, j, parts[g], :] = jnp.where(codes[g] >= coarse_dev, 0.0, cb[i, j, parts[g], :])
    for g in range(4):
        cidx[parts[g], :] = codes[g] & 127
    side_copies = []
    for src, dst, device in ((1, 0, after), (0, 1, before), (0, 2, above), (0, 3, below)):
        for kind, (source, sink) in enumerate(((bsend, brecv), (isend, irecv))):
            side_copies.append(
                pltpu.make_async_remote_copy(
                    src_ref=source.at[src],
                    dst_ref=sink.at[dst],
                    send_sem=b_send_sem.at[kind],
                    recv_sem=b_recv_sem.at[kind],
                    device_id=device,
                    device_id_type=MESH,
                )
            )
    for copy in side_copies:
        copy.start()
    def eighths(part):
        for k in (1, 2, 4):
            part = part + pltpu.roll(part, 128 - k, 1)
        return take(part, (lane & 15) * 8)

    def restrict(ref):
        out = eighths(ref[:, 0:128])
        for t in range(1, tiles):
            picked = eighths(ref[:, 128 * t : 128 * t + 128])
            out = jnp.where(lane >> 4 == t, picked, out)
        return out

    fc[...] = rhs[...] - fc[...]
    coarse = restrict(fc)
    remote = fine_remote(fine_wait(1))
    fc[:, head] -= remote
    coarse = coarse - jnp.where(lane < 16, eighths(remote), 0.0)

    def coarse_send(ex, field):
        edge = take(field, jnp.where(lane < 32, lane + (coarse_dev - 32), lane & 31))
        tile = jnp.where(rows < 4, field, edge)
        ksend[ex] = tile
        for k, (dr, dm) in enumerate(OFFSETS):
            pltpu.make_async_remote_copy(
                src_ref=ksend.at[ex],
                dst_ref=krecv.at[ex, k],
                send_sem=k_send_sem,
                recv_sem=k_recv_sem.at[ex],
                device_id=at(-dr, -dm),
                device_id_type=MESH,
            ).start()
        return tile

    def coarse_wait(ex):
        block = krecv.at[ex]
        pltpu.make_async_copy(block, block, k_recv_sem.at[ex]).wait()
        return {offset: krecv[ex, k] for k, offset in enumerate(OFFSETS)}

    def beside(left, right, lower, upper):
        low = jnp.where(quarter == 0, left, right)
        return jnp.where(quarter < 2, low, jnp.where(quarter == 2, lower, upper))

    def folded(accs):
        tile = combine(accs)
        tile = tile + pltpu.roll(tile, 64, 1)
        return tile + pltpu.roll(tile, 32, 1)

    def coarse_local(field):
        accs = [None] * 3
        tables = [spread(field[j : j + 1, :]) for j in range(3)]
        for g in range(4):
            index = cidx[parts[g], :]
            for j in range(3):
                value = take(tables[j], index)
                for i in range(3):
                    term = cb[i, j, parts[g], :] * value
                    accs[i] = term if accs[i] is None else accs[i] + term
        return combine(accs)

    def coarse_remote(halo):
        accs = [None] * 3
        index = isend[0] & 127
        for j in range(3):
            value = take(spread(halo[4 + j : 5 + j, :]), index)
            for i in range(3):
                term = fcb[i, j] * value
                accs[i] = term if accs[i] is None else accs[i] + term
        return jnp.where(lane < 32, folded(accs), 0.0)

    def coarse_ghost(tiles_of, mine):
        around = (
            ((0, -1), None),
            ((0, 1), (mine, tiles_of[0, 2], tiles_of[-1, 1], tiles_of[1, 1])),
            ((-1, 0), (tiles_of[-1, -1], tiles_of[-1, 1], tiles_of[2, 0], mine)),
            ((1, 0), (tiles_of[1, -1], tiles_of[1, 1], mine, tiles_of[2, 0])),
        )
        out = None
        for q, (offset, edges) in enumerate(around):
            code = irecv[q]
            index = code & 127
            full = tiles_of[offset]
            outer = None if edges is None else beside(*edges)
            accs = [None] * 3
            for j in range(3):
                value = take(spread(full[j : j + 1, :]), index)
                if outer is not None:
                    far = take(spread(outer[4 + j : 5 + j, :]), index)
                    value = jnp.where(code >= coarse_dev, far, value)
                for i in range(3):
                    term = brecv[q, 3 * i + j] * value
                    accs[i] = term if accs[i] is None else accs[i] + term
            tile = folded(accs)
            out = tile if out is None else jnp.where(quarter == q, tile, out)
        return out

    def lift_pair(ex, fields, halos):
        for n in range(2):
            for j in range(3):
                lift[n, j] = spread(fields[n][j : j + 1, :])

        def tile(t, carry):
            columns = pl.ds(pl.multiple_of(t * 128, 128), 128)
            accs = [None] * 6
            for g in range(4):
                where = (links(g, columns) >> 3) & 127
                for j in range(3):
                    values = [take(lift[n, j], where) for n in range(2)]
                    for i in range(3):
                        block = blocks_at(i, j, g, columns)
                        for n in range(2):
                            term = block * values[n]
                            k = 3 * n + i
                            accs[k] = term if accs[k] is None else accs[k] + term
            for k in range(6):
                pairs[k, t] = accs[k]
            return carry

        lax.fori_loop(0, tiles, tile, 0, unroll=UNROLL)
        accs = [pairs[k, 0] for k in range(6)]
        for g in range(4):
            where = fl_halo[parts[g], :]
            for j in range(3):
                values = [take(spread(halos[n][4 + j : 5 + j, :]), where) for n in range(2)]
                for i in range(3):
                    block = fbh[i, j, parts[g], :]
                    for n in range(2):
                        accs[3 * n + i] = accs[3 * n + i] + block * values[n]
        images[ex, :, 0:128] = combine_pair(accs)
        for t in range(1, tiles):
            images[ex, :, 128 * t : 128 * t + 128] = combine_pair([pairs[k, t] for k in range(6)])

        def faces(columns):
            total = None
            for j in range(3):
                value = jnp.where(
                    rows < 4, spread(images[ex, j : j + 1, columns]), spread(images[ex, j + 4 : j + 5, columns])
                )
                term = inv[j, :, columns] * value
                total = term if total is None else total + term
            return total

        for t in range(tiles):
            columns = slice(128 * t, 128 * t + 128)
            steps[:, columns] = faces(columns)
        fine_send(3 + ex, steps)

    mine = coarse_send(0, coarse)
    for g in range(4):
        node = links(g, slice(0, 128)) & 255
        fl_halo[parts[g], :] = ((node >> 6) << 5) + ((node & 63) >> 3) + jnp.where(node < 64, 24, 0)
    update = smooth(fc[...])
    fd[...] = update
    fine_send(2, fd)
    fine_local(fd, fa_image)
    extremes = spread(reduce_wait(1, e2, n2, jnp.maximum))
    lowest = jnp.min(extremes)
    largest = jnp.max(jnp.where(lane < 64, extremes, lowest), axis=1, keepdims=True)
    smallest = -jnp.max(jnp.where(lane < 64, lowest, extremes), axis=1, keepdims=True)
    largest, smallest = jnp.broadcast_to(largest, (8, 128)), jnp.broadcast_to(smallest, (8, 128))
    middle = 0.5 * largest + 0.5 * smallest
    centres = [middle, 0.1 * smallest, 1.3 * largest, smallest, largest, middle]
    width = 0.5 * largest - 0.5 * smallest + 0.125 * largest
    shrink = 1.0 / width
    for kind, sink in enumerate((brecv, irecv)):
        pltpu.make_async_copy(sink, sink, b_recv_sem.at[kind]).wait()

    def keep(ref, k, field):
        for j in range(3):
            ref[j, k : k + 1, :] = field[j : j + 1, :]

    for ex in range(STEPS):
        local = coarse_local(coarse) - centres[2 * ex] * coarse
        keep(kv, 2 * ex, coarse)
        base = coarse
        tiles_of = coarse_wait(ex)
        halo = beside(tiles_of[0, -1], tiles_of[0, 1], tiles_of[-1, 0], tiles_of[1, 0])
        coarse = (local + coarse_remote(halo)) * shrink
        ghost = (coarse_ghost(tiles_of, mine) - centres[2 * ex] * halo) * shrink
        keep(kv, 2 * ex + 1, coarse)
        pair = (base, coarse), (halo, ghost)
        coarse = (coarse_local(coarse) - centres[2 * ex + 1] * coarse + coarse_remote(ghost)) * shrink
        if ex + 1 < STEPS:
            mine = coarse_send(ex + 1, coarse)
            lift_pair(ex, *pair)
            fine_local(steps, step_images.at[ex], 2)
            if ex == 1:
                fa_image[:, head] += fine_remote(fine_wait(2))
                step_images[0, :, head] += fine_remote(fine_wait(3), 2)
    for j in range(3):
        kv[j, BASIS - 1 : BASIS, :] = coarse[j : j + 1, :]

    gram = jnp.zeros((8, 128), F32)
    for k in range(BASIS):
        column = None
        for j in range(3):
            term = kv[j] * spread(kv[j, k : k + 1, :])
            column = term if column is None else column + term
        gram = jnp.where(lane & 7 == k, jnp.sum(column, axis=1, keepdims=True), gram)
    gram = jnp.where(rows == lane >> 3, gram, 0.0)
    gram = jnp.sum(gram, axis=0, keepdims=True)
    reduce_start(2, g1, peers1, me1, gram)
    lift_pair(STEPS - 1, *pair)
    gram = reduce_wait(2, g1, n1, jnp.add)
    reduce_start(3, g2, peers2, me2, gram)
    fine_local(steps, step_images.at[STEPS - 1], 2)
    for ex in range(1, STEPS):
        step_images[ex, :, head] += fine_remote(fine_wait(3 + ex), 2)
    gram = spread(reduce_wait(3, g2, n2, jnp.add))
    entries = {
        (i, j): take(gram, jnp.full((8, 128), 8 * i + j, jnp.int32))
        for i in range(BASIS)
        for j in range(i, BASIS)
    }
    weights = [weight * shrink for weight in coefficients(entries, [centre * shrink for centre in centres])]

    def mix(ref):
        out = []
        for j in range(3):
            total = None
            for k, weight in enumerate(weights):
                term = weight[0:1] * ref[j, k : k + 1, :]
                total = term if total is None else total + term
            out.append(total)
        tile = jnp.where(rows == 1, out[1], jnp.where(rows == 2, out[2], 0.0))
        return jnp.where(rows == 0, out[0], tile)

    doubled = [jnp.where(rows < 4, weights[2 * ex], weights[2 * ex + 1]) for ex in range(STEPS)]

    def mix_pairs(tiles_of):
        total = functools.reduce(jnp.add, [w * tile for w, tile in zip(doubled, tiles_of)])
        return total + pltpu.roll(total, 4, 0)

    for t in range(tiles):
        columns = slice(128 * t, 128 * t + 128)
        fc[:, columns] = fc[:, columns] - mix_pairs([images[ex, :, columns] for ex in range(STEPS)])
    error = mix(kv)
    update = smooth(fc[...])
    for t in range(tiles):
        columns = slice(128 * t, 128 * t + 128)
        both_out[0, :, columns] = (fa[:, columns] + update[:, columns] + take(error, 16 * t + (lane >> 3)))[0:3]
        final = fc[:, columns] - fa_image[:, columns]
        final = final + mix_pairs([step_images[ex, :, columns] for ex in range(STEPS)])
        both_out[1, :, columns] = final[0:3]

    pltpu.make_async_copy(hrecv, hrecv, halo_send_sem).wait()
    pltpu.make_async_copy(krecv, krecv, k_send_sem).wait()
    for kind, sink in enumerate((brecv, irecv)):
        pltpu.make_async_copy(sink, sink, b_send_sem.at[kind]).wait()
    for buffer, count in ((e1, n1), (e2, n2), (g1, n1), (g2, n2)):
        block = buffer.at[pl.ds(0, count - 1)]
        pltpu.make_async_copy(block, block, red_send_sem).wait()


def body(regions, depth_y, depth_z, right_side, fine_blocks, fine_links, coarse_blocks, coarse_links):
    fine_dev, coarse_dev = right_side.shape[1], coarse_blocks.shape[3]
    n1, n2 = regions * depth_y, depth_z * 2
    exchanges = 3 + STEPS
    reach = len(OFFSETS)
    vmem = pl.BlockSpec(memory_space=pltpu.VMEM)
    hbm = pl.BlockSpec(memory_space=pltpu.HBM)
    out = pltpu.VMEM((2, 3, fine_dev), F32)
    both = pl.pallas_call(
        functools.partial(kernel, regions, depth_y, depth_z, fine_dev, coarse_dev),
        out_shape=out,
        in_specs=[hbm] * 5,
        out_specs=vmem,
        scratch_shapes=[
            pltpu.VMEM((3, fine_dev), F32),
            pltpu.VMEM((3, 3, SLOTS, fine_dev), F32),
            pltpu.VMEM((3, 3, 8, fine_dev), F32),
            pltpu.VMEM((3, 3, PAD, 128), F32),
            pltpu.VMEM((SLOTS - 1, fine_dev), jnp.int32),
            pltpu.VMEM((8, fine_dev), jnp.int32),
            pltpu.VMEM((3, 3, SLOTS, 128), F32),
            pltpu.VMEM((3, 3, PAD, 128), F32),
            pltpu.VMEM((SLOTS - 1, 128), jnp.int32),
            pltpu.VMEM((PAD, 128), jnp.int32),
            pltpu.VMEM((3, 8, fine_dev), F32),
            pltpu.VMEM((8, fine_dev), F32),
            pltpu.VMEM((8, fine_dev), F32),
            pltpu.VMEM((8, fine_dev), F32),
            pltpu.VMEM((8, fine_dev), F32),
            pltpu.VMEM((8, fine_dev), F32),
            pltpu.VMEM((8, fine_dev), F32),
            pltpu.VMEM((STEPS, 8, fine_dev), F32),
            pltpu.VMEM((PAD, 128), jnp.int32),
            pltpu.VMEM((2, 3, 8, 128), F32),
            pltpu.VMEM((6, fine_dev // 128, 8, 128), F32),
            pltpu.VMEM((STEPS, 8, fine_dev), F32),
            pltpu.VMEM((6, fine_dev // 128, 8, 128), F32),
            pltpu.VMEM((3, 8, 128), F32),
            pltpu.VMEM((2 * exchanges, 8, 128), F32),
            pltpu.VMEM((4 * exchanges, 8, 128), F32),
            pltpu.VMEM((STEPS, 8, 128), F32),
            pltpu.VMEM((STEPS, reach, 8, 128), F32),
            pltpu.VMEM((2, 9, 8, 128), F32),
            pltpu.VMEM((4, 9, 8, 128), F32),
            pltpu.VMEM((2, 8, 128), jnp.int32),
            pltpu.VMEM((4, 8, 128), jnp.int32),
            pltpu.VMEM((3, 3, 8, 128), F32),
            pltpu.VMEM((n1, 1, 128), F32),
            pltpu.VMEM((n2, 1, 128), F32),
            pltpu.VMEM((n1, 1, 128), F32),
            pltpu.VMEM((n2, 1, 128), F32),
            pltpu.VMEM((4, 1, 128), F32),
            pltpu.SemaphoreType.DMA((7,)),
            pltpu.SemaphoreType.DMA,
            pltpu.SemaphoreType.DMA((exchanges,)),
            pltpu.SemaphoreType.DMA,
            pltpu.SemaphoreType.DMA((STEPS,)),
            pltpu.SemaphoreType.DMA((2,)),
            pltpu.SemaphoreType.DMA((2,)),
            pltpu.SemaphoreType.DMA,
            pltpu.SemaphoreType.DMA((4,)),
        ],
        compiler_params=pltpu.CompilerParams(
            collective_id=0, has_side_effects=True, vmem_limit_bytes=60 * 1024 * 1024
        ),
    )(
        right_side,
        jnp.transpose(fine_blocks, (1, 2, 0, 3)),
        fine_links,
        jnp.transpose(coarse_blocks, (1, 2, 0, 3)),
        coarse_links,
    )
    return both[0], both[1]


def solution(mesh):
    regions, members = mesh.shape["region"], mesh.shape["member"]
    depth_y = 4 if members % 8 == 0 else 2
    depth_z = members // (2 * depth_y)
    flat = ("region", "member")
    return jax.shard_map(
        functools.partial(body, regions, depth_y, depth_z),
        mesh=mesh,
        in_specs=(
            P(None, flat),
            P(None, None, None, flat),
            P(None, flat),
            P(None, None, None, flat),
            P(None, flat),
        ),
        out_specs=(P(None, flat), P(None, flat)),
        check_vma=False,
    )
```

```python
import functools

import jax
import jax.numpy as jnp
from jax import lax
from jax.experimental import pallas as pl
from jax.experimental.pallas import tpu as pltpu
from jax.sharding import PartitionSpec as P

STEPS = 3
BASIS = 2 * STEPS + 1
RELAX = 0.6
SLOTS = 27
PAD = 32
UNROLL = 1
MESH = pl.DeviceIdType.MESH
OFFSETS = ((-1, -1), (-1, 1), (1, -1), (1, 1), (0, 2), (2, 0), (0, -1), (0, 1), (-1, 0), (1, 0))
F32 = jnp.float32


def lanes_of(shape):
    return lax.broadcasted_iota(jnp.int32, shape, len(shape) - 1)


def rows_of(shape):
    return lax.broadcasted_iota(jnp.int32, shape, len(shape) - 2)


def take(table, index):
    return jnp.take_along_axis(table, index, axis=1, mode="promise_in_bounds")


def spread(row):
    return jnp.broadcast_to(row, (8, 128))


def combine(accs):
    rows = rows_of((8, 128))
    sums = [jnp.sum(acc, axis=0, keepdims=True) for acc in accs]
    tile = jnp.where(rows & 3 == 2, sums[2], 0.0)
    tile = jnp.where(rows & 3 == 1, sums[1], tile)
    return jnp.where(rows & 3 == 0, sums[0], tile)


def combine_pair(accs):
    return jnp.where(rows_of((8, 128)) < 4, combine(accs[:3]), combine(accs[3:]))


def coefficients(gram, shifts):
    def image(x):
        y = [None] * (len(x) + 1)
        for i, value in enumerate(x):
            y[i] = value * shifts[i] if y[i] is None else y[i] + value * shifts[i]
            y[i + 1] = value
        return y

    def total(terms):
        while len(terms) > 1:
            terms = [terms[k] + terms[k + 1] if k + 1 < len(terms) else terms[k] for k in range(0, len(terms), 2)]
        return terms[0]

    def products(x, count):
        return [
            total([gram[min(i, j), max(i, j)] * value for j, value in enumerate(x)]) for i in range(count)
        ]

    def dot(x, y):
        return total([left * right for left, right in zip(x, y)])

    def axpy(x, a, y):
        out = []
        for i in range(max(len(x), len(y))):
            if i >= len(y):
                out.append(x[i])
            elif i >= len(x):
                out.append(a * y[i])
            else:
                out.append(x[i] + a * y[i])
        return out

    def shadow(x):
        return total([gram[0, j] * value for j, value in enumerate(x)])

    one = jnp.ones_like(shifts[0])
    resid, direction = [one], [one]
    error = []
    rho = gram[0, 0]
    for step in range(STEPS):
        move = image(direction)
        alpha = rho / shadow(move)
        middle = axpy(resid, -alpha, move)
        second = image(middle)
        against = products(second, len(second))
        omega = dot(middle, against) / dot(second, against)
        error = axpy(axpy(error, alpha, direction), omega, middle)
        if step + 1 < STEPS:
            resid = axpy(middle, -omega, second)
            rho_new = shadow(resid)
            beta = rho_new / rho * (alpha / omega)
            direction = axpy(resid, beta, axpy(direction, -omega, move))
            rho = rho_new
    return error


def kernel(
    regions, depth_y, depth_z, fine_dev, coarse_dev,
    rhs_hbm, fb_hbm, fl_hbm, cb_hbm, cl_hbm,
    both_out,
    rhs_raw, fb, fb_tail, fbh, fl, fl_tail, cb_raw, cb, cl, cidx, inv, rhs, fa, fc, fd, fa_image, steps, step_images, fl_halo, lift, pairs, images, tab, kv,
    hsend, hrecv, ksend, krecv, bsend, brecv, isend, irecv, fcb, e1, e2, g1, g2, row_send,
    load_sem, halo_send_sem, halo_recv_sem, k_send_sem, k_recv_sem, b_send_sem, b_recv_sem,
    red_send_sem, red_recv_sem,
):
    members = depth_y * depth_z * 2
    tiles = fine_dev // 128
    region = lax.axis_index("region")
    member = lax.axis_index("member")
    z, y, core = lax.div(member, 2 * depth_y), lax.rem(lax.div(member, 2), depth_y), lax.rem(member, 2)
    n1, n2 = regions * depth_y, depth_z * 2
    me1, me2 = region * depth_y + y, z * 2 + core
    region_at = [region] + [lax.rem(region + s, regions) for s in range(1, regions)]
    y_at = [member] + [member + 2 * (lax.rem(y + s, depth_y) - y) for s in range(1, depth_y)]
    z_at = [member] + [member + 2 * depth_y * (lax.rem(z + s, depth_z) - z) for s in range(1, depth_z)]
    def far_first(outer, inner, pair):
        around = lambda s, count: min(s, count - s)
        steps = [(s, t) for s in range(len(outer)) for t in range(len(inner))][1:]
        steps.sort(key=lambda st: -around(st[0], len(outer)) - around(st[1], len(inner)))
        return [pair(outer[s], inner[t]) for s, t in steps]

    peers1 = far_first(region_at, y_at, lambda r, m: (r, m))
    peers2 = far_first(z_at, [0, 1 - 2 * core], lambda m, flip: (region, m + flip))

    def at(dr, dm):
        r = region if dr == 0 else lax.rem(region + (regions + dr), regions)
        m = member if dm == 0 else lax.rem(member + (members + dm), members)
        return r, m

    after, before, above, below = at(0, 1), at(0, -1), at(1, 0), at(-1, 0)

    def block_tile(t, which):
        columns = pl.ds(128 * t, 128)
        return pltpu.make_async_copy(
            fb_hbm.at[:, :, :, columns], fb.at[:, :, :, columns], load_sem.at[which]
        )

    middle_tiles = fb.at[:, :, :, pl.ds(128, fine_dev - 256)]
    loads = [
        pltpu.make_async_copy(rhs_hbm, rhs_raw, load_sem.at[4]),
        pltpu.make_async_copy(middle_tiles, middle_tiles, load_sem.at[0]),
        pltpu.make_async_copy(cb_hbm, cb_raw, load_sem.at[1]),
        pltpu.make_async_copy(cl_hbm, cl, load_sem.at[2]),
        pltpu.make_async_copy(fl_hbm, fl, load_sem.at[3]),
    ]
    loads[0].start()
    face_loads = [block_tile(0, 5), block_tile(tiles - 1, 6)]
    for load in face_loads:
        load.start()
    for t in range(1, tiles - 1):
        block_tile(t, 0).start()
    for load in loads[2:]:
        load.start()

    barrier = pltpu.get_barrier_semaphore()
    for dr, dm in OFFSETS:
        device = at(-dr, -dm)
        pl.semaphore_signal(barrier, inc=1, device_id=device, device_id_type=MESH)

    for device in peers1 + peers2:
        pl.semaphore_signal(barrier, inc=1, device_id=device, device_id_type=MESH)

    lane = lanes_of((8, 128))
    rows = rows_of((8, 128))

    def halo_copies(ex, which):
        pairs = (
            (1, 0, after),
            (0, 1, before),
            (0, 2, above),
            (0, 3, below),
        )
        return [
            pltpu.make_async_remote_copy(
                src_ref=hsend.at[2 * ex + src],
                dst_ref=hrecv.at[4 * ex + dst],
                send_sem=halo_send_sem,
                recv_sem=halo_recv_sem.at[ex],
                device_id=device,
                device_id_type=MESH,
            )
            for src, dst, device in pairs
            if src in which
        ]

    def halo_send(ex, first, last):
        hsend[2 * ex] = first
        hsend[2 * ex + 1] = last
        for copy in halo_copies(ex, (0, 1)):
            copy.start()

    def halo_wait(ex):
        block = hrecv.at[pl.ds(4 * ex, 4)]
        pltpu.make_async_copy(block, block, halo_recv_sem.at[ex]).wait()
        return [hrecv[4 * ex + k] for k in range(4)]

    def reduce_start(which, buffer, peers, me, value):
        row_send[which] = value
        buffer[me] = value
        for device in peers:
            pltpu.make_async_remote_copy(
                src_ref=row_send.at[which],
                dst_ref=buffer.at[me],
                send_sem=red_send_sem,
                recv_sem=red_recv_sem.at[which],
                device_id=device,
                device_id_type=MESH,
            ).start()

    def reduce_wait(which, buffer, count, op):
        block = buffer.at[pl.ds(0, count - 1)]
        pltpu.make_async_copy(block, block, red_recv_sem.at[which]).wait()
        return functools.reduce(op, [buffer[k] for k in range(count)])

    def smooth(value, columns=slice(None)):
        total = inv[0, :, columns] * value[0:1, :]
        for j in range(1, 3):
            total = total + inv[j, :, columns] * value[j : j + 1, :]
        return total

    def links(g, columns):
        return fl[8 * g : 8 * g + 8, columns] if g < 3 else fl_tail[:, columns]

    def blocks_at(i, j, g, columns):
        return fb[i, j, 8 * g : 8 * g + 8, columns] if g < 3 else fb_tail[i, j, :, columns]

    def fine_local(source, target, count=1):
        for n in range(count):
            for j in range(3):
                for r in range(tiles):
                    row = 4 * n + j
                    tab[3 * n + j, r] = spread(source[row : row + 1, 128 * r : 128 * r + 128])

        def tile(t, carry):
            columns = pl.ds(pl.multiple_of(t * 128, 128), 128)
            accs = [None] * (3 * count)
            for g in range(4):
                index = links(g, columns)
                where = index & 127
                bits = [(index & (128 << k)) != 0 for k in range(3)]
                for j in range(3):
                    values = []
                    for n in range(count):
                        found = [take(tab[3 * n + j, r], where) for r in range(tiles)]
                        for bit in bits:
                            found = [
                                jnp.where(bit, found[2 * q + 1], found[2 * q])
                                for q in range(len(found) // 2)
                            ]
                        values.append(found[0])
                    for i in range(3):
                        block = blocks_at(i, j, g, columns)
                        for n in range(count):
                            term = block * values[n]
                            k = 3 * n + i
                            accs[k] = term if accs[k] is None else accs[k] + term
            for k in range(3 * count):
                pairs[k, t] = accs[k]
            return carry

        lax.fori_loop(0, tiles, tile, 0, unroll=UNROLL if count == 1 else 1)
        for t in range(tiles):
            sums = [pairs[k, t] for k in range(3 * count)]
            target[:, 128 * t : 128 * t + 128] = combine(sums) if count == 1 else combine_pair(sums)

    def fine_remote(halves, count=1):
        accs = [None] * (3 * count)
        for g in range(4):
            part = slice(8 * g, 8 * g + 8)
            index = links(g, slice(0, 128))
            where = index & 127
            bit = (index & 128) != 0
            for j in range(3):
                values = []
                for n in range(count):
                    row = 4 * n + j
                    low, high = (take(spread(half[row : row + 1, :]), where) for half in halves)
                    values.append(jnp.where(bit, high, low))
                for i in range(3):
                    block = fbh[i, j, part, :]
                    for n in range(count):
                        term = block * values[n]
                        k = 3 * n + i
                        accs[k] = term if accs[k] is None else accs[k] + term
        return combine(accs) if count == 1 else combine_pair(accs)

    def fine_send(ex, field):
        within = lane & 63
        halo_send(
            ex,
            take(field[:, 0:128], within),
            take(field[:, fine_dev - 128 : fine_dev], within + 64),
        )

    def fine_wait(ex):
        left, right, lower, upper = halo_wait(ex)
        return jnp.where(lane < 64, left, right), jnp.where(lane < 64, lower, upper)

    rhs[...] = jnp.zeros((8, fine_dev), F32)
    loads[0].wait()
    rhs[0:3, :] = rhs_raw[...]
    rhs[4:7, :] = rhs_raw[...]
    for load in face_loads:
        load.wait()

    def start_tile(t, carry):
        columns = pl.ds(pl.multiple_of(t * 128, 128), 128)
        (a, b, c), (d, e, f), (g_, h_, i_) = [
            [spread(fb[i, j, 26:27, columns]) for j in range(3)] for i in range(3)
        ]
        co_a = e * i_ - f * h_
        co_b = f * g_ - d * i_
        co_c = d * h_ - e * g_
        scale = RELAX / (a * co_a + b * co_b + c * co_c)
        adjugate = [
            [co_a, c * h_ - b * i_, b * f - c * e],
            [co_b, a * i_ - c * g_, c * d - a * f],
            [co_c, b * g_ - a * h_, a * e - b * d],
        ]
        total = None
        for j in range(3):
            column = jnp.where(rows & 3 == 2, adjugate[2][j], 0.0)
            column = jnp.where(rows & 3 == 1, adjugate[1][j], column)
            column = jnp.where(rows & 3 == 0, adjugate[0][j], column) * scale
            inv[j, :, columns] = column
            term = column * spread(rhs[j : j + 1, columns])
            total = term if total is None else total + term
        fa[:, columns] = total
        return carry

    start_tile(0, 0)
    start_tile(tiles - 1, 0)
    pl.semaphore_wait(barrier, len(OFFSETS) + (n1 - 1) + (n2 - 1))
    fine_send(0, fa)
    loads[1].wait()
    lax.fori_loop(1, tiles - 1, start_tile, 0, unroll=UNROLL)

    fl_tail[...] = jnp.where(rows_of((8, fine_dev)) == 2, lanes_of((8, fine_dev)), 0)
    fb_tail[...] = jnp.zeros((3, 3, 8, fine_dev), F32)
    fb_tail[:, :, 0:3, :] = fb[:, :, 24:27, :]
    loads[4].wait()
    fl_tail[0:2, :] = fl[24:26, :]
    for g in range(4):
        part = slice(8 * g, 8 * g + 8)
        outside = links(g, slice(0, 128)) >= fine_dev
        for i in range(3):
            for j in range(3):
                block = blocks_at(i, j, g, slice(0, 128))
                fbh[i, j, part, :] = jnp.where(outside, block, 0.0)
                inside = jnp.where(outside, 0.0, block)
                if g < 3:
                    fb[i, j, part, 0:128] = inside
                else:
                    fb_tail[i, j, :, 0:128] = inside

    kv[...] = jnp.zeros((3, 8, 128), F32)
    cidx[24:32, :] = jnp.where(rows == 2, lane, 0)
    cb[:, :, 24:32, :] = jnp.zeros((3, 3, 8, 128), F32)
    loads[2].wait()
    loads[3].wait()
    cb[:, :, 0:27, :] = cb_raw[...]
    cidx[0:26, :] = cl[...]
    diagonal = [cb[i, i, 26:27, :] for i in range(3)]
    largest = functools.reduce(jnp.maximum, diagonal)
    smallest = -functools.reduce(jnp.minimum, diagonal)
    largest, smallest = spread(largest), spread(smallest)
    swap = lane ^ 64
    largest = jnp.maximum(largest, take(largest, swap))
    smallest = jnp.maximum(smallest, take(smallest, swap))
    extremes = jnp.where(lane < 64, largest, smallest)[0:1]

    reduce_start(0, e1, peers1, me1, extremes)
    fine_local(fa, fc)

    head, rest = slice(0, 128), slice(128, fine_dev)
    fa[:, rest] += smooth(rhs[:, rest] - fc[:, rest], rest)
    halves = fine_wait(0)
    fa[:, head] += smooth(rhs[:, head] - fc[:, head] - fine_remote(halves), head)
    fine_send(1, fa)
    extremes = reduce_wait(0, e1, n1, jnp.maximum)
    reduce_start(1, e2, peers2, me2, extremes)
    fine_local(fa, fc)

    quarter = lane >> 5

    def packed(pieces, start):
        rolled = [pltpu.roll(piece, (128 + 32 * g - start) % 128, 1) for g, piece in enumerate(pieces)]
        low = jnp.where(quarter == 0, rolled[0], rolled[1])
        return jnp.where(quarter < 2, low, jnp.where(quarter == 2, rolled[2], rolled[3]))

    parts = [slice(8 * g, 8 * g + 8) for g in range(4)]
    codes = [cidx[part, :] for part in parts]
    for end, start in ((0, 0), (1, coarse_dev - 32)):
        isend[end] = packed(codes, start)
        for i in range(3):
            for j in range(3):
                bsend[end, 3 * i + j] = packed([cb[i, j, part, :] for part in parts], start)
    face_code = isend[0]
    for i in range(3):
        for j in range(3):
            fcb[i, j] = jnp.where(face_code >= coarse_dev, bsend[0, 3 * i + j], 0.0)
            for g in range(4):
                cb[i, j, parts[g], :] = jnp.where(codes[g] >= coarse_dev, 0.0, cb[i, j, parts[g], :])
    for g in range(4):
        cidx[parts[g], :] = codes[g] & 127
    side_copies = []
    for src, dst, device in ((1, 0, after), (0, 1, before), (0, 2, above), (0, 3, below)):
        for kind, (source, sink) in enumerate(((bsend, brecv), (isend, irecv))):
            side_copies.append(
                pltpu.make_async_remote_copy(
                    src_ref=source.at[src],
                    dst_ref=sink.at[dst],
                    send_sem=b_send_sem.at[kind],
                    recv_sem=b_recv_sem.at[kind],
                    device_id=device,
                    device_id_type=MESH,
                )
            )
    for copy in side_copies:
        copy.start()
    def eighths(part):
        for k in (1, 2, 4):
            part = part + pltpu.roll(part, 128 - k, 1)
        return take(part, (lane & 15) * 8)

    def restrict(ref):
        out = eighths(ref[:, 0:128])
        for t in range(1, tiles):
            picked = eighths(ref[:, 128 * t : 128 * t + 128])
            out = jnp.where(lane >> 4 == t, picked, out)
        return out

    fc[...] = rhs[...] - fc[...]
    coarse = restrict(fc)
    remote = fine_remote(fine_wait(1))
    fc[:, head] -= remote
    coarse = coarse - jnp.where(lane < 16, eighths(remote), 0.0)

    def coarse_send(ex, field):
        edge = take(field, jnp.where(lane < 32, lane + (coarse_dev - 32), lane & 31))
        tile = jnp.where(rows < 4, field, edge)
        ksend[ex] = tile
        for k, (dr, dm) in enumerate(OFFSETS):
            pltpu.make_async_remote_copy(
                src_ref=ksend.at[ex],
                dst_ref=krecv.at[ex, k],
                send_sem=k_send_sem,
                recv_sem=k_recv_sem.at[ex],
                device_id=at(-dr, -dm),
                device_id_type=MESH,
            ).start()
        return tile

    def coarse_wait(ex):
        block = krecv.at[ex]
        pltpu.make_async_copy(block, block, k_recv_sem.at[ex]).wait()
        return {offset: krecv[ex, k] for k, offset in enumerate(OFFSETS)}

    def beside(left, right, lower, upper):
        low = jnp.where(quarter == 0, left, right)
        return jnp.where(quarter < 2, low, jnp.where(quarter == 2, lower, upper))

    def folded(accs):
        tile = combine(accs)
        tile = tile + pltpu.roll(tile, 64, 1)
        return tile + pltpu.roll(tile, 32, 1)

    def coarse_local(field):
        accs = [None] * 3
        tables = [spread(field[j : j + 1, :]) for j in range(3)]
        for g in range(4):
            index = cidx[parts[g], :]
            for j in range(3):
                value = take(tables[j], index)
                for i in range(3):
                    term = cb[i, j, parts[g], :] * value
                    accs[i] = term if accs[i] is None else accs[i] + term
        return combine(accs)

    def coarse_remote(halo):
        accs = [None] * 3
        index = isend[0] & 127
        for j in range(3):
            value = take(spread(halo[4 + j : 5 + j, :]), index)
            for i in range(3):
                term = fcb[i, j] * value
                accs[i] = term if accs[i] is None else accs[i] + term
        return jnp.where(lane < 32, folded(accs), 0.0)

    def coarse_ghost(tiles_of, mine):
        around = (
            ((0, -1), None),
            ((0, 1), (mine, tiles_of[0, 2], tiles_of[-1, 1], tiles_of[1, 1])),
            ((-1, 0), (tiles_of[-1, -1], tiles_of[-1, 1], tiles_of[2, 0], mine)),
            ((1, 0), (tiles_of[1, -1], tiles_of[1, 1], mine, tiles_of[2, 0])),
        )
        out = None
        for q, (offset, edges) in enumerate(around):
            code = irecv[q]
            index = code & 127
            full = tiles_of[offset]
            outer = None if edges is None else beside(*edges)
            accs = [None] * 3
            for j in range(3):
                value = take(spread(full[j : j + 1, :]), index)
                if outer is not None:
                    far = take(spread(outer[4 + j : 5 + j, :]), index)
                    value = jnp.where(code >= coarse_dev, far, value)
                for i in range(3):
                    term = brecv[q, 3 * i + j] * value
                    accs[i] = term if accs[i] is None else accs[i] + term
            tile = folded(accs)
            out = tile if out is None else jnp.where(quarter == q, tile, out)
        return out

    def lift_pair(ex, fields, halos):
        for n in range(2):
            for j in range(3):
                lift[n, j] = spread(fields[n][j : j + 1, :])

        def tile(t, carry):
            columns = pl.ds(pl.multiple_of(t * 128, 128), 128)
            accs = [None] * 6
            for g in range(4):
                where = (links(g, columns) >> 3) & 127
                for j in range(3):
                    values = [take(lift[n, j], where) for n in range(2)]
                    for i in range(3):
                        block = blocks_at(i, j, g, columns)
                        for n in range(2):
                            term = block * values[n]
                            k = 3 * n + i
                            accs[k] = term if accs[k] is None else accs[k] + term
            for k in range(6):
                pairs[k, t] = accs[k]
            return carry

        lax.fori_loop(0, tiles, tile, 0, unroll=UNROLL)
        accs = [pairs[k, 0] for k in range(6)]
        for g in range(4):
            where = fl_halo[parts[g], :]
            for j in range(3):
                values = [take(spread(halos[n][4 + j : 5 + j, :]), where) for n in range(2)]
                for i in range(3):
                    block = fbh[i, j, parts[g], :]
                    for n in range(2):
                        accs[3 * n + i] = accs[3 * n + i] + block * values[n]
        images[ex, :, 0:128] = combine_pair(accs)
        for t in range(1, tiles):
            images[ex, :, 128 * t : 128 * t + 128] = combine_pair([pairs[k, t] for k in range(6)])

        def faces(columns):
            total = None
            for j in range(3):
                value = jnp.where(
                    rows < 4, spread(images[ex, j : j + 1, columns]), spread(images[ex, j + 4 : j + 5, columns])
                )
                term = inv[j, :, columns] * value
                total = term if total is None else total + term
            return total

        for t in range(tiles):
            columns = slice(128 * t, 128 * t + 128)
            steps[:, columns] = faces(columns)
        fine_send(3 + ex, steps)

    mine = coarse_send(0, coarse)
    for g in range(4):
        node = links(g, slice(0, 128)) & 255
        fl_halo[parts[g], :] = ((node >> 6) << 5) + ((node & 63) >> 3) + jnp.where(node < 64, 24, 0)
    update = smooth(fc[...])
    fd[...] = update
    fine_send(2, fd)
    fine_local(fd, fa_image)
    extremes = spread(reduce_wait(1, e2, n2, jnp.maximum))
    lowest = jnp.min(extremes)
    largest = jnp.max(jnp.where(lane < 64, extremes, lowest), axis=1, keepdims=True)
    smallest = -jnp.max(jnp.where(lane < 64, lowest, extremes), axis=1, keepdims=True)
    largest, smallest = jnp.broadcast_to(largest, (8, 128)), jnp.broadcast_to(smallest, (8, 128))
    middle = 0.5 * largest + 0.5 * smallest
    centres = [middle, 0.1 * smallest, 1.3 * largest, smallest, largest, middle]
    width = 0.5 * largest - 0.5 * smallest + 0.125 * largest
    shrink = 1.0 / width
    for kind, sink in enumerate((brecv, irecv)):
        pltpu.make_async_copy(sink, sink, b_recv_sem.at[kind]).wait()

    def keep(ref, k, field):
        for j in range(3):
            ref[j, k : k + 1, :] = field[j : j + 1, :]

    for ex in range(STEPS):
        local = coarse_local(coarse) - centres[2 * ex] * coarse
        keep(kv, 2 * ex, coarse)
        base = coarse
        tiles_of = coarse_wait(ex)
        halo = beside(tiles_of[0, -1], tiles_of[0, 1], tiles_of[-1, 0], tiles_of[1, 0])
        coarse = (local + coarse_remote(halo)) * shrink
        ghost = (coarse_ghost(tiles_of, mine) - centres[2 * ex] * halo) * shrink
        keep(kv, 2 * ex + 1, coarse)
        pair = (base, coarse), (halo, ghost)
        coarse = (coarse_local(coarse) - centres[2 * ex + 1] * coarse + coarse_remote(ghost)) * shrink
        if ex + 1 < STEPS:
            mine = coarse_send(ex + 1, coarse)
            lift_pair(ex, *pair)
            fine_local(steps, step_images.at[ex], 2)
            if ex == 1:
                fa_image[:, head] += fine_remote(fine_wait(2))
                step_images[0, :, head] += fine_remote(fine_wait(3), 2)
    for j in range(3):
        kv[j, BASIS - 1 : BASIS, :] = coarse[j : j + 1, :]

    gram = jnp.zeros((8, 128), F32)
    for k in range(BASIS):
        column = None
        for j in range(3):
            term = kv[j] * spread(kv[j, k : k + 1, :])
            column = term if column is None else column + term
        gram = jnp.where(lane & 7 == k, jnp.sum(column, axis=1, keepdims=True), gram)
    gram = jnp.where(rows == lane >> 3, gram, 0.0)
    gram = jnp.sum(gram, axis=0, keepdims=True)
    reduce_start(2, g1, peers1, me1, gram)
    lift_pair(STEPS - 1, *pair)
    gram = reduce_wait(2, g1, n1, jnp.add)
    reduce_start(3, g2, peers2, me2, gram)
    fine_local(steps, step_images.at[STEPS - 1], 2)
    for ex in range(1, STEPS):
        step_images[ex, :, head] += fine_remote(fine_wait(3 + ex), 2)
    gram = spread(reduce_wait(3, g2, n2, jnp.add))
    entries = {
        (i, j): take(gram, jnp.full((8, 128), 8 * i + j, jnp.int32))
        for i in range(BASIS)
        for j in range(i, BASIS)
    }
    weights = [weight * shrink for weight in coefficients(entries, [centre * shrink for centre in centres])]

    def mix(ref):
        out = []
        for j in range(3):
            total = None
            for k, weight in enumerate(weights):
                term = weight[0:1] * ref[j, k : k + 1, :]
                total = term if total is None else total + term
            out.append(total)
        tile = jnp.where(rows == 1, out[1], jnp.where(rows == 2, out[2], 0.0))
        return jnp.where(rows == 0, out[0], tile)

    doubled = [jnp.where(rows < 4, weights[2 * ex], weights[2 * ex + 1]) for ex in range(STEPS)]

    def mix_pairs(tiles_of):
        total = functools.reduce(jnp.add, [w * tile for w, tile in zip(doubled, tiles_of)])
        return total + pltpu.roll(total, 4, 0)

    for t in range(tiles):
        columns = slice(128 * t, 128 * t + 128)
        fc[:, columns] = fc[:, columns] - mix_pairs([images[ex, :, columns] for ex in range(STEPS)])
    error = mix(kv)
    update = smooth(fc[...])
    for t in range(tiles):
        columns = slice(128 * t, 128 * t + 128)
        both_out[0, :, columns] = (fa[:, columns] + update[:, columns] + take(error, 16 * t + (lane >> 3)))[0:3]
        final = fc[:, columns] - fa_image[:, columns]
        final = final + mix_pairs([step_images[ex, :, columns] for ex in range(STEPS)])
        both_out[1, :, columns] = final[0:3]

    pltpu.make_async_copy(hrecv, hrecv, halo_send_sem).wait()
    pltpu.make_async_copy(krecv, krecv, k_send_sem).wait()
    for kind, sink in enumerate((brecv, irecv)):
        pltpu.make_async_copy(sink, sink, b_send_sem.at[kind]).wait()
    for buffer, count in ((e1, n1), (e2, n2), (g1, n1), (g2, n2)):
        block = buffer.at[pl.ds(0, count - 1)]
        pltpu.make_async_copy(block, block, red_send_sem).wait()


def body(regions, depth_y, depth_z, right_side, fine_blocks, fine_links, coarse_blocks, coarse_links):
    fine_dev, coarse_dev = right_side.shape[1], coarse_blocks.shape[3]
    n1, n2 = regions * depth_y, depth_z * 2
    exchanges = 3 + STEPS
    reach = len(OFFSETS)
    vmem = pl.BlockSpec(memory_space=pltpu.VMEM)
    hbm = pl.BlockSpec(memory_space=pltpu.HBM)
    out = pltpu.VMEM((2, 3, fine_dev), F32)
    both = pl.pallas_call(
        functools.partial(kernel, regions, depth_y, depth_z, fine_dev, coarse_dev),
        out_shape=out,
        in_specs=[hbm] * 5,
        out_specs=vmem,
        scratch_shapes=[
            pltpu.VMEM((3, fine_dev), F32),
            pltpu.VMEM((3, 3, SLOTS, fine_dev), F32),
            pltpu.VMEM((3, 3, 8, fine_dev), F32),
            pltpu.VMEM((3, 3, PAD, 128), F32),
            pltpu.VMEM((SLOTS - 1, fine_dev), jnp.int32),
            pltpu.VMEM((8, fine_dev), jnp.int32),
            pltpu.VMEM((3, 3, SLOTS, 128), F32),
            pltpu.VMEM((3, 3, PAD, 128), F32),
            pltpu.VMEM((SLOTS - 1, 128), jnp.int32),
            pltpu.VMEM((PAD, 128), jnp.int32),
            pltpu.VMEM((3, 8, fine_dev), F32),
            pltpu.VMEM((8, fine_dev), F32),
            pltpu.VMEM((8, fine_dev), F32),
            pltpu.VMEM((8, fine_dev), F32),
            pltpu.VMEM((8, fine_dev), F32),
            pltpu.VMEM((8, fine_dev), F32),
            pltpu.VMEM((8, fine_dev), F32),
            pltpu.VMEM((STEPS, 8, fine_dev), F32),
            pltpu.VMEM((PAD, 128), jnp.int32),
            pltpu.VMEM((2, 3, 8, 128), F32),
            pltpu.VMEM((6, fine_dev // 128, 8, 128), F32),
            pltpu.VMEM((STEPS, 8, fine_dev), F32),
            pltpu.VMEM((6, fine_dev // 128, 8, 128), F32),
            pltpu.VMEM((3, 8, 128), F32),
            pltpu.VMEM((2 * exchanges, 8, 128), F32),
            pltpu.VMEM((4 * exchanges, 8, 128), F32),
            pltpu.VMEM((STEPS, 8, 128), F32),
            pltpu.VMEM((STEPS, reach, 8, 128), F32),
            pltpu.VMEM((2, 9, 8, 128), F32),
            pltpu.VMEM((4, 9, 8, 128), F32),
            pltpu.VMEM((2, 8, 128), jnp.int32),
            pltpu.VMEM((4, 8, 128), jnp.int32),
            pltpu.VMEM((3, 3, 8, 128), F32),
            pltpu.VMEM((n1, 1, 128), F32),
            pltpu.VMEM((n2, 1, 128), F32),
            pltpu.VMEM((n1, 1, 128), F32),
            pltpu.VMEM((n2, 1, 128), F32),
            pltpu.VMEM((4, 1, 128), F32),
            pltpu.SemaphoreType.DMA((7,)),
            pltpu.SemaphoreType.DMA,
            pltpu.SemaphoreType.DMA((exchanges,)),
            pltpu.SemaphoreType.DMA,
            pltpu.SemaphoreType.DMA((STEPS,)),
            pltpu.SemaphoreType.DMA((2,)),
            pltpu.SemaphoreType.DMA((2,)),
            pltpu.SemaphoreType.DMA,
            pltpu.SemaphoreType.DMA((4,)),
        ],
        compiler_params=pltpu.CompilerParams(
            collective_id=0, has_side_effects=True, vmem_limit_bytes=60 * 1024 * 1024
        ),
    )(
        right_side,
        jnp.transpose(fine_blocks, (1, 2, 0, 3)),
        fine_links,
        jnp.transpose(coarse_blocks, (1, 2, 0, 3)),
        coarse_links,
    )
    return both[0], both[1]


def solution(mesh):
    regions, members = mesh.shape["region"], mesh.shape["member"]
    depth_y = 4 if members % 8 == 0 else 2
    depth_z = members // (2 * depth_y)
    flat = ("region", "member")
    return jax.shard_map(
        functools.partial(body, regions, depth_y, depth_z),
        mesh=mesh,
        in_specs=(
            P(None, flat),
            P(None, None, None, flat),
            P(None, flat),
            P(None, None, None, flat),
            P(None, flat),
        ),
        out_specs=(P(None, flat), P(None, flat)),
        check_vma=False,
    )
```

```python
import functools

import jax
import jax.numpy as jnp
from jax import lax
from jax.experimental import pallas as pl
from jax.experimental.pallas import tpu as pltpu
from jax.sharding import PartitionSpec as P

STEPS = 3
BASIS = 2 * STEPS + 1
RELAX = 0.6
SLOTS = 27
PAD = 32
UNROLL = 2
MESH = pl.DeviceIdType.MESH
OFFSETS = ((-1, -1), (-1, 1), (1, -1), (1, 1), (0, 2), (2, 0), (0, -1), (0, 1), (-1, 0), (1, 0))
F32 = jnp.float32


def lanes_of(shape):
    return lax.broadcasted_iota(jnp.int32, shape, len(shape) - 1)


def rows_of(shape):
    return lax.broadcasted_iota(jnp.int32, shape, len(shape) - 2)


def take(table, index):
    return jnp.take_along_axis(table, index, axis=1, mode="promise_in_bounds")


def spread(row):
    return jnp.broadcast_to(row, (8, 128))


def combine(accs):
    rows = rows_of((8, 128))
    sums = [jnp.sum(acc, axis=0, keepdims=True) for acc in accs]
    tile = jnp.where(rows & 3 == 2, sums[2], 0.0)
    tile = jnp.where(rows & 3 == 1, sums[1], tile)
    return jnp.where(rows & 3 == 0, sums[0], tile)


def combine_pair(accs):
    return jnp.where(rows_of((8, 128)) < 4, combine(accs[:3]), combine(accs[3:]))


def coefficients(gram, shifts):
    def image(x):
        y = [None] * (len(x) + 1)
        for i, value in enumerate(x):
            y[i] = value * shifts[i] if y[i] is None else y[i] + value * shifts[i]
            y[i + 1] = value
        return y

    def total(terms):
        while len(terms) > 1:
            terms = [terms[k] + terms[k + 1] if k + 1 < len(terms) else terms[k] for k in range(0, len(terms), 2)]
        return terms[0]

    def products(x, count):
        return [
            total([gram[min(i, j), max(i, j)] * value for j, value in enumerate(x)]) for i in range(count)
        ]

    def dot(x, y):
        return total([left * right for left, right in zip(x, y)])

    def axpy(x, a, y):
        out = []
        for i in range(max(len(x), len(y))):
            if i >= len(y):
                out.append(x[i])
            elif i >= len(x):
                out.append(a * y[i])
            else:
                out.append(x[i] + a * y[i])
        return out

    def shadow(x):
        return total([gram[0, j] * value for j, value in enumerate(x)])

    one = jnp.ones_like(shifts[0])
    resid, direction = [one], [one]
    error = []
    rho = gram[0, 0]
    for step in range(STEPS):
        move = image(direction)
        alpha = rho / shadow(move)
        middle = axpy(resid, -alpha, move)
        second = image(middle)
        against = products(second, len(second))
        omega = dot(middle, against) / dot(second, against)
        error = axpy(axpy(error, alpha, direction), omega, middle)
        if step + 1 < STEPS:
            resid = axpy(middle, -omega, second)
            rho_new = shadow(resid)
            beta = rho_new / rho * (alpha / omega)
            direction = axpy(resid, beta, axpy(direction, -omega, move))
            rho = rho_new
    return error


def kernel(
    regions, depth_y, depth_z, fine_dev, coarse_dev,
    rhs_hbm, fb_hbm, fl_hbm, cb_hbm, cl_hbm,
    both_out,
    rhs_raw, fb, fb_tail, fbh, fl, fl_tail, cb_raw, cb, cl, cidx, inv, rhs, fa, fc, fd, fa_image, steps, step_images, fl_halo, lift, pairs, images, tab, kv,
    hsend, hrecv, ksend, krecv, bsend, brecv, isend, irecv, fcb, e1, e2, g1, g2, row_send,
    load_sem, halo_send_sem, halo_recv_sem, k_send_sem, k_recv_sem, b_send_sem, b_recv_sem,
    red_send_sem, red_recv_sem,
):
    members = depth_y * depth_z * 2
    tiles = fine_dev // 128
    region = lax.axis_index("region")
    member = lax.axis_index("member")
    z, y, core = lax.div(member, 2 * depth_y), lax.rem(lax.div(member, 2), depth_y), lax.rem(member, 2)
    n1, n2 = regions * depth_y, depth_z * 2
    me1, me2 = region * depth_y + y, z * 2 + core
    region_at = [region] + [lax.rem(region + s, regions) for s in range(1, regions)]
    y_at = [member] + [member + 2 * (lax.rem(y + s, depth_y) - y) for s in range(1, depth_y)]
    z_at = [member] + [member + 2 * depth_y * (lax.rem(z + s, depth_z) - z) for s in range(1, depth_z)]
    def far_first(outer, inner, pair):
        around = lambda s, count: min(s, count - s)
        steps = [(s, t) for s in range(len(outer)) for t in range(len(inner))][1:]
        steps.sort(key=lambda st: -around(st[0], len(outer)) - around(st[1], len(inner)))
        return [pair(outer[s], inner[t]) for s, t in steps]

    peers1 = far_first(region_at, y_at, lambda r, m: (r, m))
    peers2 = far_first(z_at, [0, 1 - 2 * core], lambda m, flip: (region, m + flip))

    def at(dr, dm):
        r = region if dr == 0 else lax.rem(region + (regions + dr), regions)
        m = member if dm == 0 else lax.rem(member + (members + dm), members)
        return r, m

    after, before, above, below = at(0, 1), at(0, -1), at(1, 0), at(-1, 0)

    def block_tile(t, which):
        columns = pl.ds(128 * t, 128)
        return pltpu.make_async_copy(
            fb_hbm.at[:, :, :, columns], fb.at[:, :, :, columns], load_sem.at[which]
        )

    middle_tiles = fb.at[:, :, :, pl.ds(128, fine_dev - 256)]
    loads = [
        pltpu.make_async_copy(rhs_hbm, rhs_raw, load_sem.at[4]),
        pltpu.make_async_copy(middle_tiles, middle_tiles, load_sem.at[0]),
        pltpu.make_async_copy(cb_hbm, cb_raw, load_sem.at[1]),
        pltpu.make_async_copy(cl_hbm, cl, load_sem.at[2]),
        pltpu.make_async_copy(fl_hbm, fl, load_sem.at[3]),
    ]
    loads[0].start()
    face_loads = [block_tile(0, 5), block_tile(tiles - 1, 6)]
    for load in face_loads:
        load.start()
    for t in range(1, tiles - 1):
        block_tile(t, 0).start()
    for load in loads[2:]:
        load.start()

    barrier = pltpu.get_barrier_semaphore()
    for dr, dm in OFFSETS:
        device = at(-dr, -dm)
        pl.semaphore_signal(barrier, inc=1, device_id=device, device_id_type=MESH)

    for device in peers1 + peers2:
        pl.semaphore_signal(barrier, inc=1, device_id=device, device_id_type=MESH)

    lane = lanes_of((8, 128))
    rows = rows_of((8, 128))

    def halo_copies(ex, which):
        pairs = (
            (1, 0, after),
            (0, 1, before),
            (0, 2, above),
            (0, 3, below),
        )
        return [
            pltpu.make_async_remote_copy(
                src_ref=hsend.at[2 * ex + src],
                dst_ref=hrecv.at[4 * ex + dst],
                send_sem=halo_send_sem,
                recv_sem=halo_recv_sem.at[ex],
                device_id=device,
                device_id_type=MESH,
            )
            for src, dst, device in pairs
            if src in which
        ]

    def halo_send(ex, first, last):
        hsend[2 * ex] = first
        hsend[2 * ex + 1] = last
        for copy in halo_copies(ex, (0, 1)):
            copy.start()

    def halo_wait(ex):
        block = hrecv.at[pl.ds(4 * ex, 4)]
        pltpu.make_async_copy(block, block, halo_recv_sem.at[ex]).wait()
        return [hrecv[4 * ex + k] for k in range(4)]

    def reduce_start(which, buffer, peers, me, value):
        row_send[which] = value
        buffer[me] = value
        for device in peers:
            pltpu.make_async_remote_copy(
                src_ref=row_send.at[which],
                dst_ref=buffer.at[me],
                send_sem=red_send_sem,
                recv_sem=red_recv_sem.at[which],
                device_id=device,
                device_id_type=MESH,
            ).start()

    def reduce_wait(which, buffer, count, op):
        block = buffer.at[pl.ds(0, count - 1)]
        pltpu.make_async_copy(block, block, red_recv_sem.at[which]).wait()
        return functools.reduce(op, [buffer[k] for k in range(count)])

    def smooth(value, columns=slice(None)):
        total = inv[0, :, columns] * value[0:1, :]
        for j in range(1, 3):
            total = total + inv[j, :, columns] * value[j : j + 1, :]
        return total

    def links(g, columns):
        return fl[8 * g : 8 * g + 8, columns] if g < 3 else fl_tail[:, columns]

    def blocks_at(i, j, g, columns):
        return fb[i, j, 8 * g : 8 * g + 8, columns] if g < 3 else fb_tail[i, j, :, columns]

    def fine_local(source, target, count=1):
        for n in range(count):
            for j in range(3):
                for r in range(tiles):
                    row = 4 * n + j
                    tab[3 * n + j, r] = spread(source[row : row + 1, 128 * r : 128 * r + 128])

        def tile(t, carry):
            columns = pl.ds(pl.multiple_of(t * 128, 128), 128)
            accs = [None] * (3 * count)
            for g in range(4):
                index = links(g, columns)
                where = index & 127
                bits = [(index & (128 << k)) != 0 for k in range(3)]
                for j in range(3):
                    values = []
                    for n in range(count):
                        found = [take(tab[3 * n + j, r], where) for r in range(tiles)]
                        for bit in bits:
                            found = [
                                jnp.where(bit, found[2 * q + 1], found[2 * q])
                                for q in range(len(found) // 2)
                            ]
                        values.append(found[0])
                    for i in range(3):
                        block = blocks_at(i, j, g, columns)
                        for n in range(count):
                            term = block * values[n]
                            k = 3 * n + i
                            accs[k] = term if accs[k] is None else accs[k] + term
            for k in range(3 * count):
                pairs[k, t] = accs[k]
            return carry

        lax.fori_loop(0, tiles, tile, 0, unroll=UNROLL if count == 1 else 1)
        for t in range(tiles):
            sums = [pairs[k, t] for k in range(3 * count)]
            target[:, 128 * t : 128 * t + 128] = combine(sums) if count == 1 else combine_pair(sums)

    def fine_remote(halves, count=1):
        accs = [None] * (3 * count)
        for g in range(4):
            part = slice(8 * g, 8 * g + 8)
            index = links(g, slice(0, 128))
            where = index & 127
            bit = (index & 128) != 0
            for j in range(3):
                values = []
                for n in range(count):
                    row = 4 * n + j
                    low, high = (take(spread(half[row : row + 1, :]), where) for half in halves)
                    values.append(jnp.where(bit, high, low))
                for i in range(3):
                    block = fbh[i, j, part, :]
                    for n in range(count):
                        term = block * values[n]
                        k = 3 * n + i
                        accs[k] = term if accs[k] is None else accs[k] + term
        return combine(accs) if count == 1 else combine_pair(accs)

    def fine_send(ex, field):
        within = lane & 63
        halo_send(
            ex,
            take(field[:, 0:128], within),
            take(field[:, fine_dev - 128 : fine_dev], within + 64),
        )

    def fine_wait(ex):
        left, right, lower, upper = halo_wait(ex)
        return jnp.where(lane < 64, left, right), jnp.where(lane < 64, lower, upper)

    rhs[...] = jnp.zeros((8, fine_dev), F32)
    loads[0].wait()
    rhs[0:3, :] = rhs_raw[...]
    rhs[4:7, :] = rhs_raw[...]
    for load in face_loads:
        load.wait()

    def start_tile(t, carry):
        columns = pl.ds(pl.multiple_of(t * 128, 128), 128)
        (a, b, c), (d, e, f), (g_, h_, i_) = [
            [spread(fb[i, j, 26:27, columns]) for j in range(3)] for i in range(3)
        ]
        co_a = e * i_ - f * h_
        co_b = f * g_ - d * i_
        co_c = d * h_ - e * g_
        scale = RELAX / (a * co_a + b * co_b + c * co_c)
        adjugate = [
            [co_a, c * h_ - b * i_, b * f - c * e],
            [co_b, a * i_ - c * g_, c * d - a * f],
            [co_c, b * g_ - a * h_, a * e - b * d],
        ]
        total = None
        for j in range(3):
            column = jnp.where(rows & 3 == 2, adjugate[2][j], 0.0)
            column = jnp.where(rows & 3 == 1, adjugate[1][j], column)
            column = jnp.where(rows & 3 == 0, adjugate[0][j], column) * scale
            inv[j, :, columns] = column
            term = column * spread(rhs[j : j + 1, columns])
            total = term if total is None else total + term
        fa[:, columns] = total
        return carry

    start_tile(0, 0)
    start_tile(tiles - 1, 0)
    pl.semaphore_wait(barrier, len(OFFSETS) + (n1 - 1) + (n2 - 1))
    fine_send(0, fa)
    loads[1].wait()
    lax.fori_loop(1, tiles - 1, start_tile, 0, unroll=UNROLL)

    fl_tail[...] = jnp.where(rows_of((8, fine_dev)) == 2, lanes_of((8, fine_dev)), 0)
    fb_tail[...] = jnp.zeros((3, 3, 8, fine_dev), F32)
    fb_tail[:, :, 0:3, :] = fb[:, :, 24:27, :]
    loads[4].wait()
    fl_tail[0:2, :] = fl[24:26, :]
    for g in range(4):
        part = slice(8 * g, 8 * g + 8)
        outside = links(g, slice(0, 128)) >= fine_dev
        for i in range(3):
            for j in range(3):
                block = blocks_at(i, j, g, slice(0, 128))
                fbh[i, j, part, :] = jnp.where(outside, block, 0.0)
                inside = jnp.where(outside, 0.0, block)
                if g < 3:
                    fb[i, j, part, 0:128] = inside
                else:
                    fb_tail[i, j, :, 0:128] = inside

    kv[...] = jnp.zeros((3, 8, 128), F32)
    cidx[24:32, :] = jnp.where(rows == 2, lane, 0)
    cb[:, :, 24:32, :] = jnp.zeros((3, 3, 8, 128), F32)
    loads[2].wait()
    loads[3].wait()
    cb[:, :, 0:27, :] = cb_raw[...]
    cidx[0:26, :] = cl[...]
    diagonal = [cb[i, i, 26:27, :] for i in range(3)]
    largest = functools.reduce(jnp.maximum, diagonal)
    smallest = -functools.reduce(jnp.minimum, diagonal)
    largest, smallest = spread(largest), spread(smallest)
    swap = lane ^ 64
    largest = jnp.maximum(largest, take(largest, swap))
    smallest = jnp.maximum(smallest, take(smallest, swap))
    extremes = jnp.where(lane < 64, largest, smallest)[0:1]

    reduce_start(0, e1, peers1, me1, extremes)
    fine_local(fa, fc)

    head, rest = slice(0, 128), slice(128, fine_dev)
    fa[:, rest] += smooth(rhs[:, rest] - fc[:, rest], rest)
    halves = fine_wait(0)
    fa[:, head] += smooth(rhs[:, head] - fc[:, head] - fine_remote(halves), head)
    fine_send(1, fa)
    extremes = reduce_wait(0, e1, n1, jnp.maximum)
    reduce_start(1, e2, peers2, me2, extremes)
    fine_local(fa, fc)

    quarter = lane >> 5

    def packed(pieces, start):
        rolled = [pltpu.roll(piece, (128 + 32 * g - start) % 128, 1) for g, piece in enumerate(pieces)]
        low = jnp.where(quarter == 0, rolled[0], rolled[1])
        return jnp.where(quarter < 2, low, jnp.where(quarter == 2, rolled[2], rolled[3]))

    parts = [slice(8 * g, 8 * g + 8) for g in range(4)]
    codes = [cidx[part, :] for part in parts]
    for end, start in ((0, 0), (1, coarse_dev - 32)):
        isend[end] = packed(codes, start)
        for i in range(3):
            for j in range(3):
                bsend[end, 3 * i + j] = packed([cb[i, j, part, :] for part in parts], start)
    face_code = isend[0]
    for i in range(3):
        for j in range(3):
            fcb[i, j] = jnp.where(face_code >= coarse_dev, bsend[0, 3 * i + j], 0.0)
            for g in range(4):
                cb[i, j, parts[g], :] = jnp.where(codes[g] >= coarse_dev, 0.0, cb[i, j, parts[g], :])
    for g in range(4):
        cidx[parts[g], :] = codes[g] & 127
    side_copies = []
    for src, dst, device in ((1, 0, after), (0, 1, before), (0, 2, above), (0, 3, below)):
        for kind, (source, sink) in enumerate(((bsend, brecv), (isend, irecv))):
            side_copies.append(
                pltpu.make_async_remote_copy(
                    src_ref=source.at[src],
                    dst_ref=sink.at[dst],
                    send_sem=b_send_sem.at[kind],
                    recv_sem=b_recv_sem.at[kind],
                    device_id=device,
                    device_id_type=MESH,
                )
            )
    for copy in side_copies:
        copy.start()
    def eighths(part):
        for k in (1, 2, 4):
            part = part + pltpu.roll(part, 128 - k, 1)
        return take(part, (lane & 15) * 8)

    def restrict(ref):
        out = eighths(ref[:, 0:128])
        for t in range(1, tiles):
            picked = eighths(ref[:, 128 * t : 128 * t + 128])
            out = jnp.where(lane >> 4 == t, picked, out)
        return out

    fc[...] = rhs[...] - fc[...]
    coarse = restrict(fc)
    remote = fine_remote(fine_wait(1))
    fc[:, head] -= remote
    coarse = coarse - jnp.where(lane < 16, eighths(remote), 0.0)

    def coarse_send(ex, field):
        edge = take(field, jnp.where(lane < 32, lane + (coarse_dev - 32), lane & 31))
        tile = jnp.where(rows < 4, field, edge)
        ksend[ex] = tile
        for k, (dr, dm) in enumerate(OFFSETS):
            pltpu.make_async_remote_copy(
                src_ref=ksend.at[ex],
                dst_ref=krecv.at[ex, k],
                send_sem=k_send_sem,
                recv_sem=k_recv_sem.at[ex],
                device_id=at(-dr, -dm),
                device_id_type=MESH,
            ).start()
        return tile

    def coarse_wait(ex):
        block = krecv.at[ex]
        pltpu.make_async_copy(block, block, k_recv_sem.at[ex]).wait()
        return {offset: krecv[ex, k] for k, offset in enumerate(OFFSETS)}

    def beside(left, right, lower, upper):
        low = jnp.where(quarter == 0, left, right)
        return jnp.where(quarter < 2, low, jnp.where(quarter == 2, lower, upper))

    def folded(accs):
        tile = combine(accs)
        tile = tile + pltpu.roll(tile, 64, 1)
        return tile + pltpu.roll(tile, 32, 1)

    def coarse_local(field):
        accs = [None] * 3
        tables = [spread(field[j : j + 1, :]) for j in range(3)]
        for g in range(4):
            index = cidx[parts[g], :]
            for j in range(3):
                value = take(tables[j], index)
                for i in range(3):
                    term = cb[i, j, parts[g], :] * value
                    accs[i] = term if accs[i] is None else accs[i] + term
        return combine(accs)

    def coarse_remote(halo):
        accs = [None] * 3
        index = isend[0] & 127
        for j in range(3):
            value = take(spread(halo[4 + j : 5 + j, :]), index)
            for i in range(3):
                term = fcb[i, j] * value
                accs[i] = term if accs[i] is None else accs[i] + term
        return jnp.where(lane < 32, folded(accs), 0.0)

    def coarse_ghost(tiles_of, mine):
        around = (
            ((0, -1), None),
            ((0, 1), (mine, tiles_of[0, 2], tiles_of[-1, 1], tiles_of[1, 1])),
            ((-1, 0), (tiles_of[-1, -1], tiles_of[-1, 1], tiles_of[2, 0], mine)),
            ((1, 0), (tiles_of[1, -1], tiles_of[1, 1], mine, tiles_of[2, 0])),
        )
        out = None
        for q, (offset, edges) in enumerate(around):
            code = irecv[q]
            index = code & 127
            full = tiles_of[offset]
            outer = None if edges is None else beside(*edges)
            accs = [None] * 3
            for j in range(3):
                value = take(spread(full[j : j + 1, :]), index)
                if outer is not None:
                    far = take(spread(outer[4 + j : 5 + j, :]), index)
                    value = jnp.where(code >= coarse_dev, far, value)
                for i in range(3):
                    term = brecv[q, 3 * i + j] * value
                    accs[i] = term if accs[i] is None else accs[i] + term
            tile = folded(accs)
            out = tile if out is None else jnp.where(quarter == q, tile, out)
        return out

    def lift_pair(ex, fields, halos):
        for n in range(2):
            for j in range(3):
                lift[n, j] = spread(fields[n][j : j + 1, :])

        def tile(t, carry):
            columns = pl.ds(pl.multiple_of(t * 128, 128), 128)
            accs = [None] * 6
            for g in range(4):
                where = (links(g, columns) >> 3) & 127
                for j in range(3):
                    values = [take(lift[n, j], where) for n in range(2)]
                    for i in range(3):
                        block = blocks_at(i, j, g, columns)
                        for n in range(2):
                            term = block * values[n]
                            k = 3 * n + i
                            accs[k] = term if accs[k] is None else accs[k] + term
            for k in range(6):
                pairs[k, t] = accs[k]
            return carry

        lax.fori_loop(0, tiles, tile, 0, unroll=UNROLL)
        accs = [pairs[k, 0] for k in range(6)]
        for g in range(4):
            where = fl_halo[parts[g], :]
            for j in range(3):
                values = [take(spread(halos[n][4 + j : 5 + j, :]), where) for n in range(2)]
                for i in range(3):
                    block = fbh[i, j, parts[g], :]
                    for n in range(2):
                        accs[3 * n + i] = accs[3 * n + i] + block * values[n]
        images[ex, :, 0:128] = combine_pair(accs)
        for t in range(1, tiles):
            images[ex, :, 128 * t : 128 * t + 128] = combine_pair([pairs[k, t] for k in range(6)])

        def faces(columns):
            total = None
            for j in range(3):
                value = jnp.where(
                    rows < 4, spread(images[ex, j : j + 1, columns]), spread(images[ex, j + 4 : j + 5, columns])
                )
                term = inv[j, :, columns] * value
                total = term if total is None else total + term
            return total

        for t in range(tiles):
            columns = slice(128 * t, 128 * t + 128)
            steps[:, columns] = faces(columns)
        fine_send(3 + ex, steps)

    mine = coarse_send(0, coarse)
    for g in range(4):
        node = links(g, slice(0, 128)) & 255
        fl_halo[parts[g], :] = ((node >> 6) << 5) + ((node & 63) >> 3) + jnp.where(node < 64, 24, 0)
    update = smooth(fc[...])
    fd[...] = update
    fine_send(2, fd)
    fine_local(fd, fa_image)
    extremes = spread(reduce_wait(1, e2, n2, jnp.maximum))
    lowest = jnp.min(extremes)
    largest = jnp.max(jnp.where(lane < 64, extremes, lowest), axis=1, keepdims=True)
    smallest = -jnp.max(jnp.where(lane < 64, lowest, extremes), axis=1, keepdims=True)
    largest, smallest = jnp.broadcast_to(largest, (8, 128)), jnp.broadcast_to(smallest, (8, 128))
    middle = 0.5 * largest + 0.5 * smallest
    centres = [middle, 0.1 * smallest, 1.3 * largest, smallest, largest, middle]
    width = 0.5 * largest - 0.5 * smallest + 0.125 * largest
    shrink = 1.0 / width
    for kind, sink in enumerate((brecv, irecv)):
        pltpu.make_async_copy(sink, sink, b_recv_sem.at[kind]).wait()

    def keep(ref, k, field):
        for j in range(3):
            ref[j, k : k + 1, :] = field[j : j + 1, :]

    for ex in range(STEPS):
        local = coarse_local(coarse) - centres[2 * ex] * coarse
        keep(kv, 2 * ex, coarse)
        base = coarse
        tiles_of = coarse_wait(ex)
        halo = beside(tiles_of[0, -1], tiles_of[0, 1], tiles_of[-1, 0], tiles_of[1, 0])
        coarse = (local + coarse_remote(halo)) * shrink
        ghost = (coarse_ghost(tiles_of, mine) - centres[2 * ex] * halo) * shrink
        keep(kv, 2 * ex + 1, coarse)
        pair = (base, coarse), (halo, ghost)
        coarse = (coarse_local(coarse) - centres[2 * ex + 1] * coarse + coarse_remote(ghost)) * shrink
        if ex + 1 < STEPS:
            mine = coarse_send(ex + 1, coarse)
            lift_pair(ex, *pair)
            fine_local(steps, step_images.at[ex], 2)
            if ex == 1:
                fa_image[:, head] += fine_remote(fine_wait(2))
                step_images[0, :, head] += fine_remote(fine_wait(3), 2)
    for j in range(3):
        kv[j, BASIS - 1 : BASIS, :] = coarse[j : j + 1, :]

    gram = jnp.zeros((8, 128), F32)
    for k in range(BASIS):
        column = None
        for j in range(3):
            term = kv[j] * spread(kv[j, k : k + 1, :])
            column = term if column is None else column + term
        gram = jnp.where(lane & 7 == k, jnp.sum(column, axis=1, keepdims=True), gram)
    gram = jnp.where(rows == lane >> 3, gram, 0.0)
    gram = jnp.sum(gram, axis=0, keepdims=True)
    reduce_start(2, g1, peers1, me1, gram)
    lift_pair(STEPS - 1, *pair)
    step_images[1, :, head] += fine_remote(fine_wait(4), 2)
    gram = reduce_wait(2, g1, n1, jnp.add)
    reduce_start(3, g2, peers2, me2, gram)
    fine_local(steps, step_images.at[STEPS - 1], 2)
    step_images[STEPS - 1, :, head] += fine_remote(fine_wait(3 + STEPS - 1), 2)
    gram = spread(reduce_wait(3, g2, n2, jnp.add))
    entries = {
        (i, j): take(gram, jnp.full((8, 128), 8 * i + j, jnp.int32))
        for i in range(BASIS)
        for j in range(i, BASIS)
    }
    weights = [weight * shrink for weight in coefficients(entries, [centre * shrink for centre in centres])]

    def mix(ref):
        out = []
        for j in range(3):
            total = None
            for k, weight in enumerate(weights):
                term = weight[0:1] * ref[j, k : k + 1, :]
                total = term if total is None else total + term
            out.append(total)
        tile = jnp.where(rows == 1, out[1], jnp.where(rows == 2, out[2], 0.0))
        return jnp.where(rows == 0, out[0], tile)

    doubled = [jnp.where(rows < 4, weights[2 * ex], weights[2 * ex + 1]) for ex in range(STEPS)]

    def mix_pairs(tiles_of):
        total = functools.reduce(jnp.add, [w * tile for w, tile in zip(doubled, tiles_of)])
        return total + pltpu.roll(total, 4, 0)

    for t in range(tiles):
        columns = slice(128 * t, 128 * t + 128)
        fc[:, columns] = fc[:, columns] - mix_pairs([images[ex, :, columns] for ex in range(STEPS)])
    error = mix(kv)
    update = smooth(fc[...])
    for t in range(tiles):
        columns = slice(128 * t, 128 * t + 128)
        both_out[0, :, columns] = (fa[:, columns] + update[:, columns] + take(error, 16 * t + (lane >> 3)))[0:3]
        final = fc[:, columns] - fa_image[:, columns]
        final = final + mix_pairs([step_images[ex, :, columns] for ex in range(STEPS)])
        both_out[1, :, columns] = final[0:3]

    pltpu.make_async_copy(hrecv, hrecv, halo_send_sem).wait()
    pltpu.make_async_copy(krecv, krecv, k_send_sem).wait()
    for kind, sink in enumerate((brecv, irecv)):
        pltpu.make_async_copy(sink, sink, b_send_sem.at[kind]).wait()
    for buffer, count in ((e1, n1), (e2, n2), (g1, n1), (g2, n2)):
        block = buffer.at[pl.ds(0, count - 1)]
        pltpu.make_async_copy(block, block, red_send_sem).wait()


def body(regions, depth_y, depth_z, right_side, fine_blocks, fine_links, coarse_blocks, coarse_links):
    fine_dev, coarse_dev = right_side.shape[1], coarse_blocks.shape[3]
    n1, n2 = regions * depth_y, depth_z * 2
    exchanges = 3 + STEPS
    reach = len(OFFSETS)
    vmem = pl.BlockSpec(memory_space=pltpu.VMEM)
    hbm = pl.BlockSpec(memory_space=pltpu.HBM)
    out = pltpu.VMEM((2, 3, fine_dev), F32)
    both = pl.pallas_call(
        functools.partial(kernel, regions, depth_y, depth_z, fine_dev, coarse_dev),
        out_shape=out,
        in_specs=[hbm] * 5,
        out_specs=vmem,
        scratch_shapes=[
            pltpu.VMEM((3, fine_dev), F32),
            pltpu.VMEM((3, 3, SLOTS, fine_dev), F32),
            pltpu.VMEM((3, 3, 8, fine_dev), F32),
            pltpu.VMEM((3, 3, PAD, 128), F32),
            pltpu.VMEM((SLOTS - 1, fine_dev), jnp.int32),
            pltpu.VMEM((8, fine_dev), jnp.int32),
            pltpu.VMEM((3, 3, SLOTS, 128), F32),
            pltpu.VMEM((3, 3, PAD, 128), F32),
            pltpu.VMEM((SLOTS - 1, 128), jnp.int32),
            pltpu.VMEM((PAD, 128), jnp.int32),
            pltpu.VMEM((3, 8, fine_dev), F32),
            pltpu.VMEM((8, fine_dev), F32),
            pltpu.VMEM((8, fine_dev), F32),
            pltpu.VMEM((8, fine_dev), F32),
            pltpu.VMEM((8, fine_dev), F32),
            pltpu.VMEM((8, fine_dev), F32),
            pltpu.VMEM((8, fine_dev), F32),
            pltpu.VMEM((STEPS, 8, fine_dev), F32),
            pltpu.VMEM((PAD, 128), jnp.int32),
            pltpu.VMEM((2, 3, 8, 128), F32),
            pltpu.VMEM((6, fine_dev // 128, 8, 128), F32),
            pltpu.VMEM((STEPS, 8, fine_dev), F32),
            pltpu.VMEM((6, fine_dev // 128, 8, 128), F32),
            pltpu.VMEM((3, 8, 128), F32),
            pltpu.VMEM((2 * exchanges, 8, 128), F32),
            pltpu.VMEM((4 * exchanges, 8, 128), F32),
            pltpu.VMEM((STEPS, 8, 128), F32),
            pltpu.VMEM((STEPS, reach, 8, 128), F32),
            pltpu.VMEM((2, 9, 8, 128), F32),
            pltpu.VMEM((4, 9, 8, 128), F32),
            pltpu.VMEM((2, 8, 128), jnp.int32),
            pltpu.VMEM((4, 8, 128), jnp.int32),
            pltpu.VMEM((3, 3, 8, 128), F32),
            pltpu.VMEM((n1, 1, 128), F32),
            pltpu.VMEM((n2, 1, 128), F32),
            pltpu.VMEM((n1, 1, 128), F32),
            pltpu.VMEM((n2, 1, 128), F32),
            pltpu.VMEM((4, 1, 128), F32),
            pltpu.SemaphoreType.DMA((7,)),
            pltpu.SemaphoreType.DMA,
            pltpu.SemaphoreType.DMA((exchanges,)),
            pltpu.SemaphoreType.DMA,
            pltpu.SemaphoreType.DMA((STEPS,)),
            pltpu.SemaphoreType.DMA((2,)),
            pltpu.SemaphoreType.DMA((2,)),
            pltpu.SemaphoreType.DMA,
            pltpu.SemaphoreType.DMA((4,)),
        ],
        compiler_params=pltpu.CompilerParams(
            collective_id=0, has_side_effects=True, vmem_limit_bytes=60 * 1024 * 1024
        ),
    )(
        right_side,
        jnp.transpose(fine_blocks, (1, 2, 0, 3)),
        fine_links,
        jnp.transpose(coarse_blocks, (1, 2, 0, 3)),
        coarse_links,
    )
    return both[0], both[1]


def solution(mesh):
    regions, members = mesh.shape["region"], mesh.shape["member"]
    depth_y = 4 if members % 8 == 0 else 2
    depth_z = members // (2 * depth_y)
    flat = ("region", "member")
    return jax.shard_map(
        functools.partial(body, regions, depth_y, depth_z),
        mesh=mesh,
        in_specs=(
            P(None, flat),
            P(None, None, None, flat),
            P(None, flat),
            P(None, None, None, flat),
            P(None, flat),
        ),
        out_specs=(P(None, flat), P(None, flat)),
        check_vma=False,
    )
```
